32 devices in a mesh: dp: 8 (over z, y), fsdp: 4 (over x, core).
Axes of the slice: x: 2, y: 2, z: 4, core: 2. Of those that a mesh axis runs over, the one named last changes fastest.
Arguments:
- inputs: bfloat16 [4, 4096, 768], P(None, ('dp', 'fsdp')), may hold values from -6 to 6
- segments: int32 [4, 4096], P(None, 'dp'), may hold values from 0 to 1, as said below
- norm1_gain: bfloat16 [768], P(('dp', 'fsdp')), may hold values from 0.5 to 1.5
- norm1_bias: bfloat16 [768], P(('dp', 'fsdp')), may hold values from -0.59765625 to 0.59765625
- qkv_weight: bfloat16 [768, 2304], P(('dp', 'fsdp')), may hold values from -0.21875 to 0.21875
- query_bias: bfloat16 [768], P(('dp', 'fsdp')), may hold values from -0.59765625 to 0.59765625
- value_bias: bfloat16 [768], P(('dp', 'fsdp')), may hold values from -0.1796875 to 0.1796875
- out_weight: bfloat16 [768, 768], P(('dp', 'fsdp')), may hold values from -3.5 to 3.5
- out_bias: bfloat16 [768], P(('dp', 'fsdp')), may hold values from -0.59765625 to 0.59765625
- norm2_gain: bfloat16 [768], P(('dp', 'fsdp')), may hold values from 0.5 to 1.5
- norm2_bias: bfloat16 [768], P(('dp', 'fsdp')), may hold values from -0.59765625 to 0.59765625
- up_weight: bfloat16 [768, 3072], P(('dp', 'fsdp')), may hold values from -0.21875 to 0.21875
- up_bias: bfloat16 [3072], P(('dp', 'fsdp')), may hold values from -0.59765625 to 0.59765625
- down_weight: bfloat16 [3072, 768], P(('dp', 'fsdp')), may hold values from -0.109375 to 0.109375
- down_bias: bfloat16 [768], P(('dp', 'fsdp')), may hold values from -0.59765625 to 0.59765625
- cotangent: bfloat16 [4, 4096, 768], P(None, ('dp', 'fsdp')), may hold values from -6 to 6
Outputs:
- output: bfloat16 [4, 4096, 768], P(None, ('dp', 'fsdp'))
- input_grad: float32 [4, 4096, 768], P(None, ('dp', 'fsdp'))
- grad_norm1_gain: float32 [768], P(('dp', 'fsdp'))
- grad_norm1_bias: float32 [768], P(('dp', 'fsdp'))
- grad_qkv_weight: float32 [768, 2304], P(('dp', 'fsdp'))
- grad_query_bias: float32 [768], P(('dp', 'fsdp'))
- grad_value_bias: float32 [768], P(('dp', 'fsdp'))
- grad_out_weight: float32 [768, 768], P(('dp', 'fsdp'))
- grad_out_bias: float32 [768], P(('dp', 'fsdp'))
- grad_norm2_gain: float32 [768], P(('dp', 'fsdp'))
- grad_norm2_bias: float32 [768], P(('dp', 'fsdp'))
- grad_up_weight: float32 [768, 3072], P(('dp', 'fsdp'))
- grad_up_bias: float32 [3072], P(('dp', 'fsdp'))
- grad_down_weight: float32 [3072, 768], P(('dp', 'fsdp'))
- grad_down_bias: float32 [768], P(('dp', 'fsdp'))
The draws below stay inside these ranges and needn't reach their ends.
Inputs may be any that keep to these rules, and one draw needn't show every extreme that they name: `segments`: in each micro-batch each index of dp holds two clips numbered 0 and 1. List the group's 512 tokens by their row within a device first and their index of fsdp second: clip 0 comes first, then clip 1. Clip 0 ends after 512 // 2 tokens of this list, moved by at most 32 either way, so that every clip has tokens on every device of fsdp.
All inputs are finite; a program needn't handle non-finite values.
Results may differ from the reference program's by a relative error of at most 0.013.
Values may be sent and summed in bfloat16 or wider, within the bound.
No kernel may reach another device: no remote copies, remote signals or barrier semaphores. Data moves between devices by JAX's collectives and lax.ppermute only.
A program may use at most 256 MiB of HBM per device.

```python
import math
import jax
import jax.numpy as jnp
from jax import lax

D = 768
HEADS = 12
HEAD_DIM = 64
FF = 3072
MICRO = 4
TOK_DEV = 128
GROUP_TOK = 512
TOKENS = 4096


def draw_segments(key, part):
    key = jax.random.fold_in(key, 17)
    groups = TOKENS // GROUP_TOK
    fsdp_count = GROUP_TOK // TOK_DEV
    quarter = TOK_DEV // 4
    first_end = GROUP_TOK // 2 + jax.random.randint(key, (MICRO, groups, 1), -quarter, quarter + 1)
    position = jnp.arange(GROUP_TOK, dtype=jnp.int32)
    listed = (position % TOK_DEV * fsdp_count + position // TOK_DEV)[None, None, :]
    labels = (listed >= first_end).astype(jnp.int32)
    return labels.reshape(MICRO, TOKENS)


def strengthened(values, own_key, source, target, parts, factor):
    def block_of(dim):
        return (jnp.arange(values.shape[dim]) // (values.shape[dim] // parts)).reshape((-1,) + (1,) * (values.ndim - 1 - dim))

    near = jax.random.permutation(own_key, parts)[block_of(target)]
    far = (block_of(target) + parts // 2) % parts
    return jnp.where((block_of(source) == near) | (block_of(source) == far), factor * values, values)


def levels(own_key, extent, split, least, largest):
    factor_of = 1.0
    for dim, parts in split:
        heights = jax.random.uniform(jax.random.fold_in(jax.random.fold_in(own_key, 6), dim), (parts,), jnp.float32, least / len(split), largest / len(split))
        factor_of = factor_of * jnp.repeat(jnp.exp(heights), extent[dim] // parts).reshape((-1,) + (1,) * (len(extent) - 1 - dim))
    return factor_of


def scatter_about(own_key, shape, deviation, most, split=(), kind=jnp.bfloat16):
    factor_of = levels(own_key, shape, split, -0.22, 0.18) if split else 1.0
    array = jax.random.normal(own_key, shape, jnp.float32) * deviation * factor_of
    return jnp.minimum(jnp.maximum(array, -most), most).astype(kind)


def heavy_noise(rng, extent, scale, most, shards, heavy, kind=jnp.bfloat16):
    values = scale * jax.random.normal(rng, extent, jnp.float32)
    if shards:
        values = values * levels(rng, extent, shards, -0.22, 0.18)
    return jnp.clip(strengthened(values, jax.random.fold_in(rng, 3), *heavy), -most, most).astype(kind)


def setup_inputs(seed: int = 0) -> dict:
    keys = jax.random.split(jax.random.key(seed), 17)
    inputs = heavy_noise(keys[0], (MICRO, TOKENS, D), 1.0, 6.0, ((1, 32),), (1, 2, 32, 2.75))
    segments = draw_segments(jax.random.fold_in(keys[16], 71), 0)
    norm1_gain = jnp.clip(1.0 + 0.1 * jax.random.normal(keys[2], (D,), jnp.float32), 0.5, 1.5).astype(jnp.bfloat16)
    norm1_bias = scatter_about(keys[3], (D,), 0.1, 0.59765625, ((0, 32),))
    qkv_weight = scatter_about(keys[4], (D, 3 * D), D ** -0.5, 0.21875, ((0, 32),))
    query_bias = scatter_about(keys[5], (D,), 0.1, 0.59765625, ((0, 32),))
    value_bias = scatter_about(keys[6], (D,), 0.03, 0.1796875, ((0, 32),))
    out_weight = scatter_about(keys[7], (D, D), (max(1, 2 * D // GROUP_TOK)) ** -0.5, 3.5, ((0, 32),))
    out_bias = scatter_about(keys[8], (D,), 0.1, 0.59765625, ((0, 32),))
    norm2_gain = jnp.clip(1.0 + 0.1 * jax.random.normal(keys[9], (D,), jnp.float32), 0.5, 1.5).astype(jnp.bfloat16)
    norm2_bias = scatter_about(keys[10], (D,), 0.1, 0.59765625, ((0, 32),))
    up_weight = scatter_about(keys[11], (D, FF), D ** -0.5, 0.21875, ((0, 32),))
    up_bias = scatter_about(keys[12], (FF,), 0.1, 0.59765625, ((0, 32),))
    down_weight = scatter_about(keys[13], (FF, D), FF ** -0.5, 0.109375, ((0, 32),))
    down_bias = scatter_about(keys[14], (D,), 0.1, 0.59765625, ((0, 32),))
    cotangent = scatter_about(keys[15], (MICRO, TOKENS, D), 1.0, 6.0, ((1, 32),))
    return dict(inputs=inputs, segments=segments, norm1_gain=norm1_gain, norm1_bias=norm1_bias, qkv_weight=qkv_weight, query_bias=query_bias, value_bias=value_bias, out_weight=out_weight, out_bias=out_bias, norm2_gain=norm2_gain, norm2_bias=norm2_bias, up_weight=up_weight, up_bias=up_bias, down_weight=down_weight, down_bias=down_bias, cotangent=cotangent)


EPSILON = 1e-06
NEG_LARGE = -1e+30

@jax.custom_vjp
def low(v):
    return lax.optimization_barrier(v.astype(jnp.bfloat16)).astype(jnp.float32)

@jax.custom_vjp
def low_back(v):
    return v

def low_keep(v):
    return (low(v), None)

def low_pass(kept, grad):
    return (grad,)

def back_keep(v):
    return (v, None)

def back_low(kept, grad):
    return (low(grad),)
low.defvjp(low_keep, low_pass)
low_back.defvjp(back_keep, back_low)

def matmul(left, right):
    return jnp.dot(left, right, precision=lax.Precision.HIGHEST)

def layer_norm(values, gain_vec, shift_vec):
    centre = values - lax.optimization_barrier(jnp.mean(values, -1, keepdims=True))
    spread = lax.optimization_barrier(jnp.mean(centre * centre, -1, keepdims=True))
    return centre * lax.rsqrt(spread + EPSILON) * gain_vec + shift_vec

def gelu_tanh(values):
    return 0.5 * values * (1.0 + jnp.tanh(0.7978845608028654 * (values + 0.044715 * values * values * values)))

def sequence(params, tokens_in, labels):
    gain_one, shift_one, qkv_full, bias_query, bias_value, out_full, bias_out, gain_two, shift_two, up_full, bias_up, down_full, bias_down = params
    length = tokens_in.shape[0]
    normed_one = low(layer_norm(tokens_in, gain_one, shift_one))
    project = matmul(normed_one, qkv_full)
    queries = low(low_back(project[:, :D] + bias_query)).reshape(length, HEADS, HEAD_DIM)
    keys_all = low(low_back(project[:, D:2 * D])).reshape(length, HEADS, HEAD_DIM)
    values_all = low(low_back(project[:, 2 * D:] + bias_value)).reshape(length, HEADS, HEAD_DIM)
    rows_block = math.gcd(512, length)
    count = length // rows_block

    def attend(pieces):
        query_block, label_block = pieces
        scores = low_back(jnp.einsum('qhd,khd->hqk', query_block, keys_all, precision=lax.Precision.HIGHEST)) * 0.125
        allowed = (label_block[:, None] == labels[None, :])[None]
        scores = jnp.where(allowed, scores, NEG_LARGE)
        biggest = lax.optimization_barrier(jnp.max(scores, -1, keepdims=True))
        exponent = jnp.where(allowed, jnp.exp(scores - biggest), 0.0)
        attend_prob = exponent / lax.optimization_barrier(jnp.sum(exponent, -1, keepdims=True))
        return jnp.einsum('hqk,khd->qhd', low(attend_prob), values_all, precision=lax.Precision.HIGHEST)
    mixed = lax.map(jax.checkpoint(attend), (queries.reshape(count, rows_block, HEADS, HEAD_DIM), labels.reshape(count, rows_block)))
    mixed = low(low_back(mixed.reshape(length, D)))
    resid = tokens_in + low_back(matmul(mixed, out_full) + bias_out)
    normed_two = low(layer_norm(resid, gain_two, shift_two))
    pre_act = low_back(matmul(normed_two, up_full) + bias_up)
    hidden = low(gelu_tanh(pre_act))
    return resid + low_back(matmul(hidden, down_full) + bias_down)

def reference(inputs, segments, norm1_gain, norm1_bias, qkv_weight, query_bias, value_bias, out_weight, out_bias, norm2_gain, norm2_bias, up_weight, up_bias, down_weight, down_bias, cotangent):
    groups = TOKENS // GROUP_TOK
    params = tuple((item.astype(jnp.float32) for item in (norm1_gain, norm1_bias, qkv_weight, query_bias, value_bias, out_weight, out_bias, norm2_gain, norm2_bias, up_weight, up_bias, down_weight, down_bias)))
    seq_in = inputs.astype(jnp.float32).reshape(MICRO * groups, GROUP_TOK, D)
    seq_labels = segments.reshape(MICRO * groups, GROUP_TOK)
    seq_cot = cotangent.astype(jnp.float32).reshape(MICRO * groups, GROUP_TOK, D)

    def forward(tokens_all, weights_all):

        def one_sequence(pieces):
            return sequence(weights_all, pieces[0], pieces[1])
        return lax.map(jax.checkpoint(one_sequence), (tokens_all, seq_labels))
    result, pull = jax.vjp(forward, seq_in, params)
    grad_in, grads = pull(seq_cot)
    return (result.reshape(MICRO, TOKENS, D).astype(jnp.bfloat16), grad_in.reshape(MICRO, TOKENS, D), grads[0], grads[1], grads[2], grads[3], grads[4], grads[5], grads[6], grads[7], grads[8], grads[9], grads[10], grads[11], grads[12])
```

```python
import functools
import math

import jax
import jax.numpy as jnp
from jax import lax
from jax.experimental import pallas as pl
from jax.experimental.pallas import tpu as pltpu
from jax.sharding import PartitionSpec as P

HEADS = 12


EPSILON = 1e-06
NEG_LARGE = -1e30
SCALE_SCORE = 0.125


def layer_norm(values, gain_vec, shift_vec):
    centre = values - jnp.mean(values, -1, keepdims=True)
    spread = jnp.mean(centre * centre, -1, keepdims=True)
    return centre * lax.rsqrt(spread + EPSILON) * gain_vec + shift_vec


def gelu_tanh(values):
    return (
        0.5
        * values
        * (1.0 + jnp.tanh(0.7978845608028654 * (values + 0.044715 * values * values * values)))
    )


def add_terms(first_terms, second_terms):
    if first_terms is None:
        return second_terms
    return jax.tree.map(jnp.add, first_terms, second_terms)


def on_device_general(
    inputs,
    segments,
    norm1_gain,
    norm1_bias,
    qkv_weight,
    query_bias,
    value_bias,
    out_weight,
    out_bias,
    norm2_gain,
    norm2_bias,
    up_weight,
    up_bias,
    down_weight,
    down_bias,
    cotangent,
):
    micro_count = inputs.shape[0]
    local_rows = inputs.shape[1]
    model_width = inputs.shape[2]
    group_rows = segments.shape[1]
    key_rows = math.gcd(512, group_rows)
    key_count = group_rows // key_rows
    offset = lax.axis_index("fsdp") * local_rows
    f32 = jnp.float32
    bf16 = jnp.bfloat16
    outputs = []
    in_grads = []
    totals = None
    for micro_index in range(micro_count):
        params_fwd = (
            lax.all_gather(norm1_gain, ("dp", "fsdp"), axis=0, tiled=True),
            lax.all_gather(norm1_bias, ("dp", "fsdp"), axis=0, tiled=True),
            lax.all_gather(qkv_weight, ("dp", "fsdp"), axis=0, tiled=True),
            lax.all_gather(query_bias, ("dp", "fsdp"), axis=0, tiled=True),
            lax.all_gather(value_bias, ("dp", "fsdp"), axis=0, tiled=True),
            lax.all_gather(out_weight, ("dp", "fsdp"), axis=0, tiled=True),
            lax.all_gather(out_bias, ("dp", "fsdp"), axis=0, tiled=True),
            lax.all_gather(norm2_gain, ("dp", "fsdp"), axis=0, tiled=True),
            lax.all_gather(norm2_bias, ("dp", "fsdp"), axis=0, tiled=True),
            lax.all_gather(up_weight, ("dp", "fsdp"), axis=0, tiled=True),
            lax.all_gather(up_bias, ("dp", "fsdp"), axis=0, tiled=True),
            lax.all_gather(down_weight, ("dp", "fsdp"), axis=0, tiled=True),
            lax.all_gather(down_bias, ("dp", "fsdp"), axis=0, tiled=True),
        )
        (
            gain_one,
            shift_one,
            qkv_full,
            bias_query,
            bias_value,
            out_full,
            bias_out,
            gain_two,
            shift_two,
            up_full,
            bias_up,
            down_full,
            bias_down,
        ) = params_fwd
        resid_in = inputs[micro_index].astype(f32)
        normed_one = layer_norm(resid_in, gain_one.astype(f32), shift_one.astype(f32)).astype(bf16)
        project = jnp.dot(normed_one, qkv_full, preferred_element_type=f32)
        queries = (project[:, :model_width] + bias_query.astype(f32)).astype(bf16)
        keys_local = project[:, model_width : 2 * model_width].astype(bf16)
        values_local = (project[:, 2 * model_width :] + bias_value.astype(f32)).astype(bf16)
        keys_all, values_all = (
            lax.all_gather(keys_local, "fsdp", axis=0, tiled=True),
            lax.all_gather(values_local, "fsdp", axis=0, tiled=True),
        )
        labels_all = segments[micro_index]
        labels_query = lax.dynamic_slice_in_dim(labels_all, offset, local_rows)
        query_heads = queries.reshape(local_rows, HEADS, -1)
        key_blocks = keys_all.reshape(key_count, key_rows, HEADS, -1)
        value_blocks = values_all.reshape(key_count, key_rows, HEADS, -1)
        label_blocks = labels_all.reshape(key_count, key_rows)

        def block_scores(key_block, label_block):
            scores = (
                jnp.einsum("qhd,khd->hqk", query_heads, key_block, preferred_element_type=f32)
                * SCALE_SCORE
            )
            allowed = (labels_query[:, None] == label_block[None, :])[None]
            return (jnp.where(allowed, scores, NEG_LARGE), allowed)

        def stat_step(state_in, pieces):
            running_max, running_sum = state_in
            scores, allowed = block_scores(pieces[0], pieces[1])
            newmax = jnp.maximum(running_max, jnp.max(scores, -1))
            exponent = jnp.where(allowed, jnp.exp(scores - newmax[..., None]), 0.0)
            running_sum = running_sum * jnp.exp(running_max - newmax) + jnp.sum(exponent, -1)
            return ((newmax, running_sum), None)

        start_state = (
            jnp.full((HEADS, local_rows), NEG_LARGE, f32),
            jnp.zeros((HEADS, local_rows), f32),
        )
        (final_max, final_sum), _ = lax.scan(stat_step, start_state, (key_blocks, label_blocks))
        log_total = final_max + jnp.log(final_sum)

        def block_prob(key_block, label_block):
            scores, allowed = block_scores(key_block, label_block)
            attend_prob = jnp.where(allowed, jnp.exp(scores - log_total[..., None]), 0.0)
            return (attend_prob, attend_prob.astype(bf16))

        def mix_step(state_in, pieces):
            mixed_acc, extra_acc = state_in
            attend_prob, prob_low = block_prob(pieces[0], pieces[2])
            remainder = (attend_prob - prob_low.astype(f32)).astype(bf16)
            mixed_acc = mixed_acc + jnp.einsum(
                "hqk,khd->qhd", prob_low, pieces[1], preferred_element_type=f32
            )
            extra_acc = extra_acc + jnp.einsum(
                "hqk,khd->qhd", remainder, pieces[1], preferred_element_type=f32
            )
            return ((mixed_acc, extra_acc), None)

        zero_heads = jnp.zeros(query_heads.shape, f32)
        (mixed_heads, extra_heads), _ = lax.scan(
            mix_step, (zero_heads, zero_heads), (key_blocks, value_blocks, label_blocks)
        )
        mixed_low = mixed_heads.reshape(local_rows, model_width).astype(bf16)
        full_mix = mixed_heads + extra_heads
        resid_mid = (
            resid_in
            + jnp.dot(mixed_low, out_full, preferred_element_type=f32)
            + bias_out.astype(f32)
        )
        normed_two = layer_norm(resid_mid, gain_two.astype(f32), shift_two.astype(f32)).astype(bf16)
        pre_act = jnp.dot(normed_two, up_full, preferred_element_type=f32) + bias_up.astype(f32)
        hidden_low = gelu_tanh(pre_act).astype(bf16)
        result = (
            resid_mid
            + jnp.dot(hidden_low, down_full, preferred_element_type=f32)
            + bias_down.astype(f32)
        )
        outputs.append(result.astype(bf16))
        params_bwd = (
            lax.all_gather(norm1_gain, ("dp", "fsdp"), axis=0, tiled=True),
            lax.all_gather(norm1_bias, ("dp", "fsdp"), axis=0, tiled=True),
            lax.all_gather(qkv_weight, ("dp", "fsdp"), axis=0, tiled=True),
            lax.all_gather(query_bias, ("dp", "fsdp"), axis=0, tiled=True),
            lax.all_gather(value_bias, ("dp", "fsdp"), axis=0, tiled=True),
            lax.all_gather(out_weight, ("dp", "fsdp"), axis=0, tiled=True),
            lax.all_gather(out_bias, ("dp", "fsdp"), axis=0, tiled=True),
            lax.all_gather(norm2_gain, ("dp", "fsdp"), axis=0, tiled=True),
            lax.all_gather(norm2_bias, ("dp", "fsdp"), axis=0, tiled=True),
            lax.all_gather(up_weight, ("dp", "fsdp"), axis=0, tiled=True),
            lax.all_gather(up_bias, ("dp", "fsdp"), axis=0, tiled=True),
            lax.all_gather(down_weight, ("dp", "fsdp"), axis=0, tiled=True),
            lax.all_gather(down_bias, ("dp", "fsdp"), axis=0, tiled=True),
        )
        (
            gain_one_b,
            shift_one_b,
            qkv_back,
            bias_query_b,
            bias_value_b,
            out_back,
            bias_out_b,
            gain_two_b,
            shift_two_b,
            up_back,
            bias_up_b,
            down_back,
            bias_down_b,
        ) = params_bwd
        cot_low = cotangent[micro_index]
        cot_full = cot_low.astype(f32)
        grad_down = jnp.einsum("tf,td->fd", hidden_low, cot_low, preferred_element_type=f32)
        grad_bias_down = jnp.sum(cot_full, 0)
        grad_hidden = jnp.einsum("td,fd->tf", cot_low, down_back, preferred_element_type=f32)
        _, gelu_pull = jax.vjp(gelu_tanh, pre_act)
        grad_pre = gelu_pull(grad_hidden)[0].astype(bf16)
        grad_up = jnp.einsum("td,tf->df", normed_two, grad_pre, preferred_element_type=f32)
        grad_bias_up = jnp.sum(grad_pre.astype(f32), 0)
        grad_normed_two = jnp.einsum("tf,df->td", grad_pre, up_back, preferred_element_type=f32)
        _, norm_two_pull = jax.vjp(
            layer_norm, resid_mid, gain_two_b.astype(f32), shift_two_b.astype(f32)
        )
        grad_mid_part, grad_gain_two, grad_shift_two = norm_two_pull(grad_normed_two)
        grad_mid = cot_full + grad_mid_part
        branch_low = grad_mid.astype(bf16)
        grad_out = jnp.einsum("td,te->de", mixed_low, branch_low, preferred_element_type=f32)
        grad_bias_out = jnp.sum(branch_low.astype(f32), 0)
        grad_mixed = jnp.einsum(
            "te,de->td", branch_low, out_back, preferred_element_type=f32
        ).astype(bf16)
        grad_heads = grad_mixed.reshape(local_rows, HEADS, -1)
        delta = jnp.einsum("qhd,qhd->hq", grad_heads.astype(f32), full_mix)

        def grad_step(query_acc, pieces):
            key_block, value_block, label_block = pieces
            attend_prob, prob_low = block_prob(key_block, label_block)
            grad_prob = jnp.einsum(
                "qhd,khd->hqk", grad_heads, value_block, preferred_element_type=f32
            )
            grad_scores = (attend_prob * (grad_prob - delta[..., None]) * SCALE_SCORE).astype(bf16)
            query_acc = query_acc + jnp.einsum(
                "hqk,khd->qhd", grad_scores, key_block, preferred_element_type=f32
            )
            key_part = jnp.einsum(
                "hqk,qhd->khd", grad_scores, query_heads, preferred_element_type=f32
            )
            value_part = jnp.einsum(
                "hqk,qhd->khd", prob_low, grad_heads, preferred_element_type=f32
            )
            return (query_acc, (key_part, value_part))

        query_grad, (key_parts, value_parts) = lax.scan(
            grad_step, zero_heads, (key_blocks, value_blocks, label_blocks)
        )
        key_parts = key_parts.reshape(group_rows, model_width)
        value_parts = value_parts.reshape(group_rows, model_width)
        key_grad, value_grad = (
            lax.psum_scatter(
                key_parts.astype(jnp.bfloat16), "fsdp", scatter_dimension=0, tiled=True
            ).astype(jnp.float32),
            lax.psum_scatter(
                value_parts.astype(jnp.bfloat16), "fsdp", scatter_dimension=0, tiled=True
            ).astype(jnp.float32),
        )
        query_low = query_grad.reshape(local_rows, model_width).astype(bf16)
        key_low = key_grad.astype(bf16)
        value_low = value_grad.astype(bf16)
        grad_project = jnp.concatenate([query_low, key_low, value_low], 1)
        grad_qkv = jnp.einsum("td,te->de", normed_one, grad_project, preferred_element_type=f32)
        grad_bias_query = jnp.sum(query_low.astype(f32), 0)
        grad_bias_value = jnp.sum(value_low.astype(f32), 0)
        grad_normed_one = jnp.einsum(
            "te,de->td", grad_project, qkv_back, preferred_element_type=f32
        )
        _, norm_one_pull = jax.vjp(
            layer_norm, resid_in, gain_one_b.astype(f32), shift_one_b.astype(f32)
        )
        grad_in_part, grad_gain_one, grad_shift_one = norm_one_pull(grad_normed_one)
        in_grads.append(grad_mid + grad_in_part)
        local_terms = (
            grad_gain_one,
            grad_shift_one,
            grad_qkv,
            grad_bias_query,
            grad_bias_value,
            grad_out,
            grad_bias_out,
            grad_gain_two,
            grad_shift_two,
            grad_up,
            grad_bias_up,
            grad_down,
            grad_bias_down,
        )
        shard_terms = (
            lax.psum_scatter(local_terms[0], ("dp", "fsdp"), scatter_dimension=0, tiled=True),
            lax.psum_scatter(local_terms[1], ("dp", "fsdp"), scatter_dimension=0, tiled=True),
            lax.psum_scatter(local_terms[2], ("dp", "fsdp"), scatter_dimension=0, tiled=True),
            lax.psum_scatter(local_terms[3], ("dp", "fsdp"), scatter_dimension=0, tiled=True),
            lax.psum_scatter(local_terms[4], ("dp", "fsdp"), scatter_dimension=0, tiled=True),
            lax.psum_scatter(local_terms[5], ("dp", "fsdp"), scatter_dimension=0, tiled=True),
            lax.psum_scatter(local_terms[6], ("dp", "fsdp"), scatter_dimension=0, tiled=True),
            lax.psum_scatter(local_terms[7], ("dp", "fsdp"), scatter_dimension=0, tiled=True),
            lax.psum_scatter(local_terms[8], ("dp", "fsdp"), scatter_dimension=0, tiled=True),
            lax.psum_scatter(local_terms[9], ("dp", "fsdp"), scatter_dimension=0, tiled=True),
            lax.psum_scatter(local_terms[10], ("dp", "fsdp"), scatter_dimension=0, tiled=True),
            lax.psum_scatter(local_terms[11], ("dp", "fsdp"), scatter_dimension=0, tiled=True),
            lax.psum_scatter(local_terms[12], ("dp", "fsdp"), scatter_dimension=0, tiled=True),
        )
        totals = add_terms(totals, shard_terms)
    return (
        jnp.stack(outputs),
        jnp.stack(in_grads),
        totals[0],
        totals[1],
        totals[2],
        totals[3],
        totals[4],
        totals[5],
        totals[6],
        totals[7],
        totals[8],
        totals[9],
        totals[10],
        totals[11],
        totals[12],
    )


AXES = ("dp", "fsdp")
BIT = {"c": 1, "x": 2, "y": 4, "z": 8, "Z": 16}
DEVICES = 32
VMEM_LIMIT = 56 * 1024 * 1024


def swap(values, bit):
    pairs = [(i, i ^ BIT[bit]) for i in range(DEVICES)]
    return lax.ppermute(values, AXES, pairs)


def slots_of(order):
    return [
        sum(BIT[bit] for place, bit in enumerate(order) if slot >> place & 1)
        for slot in range(DEVICES)
    ]


def gather_piece(shard, order):
    held = shard[None]
    for bit in order:
        held = jnp.concatenate([held, swap(held, bit)], 0)
    return held


def scatter_piece(parts, order):
    f32 = jnp.float32
    for bit in reversed(order):
        half = parts.shape[0] // 2
        got = swap(parts[half:], bit)
        parts = parts[:half].astype(f32) + got.astype(f32)
        if half > 1:
            parts = parts.astype(jnp.bfloat16)
    return parts[0]


def restore_kernel(plan, me_ref, *refs):
    out_ref = refs[-1]
    me = me_ref[0]
    for ref, (order, low, high) in zip(refs[:-1], plan):
        for slot, mask in enumerate(slots_of(order)):
            out_ref[pl.ds(lax.bitwise_xor(me, mask), 1), :, low:high] = ref[slot : slot + 1]


def restore(pieces, plan, me):
    rows, width = pieces[0].shape[1], plan[-1][2]
    vmem = pl.BlockSpec(memory_space=pltpu.VMEM)
    whole = pl.pallas_call(
        functools.partial(restore_kernel, plan),
        out_shape=jax.ShapeDtypeStruct((DEVICES, rows, width), pieces[0].dtype),
        in_specs=[pl.BlockSpec(memory_space=pltpu.SMEM)] + [vmem] * len(pieces),
        out_specs=vmem,
        compiler_params=pltpu.CompilerParams(vmem_limit_bytes=VMEM_LIMIT),
        cost_estimate=pl.CostEstimate(
            flops=0, transcendentals=0, bytes_accessed=4 * DEVICES * rows * width
        ),
    )(me, *pieces)
    return whole


def split_kernel(plan, sources, me_ref, *refs):
    me = me_ref[0]
    for out_ref, (order, low, high) in zip(refs[sources:], plan):
        first = 0
        for ref in refs[:sources]:
            last = first + ref.shape[2]
            begin, end = max(first, low), min(last, high)
            if begin < end:
                for slot, mask in enumerate(slots_of(order)):
                    out_ref[slot : slot + 1, :, begin - low : end - low] = ref[
                        pl.ds(lax.bitwise_xor(me, mask), 1), :, begin - first : end - first
                    ]
            first = last


def split(arrays, plan, me):
    rows = arrays[0].shape[1]
    vmem = pl.BlockSpec(memory_space=pltpu.VMEM)
    total = sum(a.shape[2] for a in arrays)
    return pl.pallas_call(
        functools.partial(split_kernel, plan, len(arrays)),
        out_shape=[
            jax.ShapeDtypeStruct((DEVICES, rows, high - low), arrays[0].dtype)
            for _, low, high in plan
        ],
        in_specs=[pl.BlockSpec(memory_space=pltpu.SMEM)] + [vmem] * len(arrays),
        out_specs=[vmem] * len(plan),
        compiler_params=pltpu.CompilerParams(vmem_limit_bytes=VMEM_LIMIT),
        cost_estimate=pl.CostEstimate(
            flops=0, transcendentals=0, bytes_accessed=4 * DEVICES * rows * total
        ),
    )(me, *arrays)


NT = (((1,), (1,)), ((), ()))


def make_mask(labels_row_ref, labels_col_ref, mask_ref):
    @pl.when(pl.program_id(0) == 0)
    def _():
        allowed = labels_col_ref[...] == labels_row_ref[...]
        mask_ref[...] = jnp.where(allowed, 0.0, NEG_LARGE)


def head_probs(keys, queries, head, mask_ref):
    f32 = jnp.float32
    lane = lax.broadcasted_iota(jnp.int32, queries.shape, 1)
    own = (lane // 64) == head
    chosen = jnp.where(own, queries.astype(f32) * SCALE_SCORE, 0.0).astype(jnp.bfloat16)
    scores = lax.dot_general(keys, chosen, NT, preferred_element_type=f32) + mask_ref[...]
    exponent = jnp.exp(scores - jnp.max(scores, 0, keepdims=True))
    return exponent * (1.0 / jnp.sum(exponent, 0, keepdims=True))


def attend_kernel(row_ref, col_ref, query_ref, key_ref, value_ref, out_ref, mask_ref):
    make_mask(row_ref, col_ref, mask_ref)
    keys, queries = key_ref[...], query_ref[...]
    values_across = value_ref[...].astype(jnp.float32).T.astype(jnp.bfloat16)
    mixed = []
    for head in range(2):
        prob = head_probs(keys, queries, head, mask_ref).astype(jnp.bfloat16)
        mixed.append(
            jnp.dot(
                values_across[64 * head : 64 * head + 64],
                prob,
                preferred_element_type=jnp.float32,
            )
        )
    out_ref[...] = jnp.concatenate(mixed, 0).T.astype(jnp.bfloat16)


def attend_back_kernel(
    row_ref,
    col_ref,
    query_ref,
    key_ref,
    value_ref,
    grad_ref,
    dquery_ref,
    dkey_ref,
    dvalue_ref,
    mask_ref,
):
    f32, bf16 = jnp.float32, jnp.bfloat16
    make_mask(row_ref, col_ref, mask_ref)
    keys, queries, values, grads = key_ref[...], query_ref[...], value_ref[...], grad_ref[...]
    keys_across = keys.astype(f32).T.astype(bf16)
    lane = lax.broadcasted_iota(jnp.int32, keys.shape, 1)
    dquery, dkey, dvalue = [], [], []
    for head in range(2):
        prob = head_probs(keys, queries, head, mask_ref)
        chosen = jnp.where((lane // 64) == head, grads.astype(f32), 0.0).astype(bf16)
        grad_prob = lax.dot_general(values, chosen, NT, preferred_element_type=f32)
        delta = jnp.sum(prob * grad_prob, 0, keepdims=True)
        grad_scores = (prob * (grad_prob - delta)).astype(bf16)
        dvalue.append(jnp.dot(prob.astype(bf16), grads, preferred_element_type=f32))
        dkey.append(jnp.dot(grad_scores, queries, preferred_element_type=f32))
        dquery.append(
            jnp.dot(
                keys_across[64 * head : 64 * head + 64], grad_scores, preferred_element_type=f32
            )
        )
    low_half = lane < 64
    dquery_ref[...] = (jnp.concatenate(dquery, 0).T * SCALE_SCORE).astype(bf16)
    dkey_ref[...] = (jnp.where(low_half, dkey[0], dkey[1]) * SCALE_SCORE).astype(bf16)
    dvalue_ref[...] = jnp.where(low_half, dvalue[0], dvalue[1]).astype(bf16)


def attention_specs(tokens, pairs):
    row = pl.BlockSpec((1, tokens), lambda i: (0, 0))
    col = pl.BlockSpec((tokens, 1), lambda i: (0, 0))
    parts = [
        pl.BlockSpec((tokens, 128), lambda i, part=part: (0, i + part * pairs))
        for part in range(3)
    ]
    return [row, col] + parts


def attend(labels, project):
    tokens, pairs = project.shape[0], HEADS // 2
    return pl.pallas_call(
        attend_kernel,
        grid=(pairs,),
        out_shape=jax.ShapeDtypeStruct((tokens, 128 * pairs), jnp.bfloat16),
        in_specs=attention_specs(tokens, pairs),
        out_specs=pl.BlockSpec((tokens, 128), lambda i: (0, i)),
        scratch_shapes=[pltpu.VMEM((tokens, tokens), jnp.float32)],
        compiler_params=pltpu.CompilerParams(vmem_limit_bytes=VMEM_LIMIT),
        cost_estimate=pl.CostEstimate(
            flops=8 * HEADS * tokens * tokens * 128,
            transcendentals=HEADS * tokens * tokens,
            bytes_accessed=8 * tokens * 128 * pairs,
        ),
    )(labels.reshape(1, tokens), labels.reshape(tokens, 1), project, project, project)


def attend_back(labels, project, grads):
    tokens, pairs = project.shape[0], HEADS // 2
    block = pl.BlockSpec((tokens, 128), lambda i: (0, i))
    shape = jax.ShapeDtypeStruct((tokens, 128 * pairs), jnp.bfloat16)
    return pl.pallas_call(
        attend_back_kernel,
        grid=(pairs,),
        out_shape=[shape] * 3,
        in_specs=attention_specs(tokens, pairs) + [block],
        out_specs=[block] * 3,
        scratch_shapes=[pltpu.VMEM((tokens, tokens), jnp.float32)],
        compiler_params=pltpu.CompilerParams(vmem_limit_bytes=VMEM_LIMIT),
        cost_estimate=pl.CostEstimate(
            flops=20 * HEADS * tokens * tokens * 128,
            transcendentals=HEADS * tokens * tokens,
            bytes_accessed=14 * tokens * 128 * pairs,
        ),
    )(labels.reshape(1, tokens), labels.reshape(tokens, 1), project, project, project, grads)


def norm_parts(values):
    centre = values - jnp.mean(values, -1, keepdims=True)
    scale = lax.rsqrt(jnp.mean(centre * centre, -1, keepdims=True) + EPSILON)
    return centre * scale, scale


def norm_back(grads, unit, scale, gain_vec):
    inner = grads * gain_vec
    part = inner - jnp.mean(inner, -1, keepdims=True)
    part = part - unit * jnp.mean(inner * unit, -1, keepdims=True)
    return part * scale, jnp.sum(grads * unit, 0), jnp.sum(grads, 0)


def pick(values, index, axis=0):
    return lax.dynamic_index_in_dim(values, index, axis, keepdims=False)


def to_micro(values, side, core):
    count, rows, width = values.shape
    halves = values.reshape(2, 2, rows, width)
    got = swap(pick(halves, 1 - side), "x")
    both = jnp.stack([pick(halves, side), got], 1)
    got = swap(pick(both, 1 - core), "c")
    return jnp.stack([pick(both, core), got]).reshape(count * rows, width)


def from_micro(values, side, core):
    rows, width = values.shape[0] // 4, values.shape[1]
    parts = values.reshape(2, 2, rows, width)
    got = swap(parts[1], "c")
    both = jnp.where(core == 0, jnp.stack([parts[0], got]), jnp.stack([got, parts[0]]))
    got = swap(both[:, 1], "x")
    kept = both[:, 0]
    halves = jnp.where(side == 0, jnp.stack([kept, got]), jnp.stack([got, kept]))
    return halves.reshape(4, rows, width)


QKV_PLAN = (("Zzyxc", 0, 1280), ("Zzxyc", 1280, 2432))
OUT_PLAN = (("Zzyxc", 0, 768),)
UP_PLAN = (("Zzxyc", 0, 1536), ("Zzyxc", 1536, 3072))
DOWN_PLAN = (("xyZzc", 0, 384), ("yxZzc", 384, 768))


def gather_plan(shard, plan):
    return [gather_piece(shard[:, low:high], order) for order, low, high in plan]


def scatter_plan(pieces, plan):
    done = [scatter_piece(piece, order) for piece, (order, _, _) in zip(pieces, plan)]
    return done[0] if len(done) == 1 else jnp.concatenate(done, 1)


def on_device_fast(
    inputs,
    segments,
    norm1_gain,
    norm1_bias,
    qkv_weight,
    query_bias,
    value_bias,
    out_weight,
    out_bias,
    norm2_gain,
    norm2_bias,
    up_weight,
    up_bias,
    down_weight,
    down_bias,
    cotangent,
):
    f32, bf16 = jnp.float32, jnp.bfloat16
    local_rows, width = inputs.shape[1], inputs.shape[2]
    rows = width // DEVICES
    group = lax.axis_index("fsdp")
    side, core = group // 2, group % 2
    me = (lax.axis_index("dp") * 4 + group).astype(jnp.int32).reshape(1)

    vectors = jnp.stack(
        [
            norm1_gain,
            norm1_bias,
            query_bias,
            value_bias,
            out_bias,
            norm2_gain,
            norm2_bias,
            down_bias,
        ]
    )
    vectors = jnp.concatenate([vectors, up_bias.reshape(-1, rows)], 0).T
    spare = 128 - vectors.shape[1]
    first = jnp.concatenate([qkv_weight, jnp.pad(vectors, ((0, 0), (0, spare)))], 1)
    qkv_held = gather_plan(first, QKV_PLAN)
    tokens = to_micro(inputs, side, core)
    out_held = gather_plan(out_weight, OUT_PLAN)
    up_held = gather_plan(up_weight, UP_PLAN)
    down_held = gather_plan(down_weight, DOWN_PLAN)
    cot_low = to_micro(cotangent, side, core)

    own = pick(segments, group).reshape(4, local_rows)
    labels = jnp.concatenate(
        [pick(own, lax.bitwise_xor(group, source)) for source in (0, 2, 1, 3)]
    )

    qkv_full = restore(qkv_held, QKV_PLAN, me).reshape(width, -1)
    wide = 3 * width
    vector_rows = qkv_full[:, wide : wide + 12].T.astype(f32)
    qkv_full = qkv_full[:, :wide]
    (
        gain_one,
        shift_one,
        bias_query,
        bias_value,
        bias_out,
        gain_two,
        shift_two,
        bias_down,
    ) = (vector_rows[i] for i in range(8))
    bias_up = vector_rows[8:].reshape(4, DEVICES, rows).transpose(1, 0, 2).reshape(-1)

    resid_in = tokens.astype(f32)
    unit_one, scale_one = norm_parts(resid_in)
    normed_one = (unit_one * gain_one + shift_one).astype(bf16)
    bias_project = jnp.concatenate([bias_query, jnp.zeros_like(bias_query), bias_value])
    project = (
        jnp.dot(normed_one, qkv_full, preferred_element_type=f32) + bias_project
    ).astype(bf16)
    mixed = attend(labels, project)

    out_full = restore(out_held, OUT_PLAN, me).reshape(width, width)
    resid_mid = resid_in + jnp.dot(mixed, out_full, preferred_element_type=f32) + bias_out
    unit_two, scale_two = norm_parts(resid_mid)
    normed_two = (unit_two * gain_two + shift_two).astype(bf16)
    up_full = restore(up_held, UP_PLAN, me).reshape(width, -1)
    pre_act = jnp.dot(normed_two, up_full, preferred_element_type=f32) + bias_up
    cube = pre_act * pre_act
    bend = jnp.tanh(0.7978845608028654 * pre_act * (1.0 + 0.044715 * cube))
    hidden = (0.5 * pre_act * (1.0 + bend)).astype(bf16)
    slope = 0.5 * (1.0 + bend) + 0.5 * pre_act * (1.0 - bend * bend) * (
        0.7978845608028654 * (1.0 + 3 * 0.044715 * cube)
    )

    grad_down = jnp.einsum("tf,td->fd", hidden, cot_low, preferred_element_type=f32).astype(bf16)
    grad_down = split([grad_down.reshape(DEVICES, -1, width)], DOWN_PLAN, me)
    grad_down = scatter_plan(grad_down, DOWN_PLAN)

    down_full = restore(down_held, DOWN_PLAN, me).reshape(-1, width)
    result = resid_mid + jnp.dot(hidden, down_full, preferred_element_type=f32) + bias_down
    output = from_micro(result.astype(bf16), side, core)

    cot_full = cot_low.astype(f32)
    grad_hidden = jnp.einsum("td,fd->tf", cot_low, down_full, preferred_element_type=f32)
    grad_pre = (grad_hidden * slope).astype(bf16)
    grad_up = jnp.einsum("td,tf->df", normed_two, grad_pre, preferred_element_type=f32)
    grad_up = split([grad_up.astype(bf16).reshape(DEVICES, rows, -1)], UP_PLAN, me)
    grad_up = scatter_plan(grad_up, UP_PLAN)
    grad_bias_up = jnp.sum(grad_pre.astype(f32), 0)
    grad_normed_two = jnp.einsum("tf,df->td", grad_pre, up_full, preferred_element_type=f32)
    grad_mid_part, grad_gain_two, grad_shift_two = norm_back(
        grad_normed_two, unit_two, scale_two, gain_two
    )
    grad_mid = cot_full + grad_mid_part
    branch_low = grad_mid.astype(bf16)
    grad_out = jnp.einsum("td,te->de", mixed, branch_low, preferred_element_type=f32)
    grad_out = split([grad_out.astype(bf16).reshape(DEVICES, rows, -1)], OUT_PLAN, me)
    grad_out = scatter_plan(grad_out, OUT_PLAN)
    grad_mixed = jnp.einsum("te,de->td", branch_low, out_full, preferred_element_type=f32)
    grad_query, grad_key, grad_value = attend_back(labels, project, grad_mixed.astype(bf16))
    grad_project = jnp.concatenate([grad_query, grad_key, grad_value], 1)

    grad_qkv = jnp.einsum("td,te->de", normed_one, grad_project, preferred_element_type=f32)
    grad_normed_one = jnp.einsum("te,de->td", grad_project, qkv_full, preferred_element_type=f32)
    grad_in_part, grad_gain_one, grad_shift_one = norm_back(
        grad_normed_one, unit_one, scale_one, gain_one
    )
    in_grad = from_micro((grad_mid + grad_in_part).astype(bf16), side, core).astype(f32)

    sums = jnp.stack(
        [
            grad_gain_one,
            grad_shift_one,
            jnp.sum(grad_query.astype(f32), 0),
            jnp.sum(grad_value.astype(f32), 0),
            jnp.sum(branch_low.astype(f32), 0),
            grad_gain_two,
            grad_shift_two,
            jnp.sum(cot_full, 0),
        ]
    )
    more = grad_bias_up.reshape(DEVICES, 4, rows).transpose(1, 0, 2).reshape(4, width)
    sums = jnp.concatenate([sums, more, jnp.zeros((spare, width), f32)]).T.astype(bf16)
    last = [grad_qkv.astype(bf16).reshape(DEVICES, rows, wide), sums.reshape(DEVICES, rows, 128)]
    last = scatter_plan(split(last, QKV_PLAN, me), QKV_PLAN)
    grad_qkv = last[:, :wide]
    sums = last[:, wide : wide + 12].T
    return (
        output,
        in_grad,
        sums[0],
        sums[1],
        grad_qkv,
        sums[2],
        sums[3],
        grad_out,
        sums[4],
        sums[5],
        sums[6],
        grad_up,
        sums[8:12].reshape(-1),
        grad_down,
        sums[7],
    )


def solution(mesh):
    placed = (
        P(None, ("dp", "fsdp"), None),
        P(None, "dp"),
        P(("dp", "fsdp")),
        P(("dp", "fsdp")),
        P(("dp", "fsdp"), None),
        P(("dp", "fsdp")),
        P(("dp", "fsdp")),
        P(("dp", "fsdp"), None),
        P(("dp", "fsdp")),
        P(("dp", "fsdp")),
        P(("dp", "fsdp")),
        P(("dp", "fsdp"), None),
        P(("dp", "fsdp")),
        P(("dp", "fsdp"), None),
        P(("dp", "fsdp")),
        P(None, ("dp", "fsdp"), None),
    )
    fits = mesh.shape["dp"] == 8 and mesh.shape["fsdp"] == 4
    return jax.shard_map(
        on_device_fast if fits else on_device_general,
        mesh=mesh,
        in_specs=placed,
        out_specs=(
            P(None, ("dp", "fsdp"), None),
            P(None, ("dp", "fsdp"), None),
            P(("dp", "fsdp")),
            P(("dp", "fsdp")),
            P(("dp", "fsdp"), None),
            P(("dp", "fsdp")),
            P(("dp", "fsdp")),
            P(("dp", "fsdp"), None),
            P(("dp", "fsdp")),
            P(("dp", "fsdp")),
            P(("dp", "fsdp")),
            P(("dp", "fsdp"), None),
            P(("dp", "fsdp")),
            P(("dp", "fsdp"), None),
            P(("dp", "fsdp")),
        ),
        check_vma=False,
    )
```

```python
import functools
import math

import jax
import jax.numpy as jnp
from jax import lax
from jax.experimental import pallas as pl
from jax.experimental.pallas import tpu as pltpu
from jax.sharding import PartitionSpec as P

HEADS = 12


EPSILON = 1e-06
NEG_LARGE = -1e30
SCALE_SCORE = 0.125


def layer_norm(values, gain_vec, shift_vec):
    centre = values - jnp.mean(values, -1, keepdims=True)
    spread = jnp.mean(centre * centre, -1, keepdims=True)
    return centre * lax.rsqrt(spread + EPSILON) * gain_vec + shift_vec


def gelu_tanh(values):
    return (
        0.5
        * values
        * (1.0 + jnp.tanh(0.7978845608028654 * (values + 0.044715 * values * values * values)))
    )


def add_terms(first_terms, second_terms):
    if first_terms is None:
        return second_terms
    return jax.tree.map(jnp.add, first_terms, second_terms)


def on_device_general(
    inputs,
    segments,
    norm1_gain,
    norm1_bias,
    qkv_weight,
    query_bias,
    value_bias,
    out_weight,
    out_bias,
    norm2_gain,
    norm2_bias,
    up_weight,
    up_bias,
    down_weight,
    down_bias,
    cotangent,
):
    micro_count = inputs.shape[0]
    local_rows = inputs.shape[1]
    model_width = inputs.shape[2]
    group_rows = segments.shape[1]
    key_rows = math.gcd(512, group_rows)
    key_count = group_rows // key_rows
    offset = lax.axis_index("fsdp") * local_rows
    f32 = jnp.float32
    bf16 = jnp.bfloat16
    outputs = []
    in_grads = []
    totals = None
    for micro_index in range(micro_count):
        params_fwd = (
            lax.all_gather(norm1_gain, ("dp", "fsdp"), axis=0, tiled=True),
            lax.all_gather(norm1_bias, ("dp", "fsdp"), axis=0, tiled=True),
            lax.all_gather(qkv_weight, ("dp", "fsdp"), axis=0, tiled=True),
            lax.all_gather(query_bias, ("dp", "fsdp"), axis=0, tiled=True),
            lax.all_gather(value_bias, ("dp", "fsdp"), axis=0, tiled=True),
            lax.all_gather(out_weight, ("dp", "fsdp"), axis=0, tiled=True),
            lax.all_gather(out_bias, ("dp", "fsdp"), axis=0, tiled=True),
            lax.all_gather(norm2_gain, ("dp", "fsdp"), axis=0, tiled=True),
            lax.all_gather(norm2_bias, ("dp", "fsdp"), axis=0, tiled=True),
            lax.all_gather(up_weight, ("dp", "fsdp"), axis=0, tiled=True),
            lax.all_gather(up_bias, ("dp", "fsdp"), axis=0, tiled=True),
            lax.all_gather(down_weight, ("dp", "fsdp"), axis=0, tiled=True),
            lax.all_gather(down_bias, ("dp", "fsdp"), axis=0, tiled=True),
        )
        (
            gain_one,
            shift_one,
            qkv_full,
            bias_query,
            bias_value,
            out_full,
            bias_out,
            gain_two,
            shift_two,
            up_full,
            bias_up,
            down_full,
            bias_down,
        ) = params_fwd
        resid_in = inputs[micro_index].astype(f32)
        normed_one = layer_norm(resid_in, gain_one.astype(f32), shift_one.astype(f32)).astype(bf16)
        project = jnp.dot(normed_one, qkv_full, preferred_element_type=f32)
        queries = (project[:, :model_width] + bias_query.astype(f32)).astype(bf16)
        keys_local = project[:, model_width : 2 * model_width].astype(bf16)
        values_local = (project[:, 2 * model_width :] + bias_value.astype(f32)).astype(bf16)
        keys_all, values_all = (
            lax.all_gather(keys_local, "fsdp", axis=0, tiled=True),
            lax.all_gather(values_local, "fsdp", axis=0, tiled=True),
        )
        labels_all = segments[micro_index]
        labels_query = lax.dynamic_slice_in_dim(labels_all, offset, local_rows)
        query_heads = queries.reshape(local_rows, HEADS, -1)
        key_blocks = keys_all.reshape(key_count, key_rows, HEADS, -1)
        value_blocks = values_all.reshape(key_count, key_rows, HEADS, -1)
        label_blocks = labels_all.reshape(key_count, key_rows)

        def block_scores(key_block, label_block):
            scores = (
                jnp.einsum("qhd,khd->hqk", query_heads, key_block, preferred_element_type=f32)
                * SCALE_SCORE
            )
            allowed = (labels_query[:, None] == label_block[None, :])[None]
            return (jnp.where(allowed, scores, NEG_LARGE), allowed)

        def stat_step(state_in, pieces):
            running_max, running_sum = state_in
            scores, allowed = block_scores(pieces[0], pieces[1])
            newmax = jnp.maximum(running_max, jnp.max(scores, -1))
            exponent = jnp.where(allowed, jnp.exp(scores - newmax[..., None]), 0.0)
            running_sum = running_sum * jnp.exp(running_max - newmax) + jnp.sum(exponent, -1)
            return ((newmax, running_sum), None)

        start_state = (
            jnp.full((HEADS, local_rows), NEG_LARGE, f32),
            jnp.zeros((HEADS, local_rows), f32),
        )
        (final_max, final_sum), _ = lax.scan(stat_step, start_state, (key_blocks, label_blocks))
        log_total = final_max + jnp.log(final_sum)

        def block_prob(key_block, label_block):
            scores, allowed = block_scores(key_block, label_block)
            attend_prob = jnp.where(allowed, jnp.exp(scores - log_total[..., None]), 0.0)
            return (attend_prob, attend_prob.astype(bf16))

        def mix_step(state_in, pieces):
            mixed_acc, extra_acc = state_in
            attend_prob, prob_low = block_prob(pieces[0], pieces[2])
            remainder = (attend_prob - prob_low.astype(f32)).astype(bf16)
            mixed_acc = mixed_acc + jnp.einsum(
                "hqk,khd->qhd", prob_low, pieces[1], preferred_element_type=f32
            )
            extra_acc = extra_acc + jnp.einsum(
                "hqk,khd->qhd", remainder, pieces[1], preferred_element_type=f32
            )
            return ((mixed_acc, extra_acc), None)

        zero_heads = jnp.zeros(query_heads.shape, f32)
        (mixed_heads, extra_heads), _ = lax.scan(
            mix_step, (zero_heads, zero_heads), (key_blocks, value_blocks, label_blocks)
        )
        mixed_low = mixed_heads.reshape(local_rows, model_width).astype(bf16)
        full_mix = mixed_heads + extra_heads
        resid_mid = (
            resid_in
            + jnp.dot(mixed_low, out_full, preferred_element_type=f32)
            + bias_out.astype(f32)
        )
        normed_two = layer_norm(resid_mid, gain_two.astype(f32), shift_two.astype(f32)).astype(bf16)
        pre_act = jnp.dot(normed_two, up_full, preferred_element_type=f32) + bias_up.astype(f32)
        hidden_low = gelu_tanh(pre_act).astype(bf16)
        result = (
            resid_mid
            + jnp.dot(hidden_low, down_full, preferred_element_type=f32)
            + bias_down.astype(f32)
        )
        outputs.append(result.astype(bf16))
        params_bwd = (
            lax.all_gather(norm1_gain, ("dp", "fsdp"), axis=0, tiled=True),
            lax.all_gather(norm1_bias, ("dp", "fsdp"), axis=0, tiled=True),
            lax.all_gather(qkv_weight, ("dp", "fsdp"), axis=0, tiled=True),
            lax.all_gather(query_bias, ("dp", "fsdp"), axis=0, tiled=True),
            lax.all_gather(value_bias, ("dp", "fsdp"), axis=0, tiled=True),
            lax.all_gather(out_weight, ("dp", "fsdp"), axis=0, tiled=True),
            lax.all_gather(out_bias, ("dp", "fsdp"), axis=0, tiled=True),
            lax.all_gather(norm2_gain, ("dp", "fsdp"), axis=0, tiled=True),
            lax.all_gather(norm2_bias, ("dp", "fsdp"), axis=0, tiled=True),
            lax.all_gather(up_weight, ("dp", "fsdp"), axis=0, tiled=True),
            lax.all_gather(up_bias, ("dp", "fsdp"), axis=0, tiled=True),
            lax.all_gather(down_weight, ("dp", "fsdp"), axis=0, tiled=True),
            lax.all_gather(down_bias, ("dp", "fsdp"), axis=0, tiled=True),
        )
        (
            gain_one_b,
            shift_one_b,
            qkv_back,
            bias_query_b,
            bias_value_b,
            out_back,
            bias_out_b,
            gain_two_b,
            shift_two_b,
            up_back,
            bias_up_b,
            down_back,
            bias_down_b,
        ) = params_bwd
        cot_low = cotangent[micro_index]
        cot_full = cot_low.astype(f32)
        grad_down = jnp.einsum("tf,td->fd", hidden_low, cot_low, preferred_element_type=f32)
        grad_bias_down = jnp.sum(cot_full, 0)
        grad_hidden = jnp.einsum("td,fd->tf", cot_low, down_back, preferred_element_type=f32)
        _, gelu_pull = jax.vjp(gelu_tanh, pre_act)
        grad_pre = gelu_pull(grad_hidden)[0].astype(bf16)
        grad_up = jnp.einsum("td,tf->df", normed_two, grad_pre, preferred_element_type=f32)
        grad_bias_up = jnp.sum(grad_pre.astype(f32), 0)
        grad_normed_two = jnp.einsum("tf,df->td", grad_pre, up_back, preferred_element_type=f32)
        _, norm_two_pull = jax.vjp(
            layer_norm, resid_mid, gain_two_b.astype(f32), shift_two_b.astype(f32)
        )
        grad_mid_part, grad_gain_two, grad_shift_two = norm_two_pull(grad_normed_two)
        grad_mid = cot_full + grad_mid_part
        branch_low = grad_mid.astype(bf16)
        grad_out = jnp.einsum("td,te->de", mixed_low, branch_low, preferred_element_type=f32)
        grad_bias_out = jnp.sum(branch_low.astype(f32), 0)
        grad_mixed = jnp.einsum(
            "te,de->td", branch_low, out_back, preferred_element_type=f32
        ).astype(bf16)
        grad_heads = grad_mixed.reshape(local_rows, HEADS, -1)
        delta = jnp.einsum("qhd,qhd->hq", grad_heads.astype(f32), full_mix)

        def grad_step(query_acc, pieces):
            key_block, value_block, label_block = pieces
            attend_prob, prob_low = block_prob(key_block, label_block)
            grad_prob = jnp.einsum(
                "qhd,khd->hqk", grad_heads, value_block, preferred_element_type=f32
            )
            grad_scores = (attend_prob * (grad_prob - delta[..., None]) * SCALE_SCORE).astype(bf16)
            query_acc = query_acc + jnp.einsum(
                "hqk,khd->qhd", grad_scores, key_block, preferred_element_type=f32
            )
            key_part = jnp.einsum(
                "hqk,qhd->khd", grad_scores, query_heads, preferred_element_type=f32
            )
            value_part = jnp.einsum(
                "hqk,qhd->khd", prob_low, grad_heads, preferred_element_type=f32
            )
            return (query_acc, (key_part, value_part))

        query_grad, (key_parts, value_parts) = lax.scan(
            grad_step, zero_heads, (key_blocks, value_blocks, label_blocks)
        )
        key_parts = key_parts.reshape(group_rows, model_width)
        value_parts = value_parts.reshape(group_rows, model_width)
        key_grad, value_grad = (
            lax.psum_scatter(
                key_parts.astype(jnp.bfloat16), "fsdp", scatter_dimension=0, tiled=True
            ).astype(jnp.float32),
            lax.psum_scatter(
                value_parts.astype(jnp.bfloat16), "fsdp", scatter_dimension=0, tiled=True
            ).astype(jnp.float32),
        )
        query_low = query_grad.reshape(local_rows, model_width).astype(bf16)
        key_low = key_grad.astype(bf16)
        value_low = value_grad.astype(bf16)
        grad_project = jnp.concatenate([query_low, key_low, value_low], 1)
        grad_qkv = jnp.einsum("td,te->de", normed_one, grad_project, preferred_element_type=f32)
        grad_bias_query = jnp.sum(query_low.astype(f32), 0)
        grad_bias_value = jnp.sum(value_low.astype(f32), 0)
        grad_normed_one = jnp.einsum(
            "te,de->td", grad_project, qkv_back, preferred_element_type=f32
        )
        _, norm_one_pull = jax.vjp(
            layer_norm, resid_in, gain_one_b.astype(f32), shift_one_b.astype(f32)
        )
        grad_in_part, grad_gain_one, grad_shift_one = norm_one_pull(grad_normed_one)
        in_grads.append(grad_mid + grad_in_part)
        local_terms = (
            grad_gain_one,
            grad_shift_one,
            grad_qkv,
            grad_bias_query,
            grad_bias_value,
            grad_out,
            grad_bias_out,
            grad_gain_two,
            grad_shift_two,
            grad_up,
            grad_bias_up,
            grad_down,
            grad_bias_down,
        )
        shard_terms = (
            lax.psum_scatter(local_terms[0], ("dp", "fsdp"), scatter_dimension=0, tiled=True),
            lax.psum_scatter(local_terms[1], ("dp", "fsdp"), scatter_dimension=0, tiled=True),
            lax.psum_scatter(local_terms[2], ("dp", "fsdp"), scatter_dimension=0, tiled=True),
            lax.psum_scatter(local_terms[3], ("dp", "fsdp"), scatter_dimension=0, tiled=True),
            lax.psum_scatter(local_terms[4], ("dp", "fsdp"), scatter_dimension=0, tiled=True),
            lax.psum_scatter(local_terms[5], ("dp", "fsdp"), scatter_dimension=0, tiled=True),
            lax.psum_scatter(local_terms[6], ("dp", "fsdp"), scatter_dimension=0, tiled=True),
            lax.psum_scatter(local_terms[7], ("dp", "fsdp"), scatter_dimension=0, tiled=True),
            lax.psum_scatter(local_terms[8], ("dp", "fsdp"), scatter_dimension=0, tiled=True),
            lax.psum_scatter(local_terms[9], ("dp", "fsdp"), scatter_dimension=0, tiled=True),
            lax.psum_scatter(local_terms[10], ("dp", "fsdp"), scatter_dimension=0, tiled=True),
            lax.psum_scatter(local_terms[11], ("dp", "fsdp"), scatter_dimension=0, tiled=True),
            lax.psum_scatter(local_terms[12], ("dp", "fsdp"), scatter_dimension=0, tiled=True),
        )
        totals = add_terms(totals, shard_terms)
    return (
        jnp.stack(outputs),
        jnp.stack(in_grads),
        totals[0],
        totals[1],
        totals[2],
        totals[3],
        totals[4],
        totals[5],
        totals[6],
        totals[7],
        totals[8],
        totals[9],
        totals[10],
        totals[11],
        totals[12],
    )


AXES = ("dp", "fsdp")
CORE, X, Y, Z0, Z1 = 1, 2, 4, 8, 16
LINE = (0, Z1, Z0, Z1 ^ Z0)
PLANE = (0, X, Y, X ^ Y)
DEVICES = 32
MIB = 1024 * 1024
SMALL = pl.CostEstimate(flops=1024, transcendentals=0, bytes_accessed=1024)


def swap(values, mask):
    pairs = [(i, i ^ mask) for i in range(DEVICES)]
    return lax.ppermute(values, AXES, pairs)


SLOTS = [core ^ plane ^ line for core in (0, CORE) for plane in PLANE for line in LINE]


def fence(*values):
    return lax.optimization_barrier(values)


def join(*parts):
    return lax.optimization_barrier(jnp.concatenate(parts, 0))


class Gather:
    def __init__(self, shard):
        self.held = shard[None]
        self.across = []

    def line(self):
        self.got = [swap(self.held, mask) for mask in LINE[1:]]

    def far(self):
        self.got = [swap(self.held, Z1)]

    def near(self):
        self.held = join(self.held, *self.got)
        self.got = [swap(self.held, Z0)]

    def plane(self):
        self.held = join(self.held, *self.got)
        self.got = [swap(self.held, mask) for mask in PLANE[1:]]

    def cores_early(self):
        self.across = [swap(self.held, CORE)]

    def cores(self):
        own = [self.held, *self.got]
        self.parts = own + self.across + [swap(piece, CORE) for piece in own[len(self.across) :]]

    def places(self):
        masks = [core ^ plane ^ line for core in (0, CORE) for plane in PLANE for line in LINE]
        width = self.held.shape[2]
        return [(i // 4, i % 4, mask, 0, width) for i, mask in enumerate(masks)]


def sum_low(*terms):
    total = sum(term.astype(jnp.float32) for term in terms)
    return total.astype(jnp.bfloat16)


class Scatter:
    places = [
        (slot // 16, slot % 16, core ^ plane ^ line)
        for slot, (core, plane, line) in enumerate(
            (core, plane, line) for core in (0, CORE) for plane in PLANE for line in LINE
        )
    ]

    def __init__(self, halves):
        self.kept, self.sent = halves

    def cores(self):
        self.got = swap(self.sent, CORE)

    def plane(self):
        self.kept, *quads = [
            sum_low(self.kept[4 * i : 4 * i + 4], self.got[4 * i : 4 * i + 4]) for i in range(4)
        ]
        self.got = [swap(quad, mask) for quad, mask in zip(quads, PLANE[1:])]

    def line(self):
        terms = [self.kept, *self.got]
        ones = [sum_low(*(term[i : i + 1] for term in terms)) for i in range(1, 4)]
        self.kept = sum(term[0].astype(jnp.float32) for term in terms)
        self.got = [swap(one, mask) for one, mask in zip(ones, LINE[1:])]

    def near(self):
        terms = [self.kept, *self.got]
        self.kept = sum_low(*(term[:2] for term in terms))
        self.got = [swap(sum_low(*(term[2:] for term in terms)), Z0)]

    def far(self):
        got = self.got[0]
        self.got = [swap(sum_low(self.kept[1:], got[1:]), Z1)]
        self.kept = self.kept[0].astype(jnp.float32) + got[0].astype(jnp.float32)

    def total(self):
        return self.kept + sum(got[0].astype(jnp.float32) for got in self.got)


def cuts_of(parts):
    ends = [sum(parts[: i + 1]) for i in range(len(parts))]
    return tuple((end - part, end) for end, part in zip(ends, parts))


def shuffle_kernel(moves, count, me_ref, *refs):
    me = me_ref[0]

    def part(slot):
        return pl.ds(lax.bitwise_xor(me, slot[0]) if isinstance(slot, tuple) else slot, 1)

    for source, source_slot, source_low, target, target_slot, target_low, width in moves:
        refs[count + target][part(target_slot), :, target_low : target_low + width] = refs[source][
            part(source_slot), :, source_low : source_low + width
        ]


def whole_block(shape):
    return pl.BlockSpec(shape, lambda i: (0,) * len(shape), pipeline_mode=pl.Buffered(1))


def shuffle(arrays, shapes, moves, me, pinned):
    dtype = arrays[0].dtype
    size = sum(math.prod(shape) for shape in shapes)
    make = pltpu.HBM if pinned else jax.ShapeDtypeStruct
    return pl.pallas_call(
        functools.partial(shuffle_kernel, moves, len(arrays)),
        grid=(1,),
        out_shape=[make(shape, dtype) for shape in shapes],
        in_specs=[pl.BlockSpec(memory_space=pltpu.SMEM)]
        + [whole_block(array.shape) for array in arrays],
        out_specs=[whole_block(shape) for shape in shapes],
        compiler_params=pltpu.CompilerParams(vmem_limit_bytes=16 * MIB),
        cost_estimate=SMALL,
    )(me, *arrays)


def restore(gather, cuts, me):
    moves = []
    for part, slot, mask, low, high in gather.places():
        for target, (begin, end) in enumerate(cuts):
            left, right = max(low, begin), min(high, end)
            if left < right:
                moves.append(
                    (part, slot, left - low, target, (mask,), left - begin, right - left)
                )
    rows = gather.parts[0].shape[1]
    shapes = [(DEVICES, rows, end - begin) for begin, end in cuts]
    return shuffle(gather.parts, shapes, moves, me, True)


TN = (((0,), (0,)), ((), ()))


def parts_call(kernel, inputs, rows, width, scratch, limit, me):
    half = (DEVICES // 2, rows, width)
    return pl.pallas_call(
        kernel,
        grid=(1,),
        out_shape=[jax.ShapeDtypeStruct(half, jnp.bfloat16)] * 2,
        in_specs=[pl.BlockSpec(memory_space=pltpu.SMEM)]
        + [whole_block(value.shape) for value in inputs],
        out_specs=[whole_block(half)] * 2,
        scratch_shapes=[pltpu.VMEM(scratch, jnp.float32)],
        compiler_params=pltpu.CompilerParams(vmem_limit_bytes=limit * MIB),
        cost_estimate=SMALL,
    )(me, *inputs)


def store_rows(me, sum_ref, outs, low, high):
    rows = sum_ref.shape[0] // DEVICES
    for half, slot, mask in Scatter.places:
        first = pl.multiple_of(lax.bitwise_xor(me, mask) * rows, rows)
        outs[half][slot, :, low:high] = sum_ref[pl.ds(first, rows), : high - low].astype(
            jnp.bfloat16
        )


def multiply_rows(me, left_ref, right_refs, sum_ref, outs, low):
    width = sum_ref.shape[1]
    for ref in right_refs:
        for begin in range(0, ref.shape[1], width):
            sum_ref[...] = lax.dot_general(
                left_ref[...],
                ref[:, begin : begin + width],
                TN,
                preferred_element_type=jnp.float32,
            )
            store_rows(me, sum_ref, outs, low + begin, low + begin + width)
        low += ref.shape[1]
    return low


def second_parts_kernel(
    me_ref, mixed_ref, branch_ref, normed_ref, pre_ref, kept_ref, sent_ref, sum_ref
):
    me, outs = me_ref[0], (kept_ref, sent_ref)
    low = multiply_rows(me, mixed_ref, [branch_ref], sum_ref, outs, 0)
    multiply_rows(me, normed_ref, [pre_ref], sum_ref, outs, low)


def first_parts_kernel(
    me_ref, normed_ref, query_ref, key_ref, value_ref, sums_ref, kept_ref, sent_ref, sum_ref
):
    me, outs = me_ref[0], (kept_ref, sent_ref)
    low = multiply_rows(me, normed_ref, [query_ref, key_ref, value_ref], sum_ref, outs, 0)
    for half, slot, mask in Scatter.places:
        outs[half][slot, :, low:] = sums_ref[lax.bitwise_xor(me, mask)]


def third_parts_kernel(me_ref, hidden_ref, cot_ref, kept_ref, sent_ref, sum_ref):
    me, outs = me_ref[0], (kept_ref, sent_ref)
    rows = kept_ref.shape[1]
    for block in range(DEVICES // 4):
        first = pl.multiple_of(lax.bitwise_xor(me // 4, block) * (4 * rows), 4 * rows)
        sum_ref[...] = lax.dot_general(
            hidden_ref[:, pl.ds(first, 4 * rows)],
            cot_ref[...],
            TN,
            preferred_element_type=jnp.float32,
        )
        for half, slot, mask in Scatter.places:
            if mask // 4 == block:
                first = pl.multiple_of(lax.bitwise_xor(me % 4, mask % 4) * rows, rows)
                outs[half][slot] = sum_ref[pl.ds(first, rows)].astype(jnp.bfloat16)


NT = (((1,), (1,)), ((), ()))


def make_mask(labels_row_ref, labels_col_ref, mask_ref):
    @pl.when(pl.program_id(0) == 0)
    def _():
        allowed = labels_col_ref[...] == labels_row_ref[...]
        mask_ref[...] = jnp.where(allowed, 0.0, NEG_LARGE)


def head_probs(keys, queries, head, mask_ref):
    f32 = jnp.float32
    lane = lax.broadcasted_iota(jnp.int32, queries.shape, 1)
    own = (lane // 64) == head
    chosen = jnp.where(own, queries.astype(f32) * SCALE_SCORE, 0.0).astype(jnp.bfloat16)
    scores = lax.dot_general(keys, chosen, NT, preferred_element_type=f32) + mask_ref[...]
    exponent = jnp.exp(scores - jnp.max(scores, 0, keepdims=True))
    return exponent * (1.0 / jnp.sum(exponent, 0, keepdims=True))


def attend_kernel(row_ref, col_ref, query_ref, key_ref, value_ref, out_ref, prob_ref, mask_ref):
    make_mask(row_ref, col_ref, mask_ref)
    keys, queries = key_ref[...], query_ref[...]
    values_across = value_ref[...].astype(jnp.float32).T.astype(jnp.bfloat16)
    mixed = []
    for head in range(2):
        prob_ref[head] = head_probs(keys, queries, head, mask_ref).astype(jnp.bfloat16)
        mixed.append(
            jnp.dot(
                values_across[64 * head : 64 * head + 64],
                prob_ref[head],
                preferred_element_type=jnp.float32,
            )
        )
    out_ref[...] = jnp.concatenate(mixed, 0).T.astype(jnp.bfloat16)


def attend_back_kernel(
    query_ref, key_ref, value_ref, prob_ref, grad_ref, dquery_ref, dkey_ref, dvalue_ref
):
    f32, bf16 = jnp.float32, jnp.bfloat16
    keys, queries, values, grads = key_ref[...], query_ref[...], value_ref[...], grad_ref[...]
    keys_across = keys.astype(f32).T.astype(bf16)
    lane = lax.broadcasted_iota(jnp.int32, keys.shape, 1)
    dquery, dkey, dvalue = [], [], []
    for head in range(2):
        chosen = jnp.where((lane // 64) == head, grads.astype(f32), 0.0).astype(bf16)
        grad_prob = lax.dot_general(values, chosen, NT, preferred_element_type=f32)
        prob = prob_ref[head].astype(f32)
        delta = jnp.sum(prob * grad_prob, 0, keepdims=True)
        grad_scores = (prob * (grad_prob - delta)).astype(bf16)
        dvalue.append(jnp.dot(prob_ref[head], grads, preferred_element_type=f32))
        dkey.append(jnp.dot(grad_scores, queries, preferred_element_type=f32))
        dquery.append(
            jnp.dot(
                keys_across[64 * head : 64 * head + 64], grad_scores, preferred_element_type=f32
            )
        )
    low_half = lane < 64
    dquery_ref[...] = (jnp.concatenate(dquery, 0).T * SCALE_SCORE).astype(bf16)
    dkey_ref[...] = (jnp.where(low_half, dkey[0], dkey[1]) * SCALE_SCORE).astype(bf16)
    dvalue_ref[...] = jnp.where(low_half, dvalue[0], dvalue[1]).astype(bf16)


def pair_specs(tokens, pairs):
    parts = [
        pl.BlockSpec((tokens, 128), lambda i, part=part: (0, i + part * pairs))
        for part in range(3)
    ]
    return parts, pl.BlockSpec((2, tokens, tokens), lambda i: (i, 0, 0))


def in_hbm(array):
    return pltpu.with_memory_space_constraint(array, pltpu.HBM)


def attend(labels, project):
    tokens, pairs = project.shape[0], HEADS // 2
    parts, probs = pair_specs(tokens, pairs)
    return pl.pallas_call(
        attend_kernel,
        grid=(pairs,),
        out_shape=[
            jax.ShapeDtypeStruct((tokens, 128 * pairs), jnp.bfloat16),
            pltpu.HBM((HEADS, tokens, tokens), jnp.bfloat16),
        ],
        in_specs=[
            pl.BlockSpec((1, tokens), lambda i: (0, 0)),
            pl.BlockSpec((tokens, 1), lambda i: (0, 0)),
            *parts,
        ],
        out_specs=[pl.BlockSpec((tokens, 128), lambda i: (0, i)), probs],
        scratch_shapes=[pltpu.VMEM((tokens, tokens), jnp.float32)],
        compiler_params=pltpu.CompilerParams(vmem_limit_bytes=12 * MIB),
        cost_estimate=SMALL,
    )(labels.reshape(1, tokens), labels.reshape(tokens, 1), project, project, project)


def attend_back(project, probs, grads):
    tokens, pairs = project.shape[0], HEADS // 2
    block = pl.BlockSpec((tokens, 128), lambda i: (0, i))
    shape = jax.ShapeDtypeStruct((tokens, 128 * pairs), jnp.bfloat16)
    parts, prob_spec = pair_specs(tokens, pairs)
    return pl.pallas_call(
        attend_back_kernel,
        grid=(pairs,),
        out_shape=[shape] * 3,
        in_specs=[*parts, prob_spec, block],
        out_specs=[block] * 3,
        compiler_params=pltpu.CompilerParams(vmem_limit_bytes=14 * MIB),
        cost_estimate=SMALL,
    )(project, project, project, in_hbm(probs), grads)


def norm_parts(values):
    centre = values - jnp.mean(values, -1, keepdims=True)
    scale = lax.rsqrt(jnp.mean(centre * centre, -1, keepdims=True) + EPSILON)
    return centre * scale, scale


def norm_back(grads, values, gain_row):
    unit, scale = norm_parts(values)
    inner = grads * gain_row
    part = inner - jnp.mean(inner, -1, keepdims=True)
    part = part - unit * jnp.mean(inner * unit, -1, keepdims=True)
    gain, shift = jnp.sum(grads * unit, 0, keepdims=True), jnp.sum(grads, 0, keepdims=True)
    return part * scale, gain, shift


def column_sum(values):
    return jnp.sum(values.astype(jnp.float32), 0, keepdims=True)


def up_kernel(normed_ref, weight_ref, bias_ref, hidden_ref, slope_ref):
    bf16 = jnp.bfloat16
    pre = jnp.dot(normed_ref[...], weight_ref[...], preferred_element_type=jnp.float32)
    pre = pre + bias_ref[...]
    square = pre * pre
    bend = jnp.tanh(pre * (0.7978845608028654 + 0.7978845608028654 * 0.044715 * square))
    half = 0.5 * (1.0 + bend)
    hidden_ref[...] = (pre * half).astype(bf16)
    inner = 0.7978845608028654 + 3 * 0.7978845608028654 * 0.044715 * square
    slope_ref[...] = (half + 0.5 * pre * (1.0 - bend * bend) * inner).astype(bf16)


def up_forward(normed, up_full, bias_row):
    tokens, width = normed.shape
    inner, tile = up_full.shape[1], 512
    block = pl.BlockSpec((tokens, tile), lambda i: (0, i))
    shape = jax.ShapeDtypeStruct((tokens, inner), jnp.bfloat16)
    return pl.pallas_call(
        up_kernel,
        grid=(inner // tile,),
        out_shape=[shape, shape],
        in_specs=[
            pl.BlockSpec((tokens, width), lambda i: (0, 0)),
            pl.BlockSpec((width, tile), lambda i: (0, i)),
            pl.BlockSpec((1, tile), lambda i: (0, i)),
        ],
        out_specs=[block, block],
        compiler_params=pltpu.CompilerParams(vmem_limit_bytes=14 * MIB),
        cost_estimate=SMALL,
    )(normed, in_hbm(up_full), bias_row)


def pre_kernel(cot_ref, weight_ref, slope_ref, pre_ref, sum_ref):
    f32 = jnp.float32
    grads = lax.dot_general(cot_ref[...], weight_ref[...], NT, preferred_element_type=f32)
    low = (grads * slope_ref[...].astype(f32)).astype(jnp.bfloat16)
    pre_ref[...] = low
    sum_ref[...] = column_sum(low)


def pre_back(cot_low, down_full, slope):
    tokens, width = cot_low.shape
    inner, tile = down_full.shape[0], 512
    block = pl.BlockSpec((tokens, tile), lambda i: (0, i))
    return pl.pallas_call(
        pre_kernel,
        grid=(inner // tile,),
        out_shape=[
            jax.ShapeDtypeStruct((tokens, inner), jnp.bfloat16),
            jax.ShapeDtypeStruct((1, inner), jnp.float32),
        ],
        in_specs=[
            pl.BlockSpec((tokens, width), lambda i: (0, 0)),
            pl.BlockSpec((tile, width), lambda i: (i, 0)),
            block,
        ],
        out_specs=[block, pl.BlockSpec((1, tile), lambda i: (0, i))],
        compiler_params=pltpu.CompilerParams(vmem_limit_bytes=12 * MIB),
        cost_estimate=SMALL,
    )(cot_low, in_hbm(down_full), slope)


def middle_kernel(pre_ref, up_ref, resid_ref, gain_ref, cot_ref, out_ref, mid_ref, low_ref, mixed_ref, sums_ref):
    f32, bf16 = jnp.float32, jnp.bfloat16

    @pl.when(pl.program_id(0) == 0)
    def _():
        sums_ref[...] = jnp.zeros_like(sums_ref)

    grads = lax.dot_general(pre_ref[...], up_ref[...], NT, preferred_element_type=f32)
    part, gain, shift = norm_back(grads, resid_ref[...], gain_ref[...])
    cot = cot_ref[...].astype(f32)
    mid = cot + part
    low = mid.astype(bf16)
    mid_ref[...] = mid
    low_ref[...] = low
    mixed_ref[...] = lax.dot_general(
        low, out_ref[...], NT, preferred_element_type=f32
    ).astype(bf16)
    for row, value in enumerate((column_sum(low), gain, shift, column_sum(cot))):
        sums_ref[row : row + 1] += value


def middle_back(grad_pre, up_full, resid_mid, gain_row, cot_low, out_full):
    tokens, inner = grad_pre.shape
    width, tile = resid_mid.shape[1], 256
    block = pl.BlockSpec((tile, width), lambda i: (i, 0))
    whole = lambda *shape: pl.BlockSpec(shape, lambda i: (0, 0))
    return pl.pallas_call(
        middle_kernel,
        grid=(tokens // tile,),
        out_shape=[
            jax.ShapeDtypeStruct((tokens, width), jnp.float32),
            jax.ShapeDtypeStruct((tokens, width), jnp.bfloat16),
            jax.ShapeDtypeStruct((tokens, width), jnp.bfloat16),
            jax.ShapeDtypeStruct((8, width), jnp.float32),
        ],
        in_specs=[
            pl.BlockSpec((tile, inner), lambda i: (i, 0)),
            whole(width, inner),
            block,
            whole(1, width),
            block,
            whole(width, width),
        ],
        out_specs=[block, block, block, whole(8, width)],
        compiler_params=pltpu.CompilerParams(vmem_limit_bytes=20 * MIB),
        cost_estimate=SMALL,
    )(grad_pre, up_full, resid_mid, gain_row, cot_low, out_full)


def first_kernel(
    query_ref, key_ref, value_ref, weight_ref, token_ref, gain_ref, mid_ref, in_ref, sums_ref
):
    f32 = jnp.float32

    @pl.when(pl.program_id(0) == 0)
    def _():
        sums_ref[...] = jnp.zeros_like(sums_ref)

    width = query_ref.shape[1]
    grads = sum(
        lax.dot_general(
            ref[...],
            weight_ref[:, width * i : width * (i + 1)],
            NT,
            preferred_element_type=f32,
        )
        for i, ref in enumerate((query_ref, key_ref, value_ref))
    )
    part, gain, shift = norm_back(grads, token_ref[...].astype(f32), gain_ref[...])
    in_ref[...] = (mid_ref[...] + part).astype(jnp.bfloat16)
    rows = (gain, shift, column_sum(query_ref[...]), column_sum(value_ref[...]))
    for row, value in enumerate(rows):
        sums_ref[row : row + 1] += value


def first_back(grad_query, grad_key, grad_value, qkv_full, tokens_in, gain_row, grad_mid):
    tokens, width = tokens_in.shape
    tile = 256
    block = pl.BlockSpec((tile, width), lambda i: (i, 0))
    whole = lambda *shape: pl.BlockSpec(shape, lambda i: (0, 0))
    return pl.pallas_call(
        first_kernel,
        grid=(tokens // tile,),
        out_shape=[
            jax.ShapeDtypeStruct((tokens, width), jnp.bfloat16),
            jax.ShapeDtypeStruct((8, width), jnp.float32),
        ],
        in_specs=[
            block,
            block,
            block,
            whole(width, 3 * width),
            block,
            whole(1, width),
            block,
        ],
        out_specs=[block, whole(8, width)],
        compiler_params=pltpu.CompilerParams(vmem_limit_bytes=16 * MIB),
        cost_estimate=SMALL,
    )(grad_query, grad_key, grad_value, qkv_full, tokens_in, gain_row, grad_mid)


def pick(values, index, axis=0):
    return lax.dynamic_index_in_dim(values, index, axis, keepdims=False)


def to_micro_x(values, side):
    count, rows, width = values.shape
    halves = values.reshape(2, 2, rows, width)
    return swap(pick(halves, 1 - side), 2), halves


def to_micro_c(got, halves, side, core):
    both = jnp.stack([pick(halves, side), got], 1)
    return pick(both, core), swap(pick(both, 1 - core), CORE)


def to_micro_end(kept, got):
    return jnp.concatenate([kept, got]).reshape(-1, kept.shape[-1])


def from_micro_c(values):
    rows, width = values.shape[0] // 4, values.shape[1]
    parts = values.reshape(2, 2, rows, width)
    return parts[0], swap(parts[1], CORE)


def from_micro_x(kept, got, core):
    both = jnp.where(core == 0, jnp.stack([kept, got]), jnp.stack([got, kept]))
    return both[:, 0], swap(both[:, 1], 2)


def from_micro_end(kept, got, side):
    halves = jnp.where(side == 0, jnp.stack([kept, got]), jnp.stack([got, kept]))
    return halves.reshape(4, *kept.shape[1:])


def on_device_fast(
    inputs,
    segments,
    norm1_gain,
    norm1_bias,
    qkv_weight,
    query_bias,
    value_bias,
    out_weight,
    out_bias,
    norm2_gain,
    norm2_bias,
    up_weight,
    up_bias,
    down_weight,
    down_bias,
    cotangent,
):
    f32, bf16 = jnp.float32, jnp.bfloat16
    local_rows, width = inputs.shape[1], inputs.shape[2]
    rows = width // DEVICES
    wide, inner = qkv_weight.shape[1], up_weight.shape[1]
    group = lax.axis_index("fsdp")
    side, core = group // 2, group % 2
    me = (lax.axis_index("dp") * 4 + group).astype(jnp.int32).reshape(1)

    vectors = (
        norm1_gain,
        norm1_bias,
        query_bias,
        value_bias,
        out_bias,
        norm2_gain,
        norm2_bias,
        down_bias,
    )
    row = lax.broadcasted_iota(jnp.int32, (rows, rows), 0)
    block = jnp.pad(up_bias.reshape(4, rows), ((8, rows - 12), (0, 0)))
    for j, vector in enumerate(vectors):
        block = jnp.where(row == j, vector[None], block)
    block = jnp.pad(block, ((0, 0), (0, 128 - rows)))
    first = Gather(jnp.concatenate([qkv_weight, block], 1))
    second = Gather(jnp.concatenate([out_weight, up_weight], 1))
    third = Gather(down_weight)

    first.line()
    token_got, token_halves = to_micro_x(inputs, side)
    own = pick(segments, group).reshape(4, local_rows)
    labels = jnp.concatenate(
        [pick(own, lax.bitwise_xor(group, source)) for source in (0, 2, 1, 3)]
    )
    first.held, first.got, token_got, token_halves, second.held = fence(
        first.held, first.got, token_got, token_halves, second.held
    )

    first.plane()
    second.far()
    second.near()
    third.far()
    token_kept, token_got = to_micro_c(token_got, token_halves, side, core)
    tokens = to_micro_end(token_kept, token_got)
    resid_in = tokens.astype(f32)
    unit_one, _ = norm_parts(resid_in)
    first.held, first.got, second.held, second.got, third.held, third.got, unit_one = fence(
        first.held, first.got, second.held, second.got, third.held, third.got, unit_one
    )

    first.cores()
    second.plane()
    third.near()
    qkv_full, vectors = restore(first, cuts_of((wide, 128)), me)
    qkv_full = qkv_full.reshape(width, wide)
    vectors = vectors[:, :12, :rows].astype(f32)
    bias_up = vectors[:, 8:].reshape(1, -1)
    (vectors,) = fence(vectors[:, :8].transpose(1, 0, 2).reshape(8, width))
    (
        gain_one,
        shift_one,
        bias_query,
        bias_value,
        bias_out,
        gain_two,
        shift_two,
        bias_down,
    ) = (vectors[i : i + 1] for i in range(8))
    normed_one = (unit_one * gain_one + shift_one).astype(bf16)
    bias_project = jnp.concatenate([bias_query, jnp.zeros_like(bias_query), bias_value], 1)
    project = (
        jnp.dot(normed_one, qkv_full, preferred_element_type=f32) + bias_project
    ).astype(bf16)
    mixed, probs = attend(labels, project)
    second.held, second.got, third.held, third.got, mixed, cotangent = fence(
        second.held, second.got, third.held, third.got, mixed, cotangent
    )

    second.cores()
    cot_got, cot_halves = to_micro_x(cotangent, side)
    second.parts, third.held, third.got, mixed, cot_got, cot_halves = fence(
        second.parts, third.held, third.got, mixed, cot_got, cot_halves
    )

    third.plane()
    cot_kept, cot_got = to_micro_c(cot_got, cot_halves, side, core)
    cot_low = to_micro_end(cot_kept, cot_got)
    out_full, up_full = restore(second, cuts_of((width, inner)), me)
    out_full, up_full = out_full.reshape(width, width), up_full.reshape(width, inner)
    resid_mid = resid_in + jnp.dot(mixed, out_full, preferred_element_type=f32) + bias_out
    unit_two, _ = norm_parts(resid_mid)
    normed_two = (unit_two * gain_two + shift_two).astype(bf16)
    hidden, slope = up_forward(normed_two, up_full, bias_up)
    deep = inner // DEVICES
    down_sum = Scatter(
        parts_call(
            third_parts_kernel, [hidden, cot_low], deep, width, (4 * deep, width), 16, me
        )
    )
    third.held, third.got, down_sum.kept, down_sum.sent, hidden, cot_low = fence(
        third.held, third.got, down_sum.kept, down_sum.sent, hidden, cot_low
    )

    third.cores()
    down_sum.cores()
    third.parts, down_sum.kept, down_sum.got, hidden, cot_low = fence(
        third.parts, down_sum.kept, down_sum.got, hidden, cot_low
    )

    down_sum.plane()
    (down_full,) = restore(third, cuts_of((width,)), me)
    down_full = down_full.reshape(inner, width)
    grad_pre, grad_bias_up = pre_back(cot_low, down_full, slope)
    grad_mid, branch_low, grad_mixed, sums_two = middle_back(
        grad_pre, up_full, resid_mid, gain_two, cot_low, out_full
    )
    up_sum = Scatter(
        parts_call(
            second_parts_kernel,
            [mixed, branch_low, normed_two, grad_pre],
            rows,
            width + inner,
            (width, width),
            20,
            me,
        )
    )
    result = resid_mid + jnp.dot(hidden, down_full, preferred_element_type=f32) + bias_down
    result = result.astype(bf16)
    down_sum.kept, down_sum.got, up_sum.kept, up_sum.sent, grad_mixed, result = fence(
        down_sum.kept, down_sum.got, up_sum.kept, up_sum.sent, grad_mixed, result
    )

    up_sum.cores()
    out_kept, out_got = from_micro_c(result)
    (
        down_sum.kept,
        down_sum.got,
        up_sum.kept,
        up_sum.got,
        grad_mixed,
        out_kept,
        out_got,
    ) = fence(
        down_sum.kept, down_sum.got, up_sum.kept, up_sum.got, grad_mixed, out_kept, out_got
    )

    up_sum.plane()
    down_sum.near()
    down_sum.far()
    grad_query, grad_key, grad_value = attend_back(project, probs, grad_mixed)
    in_grad, sums_one = first_back(
        grad_query, grad_key, grad_value, qkv_full, tokens, gain_one, grad_mid
    )
    sums = jnp.concatenate([sums_one[:4], sums_two[:4]], 0)
    sums = sums.reshape(8, DEVICES, rows).transpose(1, 0, 2)
    sums = jnp.concatenate([sums, grad_bias_up.reshape(DEVICES, 4, rows)], 1)
    sums = jnp.pad(sums, ((0, 0), (0, rows - 12), (0, 128 - rows))).astype(bf16)
    qkv_sum = Scatter(
        parts_call(
            first_parts_kernel,
            [normed_one, grad_query, grad_key, grad_value, sums],
            rows,
            wide + 128,
            (width, width),
            16,
            me,
        )
    )
    (
        down_sum.kept,
        down_sum.got,
        up_sum.kept,
        up_sum.got,
        qkv_sum.kept,
        qkv_sum.sent,
        in_grad,
        out_kept,
        out_got,
    ) = fence(
        down_sum.kept,
        down_sum.got,
        up_sum.kept,
        up_sum.got,
        qkv_sum.kept,
        qkv_sum.sent,
        in_grad,
        out_kept,
        out_got,
    )

    qkv_sum.cores()
    in_kept, in_got = from_micro_c(in_grad)
    (
        down_sum.kept,
        down_sum.got,
        up_sum.kept,
        up_sum.got,
        qkv_sum.kept,
        qkv_sum.got,
        in_kept,
        in_got,
    ) = fence(
        down_sum.kept,
        down_sum.got,
        up_sum.kept,
        up_sum.got,
        qkv_sum.kept,
        qkv_sum.got,
        in_kept,
        in_got,
    )

    qkv_sum.plane()
    up_sum.near()
    up_sum.far()
    out_kept, out_got = from_micro_x(out_kept, out_got, core)
    (
        qkv_sum.kept,
        qkv_sum.got,
        up_sum.kept,
        up_sum.got,
        down_sum.kept,
        down_sum.got,
        in_kept,
        in_got,
        out_kept,
        out_got,
    ) = fence(
        qkv_sum.kept,
        qkv_sum.got,
        up_sum.kept,
        up_sum.got,
        down_sum.kept,
        down_sum.got,
        in_kept,
        in_got,
        out_kept,
        out_got,
    )

    qkv_sum.line()
    in_kept, in_got = from_micro_x(in_kept, in_got, core)
    grad_down = down_sum.total()
    last = up_sum.total()
    grad_out, grad_up = last[:, :width], last[:, width:]
    qkv_sum.kept, qkv_sum.got, in_kept, in_got, out_kept, out_got = fence(
        qkv_sum.kept, qkv_sum.got, in_kept, in_got, out_kept, out_got
    )

    output = from_micro_end(out_kept, out_got, side)
    in_grad = from_micro_end(in_kept, in_got, side).astype(f32)
    last = qkv_sum.total()
    grad_qkv = last[:, :wide]
    sums = last[:12, wide : wide + rows]
    return (
        output,
        in_grad,
        sums[0],
        sums[1],
        grad_qkv,
        sums[2],
        sums[3],
        grad_out,
        sums[4],
        sums[5],
        sums[6],
        grad_up,
        sums[8:12].reshape(-1),
        grad_down,
        sums[7],
    )


def solution(mesh):
    placed = (
        P(None, ("dp", "fsdp"), None),
        P(None, "dp"),
        P(("dp", "fsdp")),
        P(("dp", "fsdp")),
        P(("dp", "fsdp"), None),
        P(("dp", "fsdp")),
        P(("dp", "fsdp")),
        P(("dp", "fsdp"), None),
        P(("dp", "fsdp")),
        P(("dp", "fsdp")),
        P(("dp", "fsdp")),
        P(("dp", "fsdp"), None),
        P(("dp", "fsdp")),
        P(("dp", "fsdp"), None),
        P(("dp", "fsdp")),
        P(None, ("dp", "fsdp"), None),
    )
    fits = mesh.shape["dp"] == 8 and mesh.shape["fsdp"] == 4
    return jax.shard_map(
        on_device_fast if fits else on_device_general,
        mesh=mesh,
        in_specs=placed,
        out_specs=(
            P(None, ("dp", "fsdp"), None),
            P(None, ("dp", "fsdp"), None),
            P(("dp", "fsdp")),
            P(("dp", "fsdp")),
            P(("dp", "fsdp"), None),
            P(("dp", "fsdp")),
            P(("dp", "fsdp")),
            P(("dp", "fsdp"), None),
            P(("dp", "fsdp")),
            P(("dp", "fsdp")),
            P(("dp", "fsdp")),
            P(("dp", "fsdp"), None),
            P(("dp", "fsdp")),
            P(("dp", "fsdp"), None),
            P(("dp", "fsdp")),
        ),
        check_vma=False,
    )
```

```python
import functools
import math

import jax
import jax.numpy as jnp
from jax import lax
from jax.experimental import pallas as pl
from jax.experimental.pallas import tpu as pltpu
from jax.sharding import PartitionSpec as P

HEADS = 12


EPSILON = 1e-06
NEG_LARGE = -1e30
SCALE_SCORE = 0.125


def layer_norm(values, gain_vec, shift_vec):
    centre = values - jnp.mean(values, -1, keepdims=True)
    spread = jnp.mean(centre * centre, -1, keepdims=True)
    return centre * lax.rsqrt(spread + EPSILON) * gain_vec + shift_vec


def gelu_tanh(values):
    return (
        0.5
        * values
        * (1.0 + jnp.tanh(0.7978845608028654 * (values + 0.044715 * values * values * values)))
    )


def add_terms(first_terms, second_terms):
    if first_terms is None:
        return second_terms
    return jax.tree.map(jnp.add, first_terms, second_terms)


def on_device_general(
    inputs,
    segments,
    norm1_gain,
    norm1_bias,
    qkv_weight,
    query_bias,
    value_bias,
    out_weight,
    out_bias,
    norm2_gain,
    norm2_bias,
    up_weight,
    up_bias,
    down_weight,
    down_bias,
    cotangent,
):
    micro_count = inputs.shape[0]
    local_rows = inputs.shape[1]
    model_width = inputs.shape[2]
    group_rows = segments.shape[1]
    key_rows = math.gcd(512, group_rows)
    key_count = group_rows // key_rows
    offset = lax.axis_index("fsdp") * local_rows
    f32 = jnp.float32
    bf16 = jnp.bfloat16
    outputs = []
    in_grads = []
    totals = None
    for micro_index in range(micro_count):
        params_fwd = (
            lax.all_gather(norm1_gain, ("dp", "fsdp"), axis=0, tiled=True),
            lax.all_gather(norm1_bias, ("dp", "fsdp"), axis=0, tiled=True),
            lax.all_gather(qkv_weight, ("dp", "fsdp"), axis=0, tiled=True),
            lax.all_gather(query_bias, ("dp", "fsdp"), axis=0, tiled=True),
            lax.all_gather(value_bias, ("dp", "fsdp"), axis=0, tiled=True),
            lax.all_gather(out_weight, ("dp", "fsdp"), axis=0, tiled=True),
            lax.all_gather(out_bias, ("dp", "fsdp"), axis=0, tiled=True),
            lax.all_gather(norm2_gain, ("dp", "fsdp"), axis=0, tiled=True),
            lax.all_gather(norm2_bias, ("dp", "fsdp"), axis=0, tiled=True),
            lax.all_gather(up_weight, ("dp", "fsdp"), axis=0, tiled=True),
            lax.all_gather(up_bias, ("dp", "fsdp"), axis=0, tiled=True),
            lax.all_gather(down_weight, ("dp", "fsdp"), axis=0, tiled=True),
            lax.all_gather(down_bias, ("dp", "fsdp"), axis=0, tiled=True),
        )
        (
            gain_one,
            shift_one,
            qkv_full,
            bias_query,
            bias_value,
            out_full,
            bias_out,
            gain_two,
            shift_two,
            up_full,
            bias_up,
            down_full,
            bias_down,
        ) = params_fwd
        resid_in = inputs[micro_index].astype(f32)
        normed_one = layer_norm(resid_in, gain_one.astype(f32), shift_one.astype(f32)).astype(bf16)
        project = jnp.dot(normed_one, qkv_full, preferred_element_type=f32)
        queries = (project[:, :model_width] + bias_query.astype(f32)).astype(bf16)
        keys_local = project[:, model_width : 2 * model_width].astype(bf16)
        values_local = (project[:, 2 * model_width :] + bias_value.astype(f32)).astype(bf16)
        keys_all, values_all = (
            lax.all_gather(keys_local, "fsdp", axis=0, tiled=True),
            lax.all_gather(values_local, "fsdp", axis=0, tiled=True),
        )
        labels_all = segments[micro_index]
        labels_query = lax.dynamic_slice_in_dim(labels_all, offset, local_rows)
        query_heads = queries.reshape(local_rows, HEADS, -1)
        key_blocks = keys_all.reshape(key_count, key_rows, HEADS, -1)
        value_blocks = values_all.reshape(key_count, key_rows, HEADS, -1)
        label_blocks = labels_all.reshape(key_count, key_rows)

        def block_scores(key_block, label_block):
            scores = (
                jnp.einsum("qhd,khd->hqk", query_heads, key_block, preferred_element_type=f32)
                * SCALE_SCORE
            )
            allowed = (labels_query[:, None] == label_block[None, :])[None]
            return (jnp.where(allowed, scores, NEG_LARGE), allowed)

        def stat_step(state_in, pieces):
            running_max, running_sum = state_in
            scores, allowed = block_scores(pieces[0], pieces[1])
            newmax = jnp.maximum(running_max, jnp.max(scores, -1))
            exponent = jnp.where(allowed, jnp.exp(scores - newmax[..., None]), 0.0)
            running_sum = running_sum * jnp.exp(running_max - newmax) + jnp.sum(exponent, -1)
            return ((newmax, running_sum), None)

        start_state = (
            jnp.full((HEADS, local_rows), NEG_LARGE, f32),
            jnp.zeros((HEADS, local_rows), f32),
        )
        (final_max, final_sum), _ = lax.scan(stat_step, start_state, (key_blocks, label_blocks))
        log_total = final_max + jnp.log(final_sum)

        def block_prob(key_block, label_block):
            scores, allowed = block_scores(key_block, label_block)
            attend_prob = jnp.where(allowed, jnp.exp(scores - log_total[..., None]), 0.0)
            return (attend_prob, attend_prob.astype(bf16))

        def mix_step(state_in, pieces):
            mixed_acc, extra_acc = state_in
            attend_prob, prob_low = block_prob(pieces[0], pieces[2])
            remainder = (attend_prob - prob_low.astype(f32)).astype(bf16)
            mixed_acc = mixed_acc + jnp.einsum(
                "hqk,khd->qhd", prob_low, pieces[1], preferred_element_type=f32
            )
            extra_acc = extra_acc + jnp.einsum(
                "hqk,khd->qhd", remainder, pieces[1], preferred_element_type=f32
            )
            return ((mixed_acc, extra_acc), None)

        zero_heads = jnp.zeros(query_heads.shape, f32)
        (mixed_heads, extra_heads), _ = lax.scan(
            mix_step, (zero_heads, zero_heads), (key_blocks, value_blocks, label_blocks)
        )
        mixed_low = mixed_heads.reshape(local_rows, model_width).astype(bf16)
        full_mix = mixed_heads + extra_heads
        resid_mid = (
            resid_in
            + jnp.dot(mixed_low, out_full, preferred_element_type=f32)
            + bias_out.astype(f32)
        )
        normed_two = layer_norm(resid_mid, gain_two.astype(f32), shift_two.astype(f32)).astype(bf16)
        pre_act = jnp.dot(normed_two, up_full, preferred_element_type=f32) + bias_up.astype(f32)
        hidden_low = gelu_tanh(pre_act).astype(bf16)
        result = (
            resid_mid
            + jnp.dot(hidden_low, down_full, preferred_element_type=f32)
            + bias_down.astype(f32)
        )
        outputs.append(result.astype(bf16))
        params_bwd = (
            lax.all_gather(norm1_gain, ("dp", "fsdp"), axis=0, tiled=True),
            lax.all_gather(norm1_bias, ("dp", "fsdp"), axis=0, tiled=True),
            lax.all_gather(qkv_weight, ("dp", "fsdp"), axis=0, tiled=True),
            lax.all_gather(query_bias, ("dp", "fsdp"), axis=0, tiled=True),
            lax.all_gather(value_bias, ("dp", "fsdp"), axis=0, tiled=True),
            lax.all_gather(out_weight, ("dp", "fsdp"), axis=0, tiled=True),
            lax.all_gather(out_bias, ("dp", "fsdp"), axis=0, tiled=True),
            lax.all_gather(norm2_gain, ("dp", "fsdp"), axis=0, tiled=True),
            lax.all_gather(norm2_bias, ("dp", "fsdp"), axis=0, tiled=True),
            lax.all_gather(up_weight, ("dp", "fsdp"), axis=0, tiled=True),
            lax.all_gather(up_bias, ("dp", "fsdp"), axis=0, tiled=True),
            lax.all_gather(down_weight, ("dp", "fsdp"), axis=0, tiled=True),
            lax.all_gather(down_bias, ("dp", "fsdp"), axis=0, tiled=True),
        )
        (
            gain_one_b,
            shift_one_b,
            qkv_back,
            bias_query_b,
            bias_value_b,
            out_back,
            bias_out_b,
            gain_two_b,
            shift_two_b,
            up_back,
            bias_up_b,
            down_back,
            bias_down_b,
        ) = params_bwd
        cot_low = cotangent[micro_index]
        cot_full = cot_low.astype(f32)
        grad_down = jnp.einsum("tf,td->fd", hidden_low, cot_low, preferred_element_type=f32)
        grad_bias_down = jnp.sum(cot_full, 0)
        grad_hidden = jnp.einsum("td,fd->tf", cot_low, down_back, preferred_element_type=f32)
        _, gelu_pull = jax.vjp(gelu_tanh, pre_act)
        grad_pre = gelu_pull(grad_hidden)[0].astype(bf16)
        grad_up = jnp.einsum("td,tf->df", normed_two, grad_pre, preferred_element_type=f32)
        grad_bias_up = jnp.sum(grad_pre.astype(f32), 0)
        grad_normed_two = jnp.einsum("tf,df->td", grad_pre, up_back, preferred_element_type=f32)
        _, norm_two_pull = jax.vjp(
            layer_norm, resid_mid, gain_two_b.astype(f32), shift_two_b.astype(f32)
        )
        grad_mid_part, grad_gain_two, grad_shift_two = norm_two_pull(grad_normed_two)
        grad_mid = cot_full + grad_mid_part
        branch_low = grad_mid.astype(bf16)
        grad_out = jnp.einsum("td,te->de", mixed_low, branch_low, preferred_element_type=f32)
        grad_bias_out = jnp.sum(branch_low.astype(f32), 0)
        grad_mixed = jnp.einsum(
            "te,de->td", branch_low, out_back, preferred_element_type=f32
        ).astype(bf16)
        grad_heads = grad_mixed.reshape(local_rows, HEADS, -1)
        delta = jnp.einsum("qhd,qhd->hq", grad_heads.astype(f32), full_mix)

        def grad_step(query_acc, pieces):
            key_block, value_block, label_block = pieces
            attend_prob, prob_low = block_prob(key_block, label_block)
            grad_prob = jnp.einsum(
                "qhd,khd->hqk", grad_heads, value_block, preferred_element_type=f32
            )
            grad_scores = (attend_prob * (grad_prob - delta[..., None]) * SCALE_SCORE).astype(bf16)
            query_acc = query_acc + jnp.einsum(
                "hqk,khd->qhd", grad_scores, key_block, preferred_element_type=f32
            )
            key_part = jnp.einsum(
                "hqk,qhd->khd", grad_scores, query_heads, preferred_element_type=f32
            )
            value_part = jnp.einsum(
                "hqk,qhd->khd", prob_low, grad_heads, preferred_element_type=f32
            )
            return (query_acc, (key_part, value_part))

        query_grad, (key_parts, value_parts) = lax.scan(
            grad_step, zero_heads, (key_blocks, value_blocks, label_blocks)
        )
        key_parts = key_parts.reshape(group_rows, model_width)
        value_parts = value_parts.reshape(group_rows, model_width)
        key_grad, value_grad = (
            lax.psum_scatter(
                key_parts.astype(jnp.bfloat16), "fsdp", scatter_dimension=0, tiled=True
            ).astype(jnp.float32),
            lax.psum_scatter(
                value_parts.astype(jnp.bfloat16), "fsdp", scatter_dimension=0, tiled=True
            ).astype(jnp.float32),
        )
        query_low = query_grad.reshape(local_rows, model_width).astype(bf16)
        key_low = key_grad.astype(bf16)
        value_low = value_grad.astype(bf16)
        grad_project = jnp.concatenate([query_low, key_low, value_low], 1)
        grad_qkv = jnp.einsum("td,te->de", normed_one, grad_project, preferred_element_type=f32)
        grad_bias_query = jnp.sum(query_low.astype(f32), 0)
        grad_bias_value = jnp.sum(value_low.astype(f32), 0)
        grad_normed_one = jnp.einsum(
            "te,de->td", grad_project, qkv_back, preferred_element_type=f32
        )
        _, norm_one_pull = jax.vjp(
            layer_norm, resid_in, gain_one_b.astype(f32), shift_one_b.astype(f32)
        )
        grad_in_part, grad_gain_one, grad_shift_one = norm_one_pull(grad_normed_one)
        in_grads.append(grad_mid + grad_in_part)
        local_terms = (
            grad_gain_one,
            grad_shift_one,
            grad_qkv,
            grad_bias_query,
            grad_bias_value,
            grad_out,
            grad_bias_out,
            grad_gain_two,
            grad_shift_two,
            grad_up,
            grad_bias_up,
            grad_down,
            grad_bias_down,
        )
        shard_terms = (
            lax.psum_scatter(local_terms[0], ("dp", "fsdp"), scatter_dimension=0, tiled=True),
            lax.psum_scatter(local_terms[1], ("dp", "fsdp"), scatter_dimension=0, tiled=True),
            lax.psum_scatter(local_terms[2], ("dp", "fsdp"), scatter_dimension=0, tiled=True),
            lax.psum_scatter(local_terms[3], ("dp", "fsdp"), scatter_dimension=0, tiled=True),
            lax.psum_scatter(local_terms[4], ("dp", "fsdp"), scatter_dimension=0, tiled=True),
            lax.psum_scatter(local_terms[5], ("dp", "fsdp"), scatter_dimension=0, tiled=True),
            lax.psum_scatter(local_terms[6], ("dp", "fsdp"), scatter_dimension=0, tiled=True),
            lax.psum_scatter(local_terms[7], ("dp", "fsdp"), scatter_dimension=0, tiled=True),
            lax.psum_scatter(local_terms[8], ("dp", "fsdp"), scatter_dimension=0, tiled=True),
            lax.psum_scatter(local_terms[9], ("dp", "fsdp"), scatter_dimension=0, tiled=True),
            lax.psum_scatter(local_terms[10], ("dp", "fsdp"), scatter_dimension=0, tiled=True),
            lax.psum_scatter(local_terms[11], ("dp", "fsdp"), scatter_dimension=0, tiled=True),
            lax.psum_scatter(local_terms[12], ("dp", "fsdp"), scatter_dimension=0, tiled=True),
        )
        totals = add_terms(totals, shard_terms)
    return (
        jnp.stack(outputs),
        jnp.stack(in_grads),
        totals[0],
        totals[1],
        totals[2],
        totals[3],
        totals[4],
        totals[5],
        totals[6],
        totals[7],
        totals[8],
        totals[9],
        totals[10],
        totals[11],
        totals[12],
    )


AXES = ("dp", "fsdp")
CORE, X, Y, Z0, Z1 = 1, 2, 4, 8, 16
LINE = (0, Z1, Z0, Z1 ^ Z0)
PLANE = (0, X, Y, X ^ Y)
DEVICES = 32
MIB = 1024 * 1024
SMALL = pl.CostEstimate(flops=1024, transcendentals=0, bytes_accessed=1024)


def swap(values, mask):
    pairs = [(i, i ^ mask) for i in range(DEVICES)]
    return lax.ppermute(values, AXES, pairs)


SLOTS = [core ^ plane ^ line for core in (0, CORE) for plane in PLANE for line in LINE]


def fence(*values):
    return lax.optimization_barrier(values)


def join(*parts):
    return lax.optimization_barrier(jnp.concatenate(parts, 0))


def halves_of(width):
    half = width // 256 * 128
    return ((0, half), (half, width))


class Gather:
    def __init__(self, shard):
        self.held = shard[None]
        self.across = []

    def line(self):
        self.got = [swap(self.held, mask) for mask in LINE[1:]]

    def far(self):
        self.got = [swap(self.held, Z1)]

    def near(self):
        self.held = join(self.held, *self.got)
        self.got = [swap(self.held, Z0)]

    def plane(self):
        self.held = join(self.held, *self.got)
        self.got = [swap(self.held, mask) for mask in PLANE[1:]]

    def plane_one(self):
        self.held = join(self.held, *self.got)
        self.quads = [self.held[..., low:high] for low, high in halves_of(self.held.shape[2])]
        self.got = [swap(quad, bit) for quad, bit in zip(self.quads, (X, Y))]

    def plane_two(self):
        own = []
        for quad, got, bit in zip(self.quads, self.got, (Y, X)):
            eight = join(quad, got)
            own += [eight, swap(eight, bit)]
        self.held, self.got = own[0], own[1:]

    def cores(self):
        own = [self.held, *self.got]
        self.parts = own + [swap(piece, CORE) for piece in own]

    def places(self):
        width = self.held.shape[2]
        if self.held.shape[0] == 4:
            masks = [core ^ plane ^ line for core in (0, CORE) for plane in PLANE for line in LINE]
            return [(i // 4, i % 4, mask, 0, width) for i, mask in enumerate(masks)]
        spans = ((0, width), (width, width + self.got[1].shape[2]))
        return [
            (4 * core + 2 * half + second, 4 * first + i, mask, low, high)
            for core in (0, CORE)
            for half, ((low, high), bits) in enumerate(zip(spans, ((X, Y), (Y, X))))
            for second in (0, 1)
            for first in (0, 1)
            for i, line in enumerate(LINE)
            for mask in (core ^ line ^ bits[0] * first ^ bits[1] * second,)
        ]


def sum_low(*terms):
    total = sum(term.astype(jnp.float32) for term in terms)
    return total.astype(jnp.bfloat16)


class Scatter:
    places = [
        (slot // 16, slot % 16, core ^ plane ^ line)
        for slot, (core, plane, line) in enumerate(
            (core, plane, line) for core in (0, CORE) for plane in PLANE for line in LINE
        )
    ]

    def __init__(self, halves):
        self.kept, self.sent = halves

    def cores(self):
        self.got = swap(self.sent, CORE)

    def plane(self):
        self.kept, *quads = [
            sum_low(self.kept[4 * i : 4 * i + 4], self.got[4 * i : 4 * i + 4]) for i in range(4)
        ]
        self.got = [swap(quad, mask) for quad, mask in zip(quads, PLANE[1:])]

    def line(self):
        terms = [self.kept, *self.got]
        ones = [sum_low(*(term[i : i + 1] for term in terms)) for i in range(1, 4)]
        self.kept = sum(term[0].astype(jnp.float32) for term in terms)
        self.got = [swap(one, mask) for one, mask in zip(ones, LINE[1:])]

    def plane_one(self):
        kept, got = [], []
        spans = halves_of(self.kept.shape[2])
        for (low, high), bit, order in zip(spans, (Y, X), ((0, 1, 2, 3), (0, 2, 1, 3))):
            quads = [
                sum_low(
                    self.kept[4 * i : 4 * i + 4, :, low:high],
                    self.got[4 * i : 4 * i + 4, :, low:high],
                )
                for i in order
            ]
            kept.append(quads[:2])
            got.append(swap(jnp.concatenate(quads[2:], 0), bit))
        self.kept, self.got = kept, got

    def plane_two(self):
        sent = [
            swap(sum_low(kept[1], got[4:]), bit)
            for kept, got, bit in zip(self.kept, self.got, (X, Y))
        ]
        kept = [sum_low(kept[0], got[:4]) for kept, got in zip(self.kept, self.got)]
        self.kept, self.got = jnp.concatenate(kept, -1), sent

    def plane_end(self):
        self.got = [jnp.concatenate(self.got, -1)]

    def near(self):
        terms = [self.kept, *self.got]
        self.kept = sum_low(*(term[:2] for term in terms))
        self.got = [swap(sum_low(*(term[2:] for term in terms)), Z0)]

    def far(self):
        got = self.got[0]
        self.got = [swap(sum_low(self.kept[1:], got[1:]), Z1)]
        self.kept = self.kept[0].astype(jnp.float32) + got[0].astype(jnp.float32)

    def total(self):
        return self.kept + sum(got[0].astype(jnp.float32) for got in self.got)


def cuts_of(parts):
    ends = [sum(parts[: i + 1]) for i in range(len(parts))]
    return tuple((end - part, end) for end, part in zip(ends, parts))


def shuffle_kernel(moves, count, me_ref, *refs):
    me = me_ref[0]

    def part(slot):
        return pl.ds(lax.bitwise_xor(me, slot[0]) if isinstance(slot, tuple) else slot, 1)

    for source, source_slot, source_low, target, target_slot, target_low, width in moves:
        refs[count + target][part(target_slot), :, target_low : target_low + width] = refs[source][
            part(source_slot), :, source_low : source_low + width
        ]


def whole_block(shape):
    return pl.BlockSpec(shape, lambda i: (0,) * len(shape), pipeline_mode=pl.Buffered(1))


def shuffle(arrays, shapes, moves, me, pinned):
    dtype = arrays[0].dtype
    size = sum(math.prod(shape) for shape in shapes)
    make = pltpu.HBM if pinned else jax.ShapeDtypeStruct
    return pl.pallas_call(
        functools.partial(shuffle_kernel, moves, len(arrays)),
        grid=(1,),
        out_shape=[make(shape, dtype) for shape in shapes],
        in_specs=[pl.BlockSpec(memory_space=pltpu.SMEM)]
        + [whole_block(array.shape) for array in arrays],
        out_specs=[whole_block(shape) for shape in shapes],
        compiler_params=pltpu.CompilerParams(vmem_limit_bytes=16 * MIB),
        cost_estimate=SMALL,
    )(me, *arrays)


def restore(gather, cuts, me, pinned=True):
    moves = []
    for part, slot, mask, low, high in gather.places():
        for target, (begin, end) in enumerate(cuts):
            left, right = max(low, begin), min(high, end)
            if left < right:
                moves.append(
                    (part, slot, left - low, target, (mask,), left - begin, right - left)
                )
    rows = gather.parts[0].shape[1]
    shapes = [(DEVICES, rows, end - begin) for begin, end in cuts]
    return shuffle(gather.parts, shapes, moves, me, pinned)


TN = (((0,), (0,)), ((), ()))


def parts_call(kernel, inputs, rows, width, scratch, limit, me):
    half = (DEVICES // 2, rows, width)
    return pl.pallas_call(
        kernel,
        grid=(1,),
        out_shape=[jax.ShapeDtypeStruct(half, jnp.bfloat16)] * 2,
        in_specs=[pl.BlockSpec(memory_space=pltpu.SMEM)]
        + [whole_block(value.shape) for value in inputs],
        out_specs=[whole_block(half)] * 2,
        scratch_shapes=[pltpu.VMEM(scratch, jnp.float32)],
        compiler_params=pltpu.CompilerParams(vmem_limit_bytes=limit * MIB),
        cost_estimate=SMALL,
    )(me, *inputs)


def store_rows(me, sum_ref, outs, low, high):
    rows = sum_ref.shape[0] // DEVICES
    for half, slot, mask in Scatter.places:
        first = pl.multiple_of(lax.bitwise_xor(me, mask) * rows, rows)
        outs[half][slot, :, low:high] = sum_ref[pl.ds(first, rows), : high - low].astype(
            jnp.bfloat16
        )


def multiply_rows(me, left_ref, right_refs, sum_ref, outs, low):
    width = sum_ref.shape[1]
    for ref in right_refs:
        for begin in range(0, ref.shape[1], width):
            sum_ref[...] = lax.dot_general(
                left_ref[...],
                ref[:, begin : begin + width],
                TN,
                preferred_element_type=jnp.float32,
            )
            store_rows(me, sum_ref, outs, low + begin, low + begin + width)
        low += ref.shape[1]
    return low


def second_parts_kernel(
    me_ref, mixed_ref, branch_ref, normed_ref, pre_ref, kept_ref, sent_ref, sum_ref
):
    me, outs = me_ref[0], (kept_ref, sent_ref)
    low = multiply_rows(me, mixed_ref, [branch_ref], sum_ref, outs, 0)
    multiply_rows(me, normed_ref, [pre_ref], sum_ref, outs, low)


def first_parts_kernel(
    me_ref,
    normed_ref,
    query_ref,
    key_ref,
    value_ref,
    one_ref,
    two_ref,
    bias_ref,
    kept_ref,
    sent_ref,
    sum_ref,
):
    me, outs = me_ref[0], (kept_ref, sent_ref)
    low = multiply_rows(me, normed_ref, [query_ref, key_ref, value_ref], sum_ref, outs, 0)
    rows = kept_ref.shape[1]
    vectors = jnp.concatenate([one_ref[:4], two_ref[:4]], 0)
    width, bias = vectors.shape[1], jnp.broadcast_to(bias_ref[...], (8, bias_ref.shape[1]))
    deep = bias.shape[1] // DEVICES
    spare = jnp.zeros((rows - 16, 128), jnp.float32)
    for half, slot, mask in Scatter.places:
        owner = lax.bitwise_xor(me, mask)
        here = pltpu.roll(vectors, lax.rem(width - rows * owner, width), 1)[:, :128]
        bias_here = pltpu.roll(bias, lax.rem(DEVICES * deep - deep * owner, DEVICES * deep), 1)
        outs[half][slot, :, low:] = jnp.concatenate(
            [here, bias_here[:, :128], spare], 0
        ).astype(jnp.bfloat16)


def third_parts_kernel(me_ref, hidden_ref, cot_ref, kept_ref, sent_ref, sum_ref):
    me, outs = me_ref[0], (kept_ref, sent_ref)
    rows = kept_ref.shape[1]
    for block in range(DEVICES // 4):
        first = pl.multiple_of(lax.bitwise_xor(me // 4, block) * (4 * rows), 4 * rows)
        sum_ref[...] = lax.dot_general(
            hidden_ref[:, pl.ds(first, 4 * rows)],
            cot_ref[...],
            TN,
            preferred_element_type=jnp.float32,
        )
        for half, slot, mask in Scatter.places:
            if mask // 4 == block:
                first = pl.multiple_of(lax.bitwise_xor(me % 4, mask % 4) * rows, rows)
                outs[half][slot] = sum_ref[pl.ds(first, rows)].astype(jnp.bfloat16)


NT = (((1,), (1,)), ((), ()))


def make_mask(labels_row_ref, labels_col_ref, mask_ref):
    @pl.when(pl.program_id(0) == 0)
    def _():
        allowed = labels_col_ref[...] == labels_row_ref[...]
        mask_ref[...] = jnp.where(allowed, 0.0, NEG_LARGE)


def head_probs(keys, queries, head, mask_ref):
    f32 = jnp.float32
    lane = lax.broadcasted_iota(jnp.int32, queries.shape, 1)
    own = (lane // 64) == head
    chosen = jnp.where(own, queries.astype(f32) * SCALE_SCORE, 0.0).astype(jnp.bfloat16)
    scores = lax.dot_general(keys, chosen, NT, preferred_element_type=f32) + mask_ref[...]
    exponent = jnp.exp(scores - jnp.max(scores, 0, keepdims=True))
    return exponent * (1.0 / jnp.sum(exponent, 0, keepdims=True))


def attend_kernel(row_ref, col_ref, query_ref, key_ref, value_ref, out_ref, prob_ref, mask_ref):
    make_mask(row_ref, col_ref, mask_ref)
    keys, queries = key_ref[...], query_ref[...]
    values_across = value_ref[...].astype(jnp.float32).T.astype(jnp.bfloat16)
    mixed = []
    for head in range(2):
        prob_ref[head] = head_probs(keys, queries, head, mask_ref).astype(jnp.bfloat16)
        mixed.append(
            jnp.dot(
                values_across[64 * head : 64 * head + 64],
                prob_ref[head],
                preferred_element_type=jnp.float32,
            )
        )
    out_ref[...] = jnp.concatenate(mixed, 0).T.astype(jnp.bfloat16)


def attend_back_kernel(
    query_ref, key_ref, value_ref, prob_ref, grad_ref, dquery_ref, dkey_ref, dvalue_ref
):
    f32, bf16 = jnp.float32, jnp.bfloat16
    keys, queries, values, grads = key_ref[...], query_ref[...], value_ref[...], grad_ref[...]
    keys_across = keys.astype(f32).T.astype(bf16)
    lane = lax.broadcasted_iota(jnp.int32, keys.shape, 1)
    dquery, dkey, dvalue = [], [], []
    for head in range(2):
        chosen = jnp.where((lane // 64) == head, grads.astype(f32), 0.0).astype(bf16)
        grad_prob = lax.dot_general(values, chosen, NT, preferred_element_type=f32)
        prob = prob_ref[head].astype(f32)
        delta = jnp.sum(prob * grad_prob, 0, keepdims=True)
        grad_scores = (prob * (grad_prob - delta)).astype(bf16)
        dvalue.append(jnp.dot(prob_ref[head], grads, preferred_element_type=f32))
        dkey.append(jnp.dot(grad_scores, queries, preferred_element_type=f32))
        dquery.append(
            jnp.dot(
                keys_across[64 * head : 64 * head + 64], grad_scores, preferred_element_type=f32
            )
        )
    low_half = lane < 64
    dquery_ref[...] = (jnp.concatenate(dquery, 0).T * SCALE_SCORE).astype(bf16)
    dkey_ref[...] = (jnp.where(low_half, dkey[0], dkey[1]) * SCALE_SCORE).astype(bf16)
    dvalue_ref[...] = jnp.where(low_half, dvalue[0], dvalue[1]).astype(bf16)


def pair_specs(tokens, pairs):
    parts = [
        pl.BlockSpec((tokens, 128), lambda i, part=part: (0, i + part * pairs))
        for part in range(3)
    ]
    return parts, pl.BlockSpec((2, tokens, tokens), lambda i: (i, 0, 0))


def in_hbm(array):
    return pltpu.with_memory_space_constraint(array, pltpu.HBM)


def attend(labels, project):
    tokens, pairs = project.shape[0], HEADS // 2
    parts, probs = pair_specs(tokens, pairs)
    return pl.pallas_call(
        attend_kernel,
        grid=(pairs,),
        out_shape=[
            jax.ShapeDtypeStruct((tokens, 128 * pairs), jnp.bfloat16),
            pltpu.HBM((HEADS, tokens, tokens), jnp.bfloat16),
        ],
        in_specs=[
            pl.BlockSpec((1, tokens), lambda i: (0, 0)),
            pl.BlockSpec((tokens, 1), lambda i: (0, 0)),
            *parts,
        ],
        out_specs=[pl.BlockSpec((tokens, 128), lambda i: (0, i)), probs],
        scratch_shapes=[pltpu.VMEM((tokens, tokens), jnp.float32)],
        compiler_params=pltpu.CompilerParams(vmem_limit_bytes=12 * MIB),
        cost_estimate=SMALL,
    )(labels.reshape(1, tokens), labels.reshape(tokens, 1), project, project, project)


def attend_back(project, probs, grads):
    tokens, pairs = project.shape[0], HEADS // 2
    block = pl.BlockSpec((tokens, 128), lambda i: (0, i))
    shape = jax.ShapeDtypeStruct((tokens, 128 * pairs), jnp.bfloat16)
    parts, prob_spec = pair_specs(tokens, pairs)
    return pl.pallas_call(
        attend_back_kernel,
        grid=(pairs,),
        out_shape=[shape] * 3,
        in_specs=[*parts, prob_spec, block],
        out_specs=[block] * 3,
        compiler_params=pltpu.CompilerParams(vmem_limit_bytes=14 * MIB),
        cost_estimate=SMALL,
    )(project, project, project, in_hbm(probs), grads)


def norm_parts(values):
    centre = values - jnp.mean(values, -1, keepdims=True)
    scale = lax.rsqrt(jnp.mean(centre * centre, -1, keepdims=True) + EPSILON)
    return centre * scale, scale


def norm_back(grads, values, gain_row):
    unit, scale = norm_parts(values)
    inner = grads * gain_row
    part = inner - jnp.mean(inner, -1, keepdims=True)
    part = part - unit * jnp.mean(inner * unit, -1, keepdims=True)
    gain, shift = jnp.sum(grads * unit, 0, keepdims=True), jnp.sum(grads, 0, keepdims=True)
    return part * scale, gain, shift


def column_sum(values):
    return jnp.sum(values.astype(jnp.float32), 0, keepdims=True)


def up_kernel(normed_ref, weight_ref, bias_ref, hidden_ref, slope_ref):
    bf16 = jnp.bfloat16
    first, third = 0.7978845608028654, 0.7978845608028654 * 0.044715
    for row in range(0, normed_ref.shape[0], 128):
        rows = slice(row, row + 128)
        pre = jnp.dot(normed_ref[rows], weight_ref[...], preferred_element_type=jnp.float32)
        pre = pre + bias_ref[...]
        square = pre * pre
        half = 0.5 + 0.5 * jnp.tanh(pre * (first + third * square))
        hidden_ref[rows] = (pre * half).astype(bf16)
        inner = pre * (2 * first + 6 * third * square)
        slope_ref[rows] = (half + half * inner * (1.0 - half)).astype(bf16)


def up_forward(normed, up_full, bias_row):
    tokens, width = normed.shape
    inner, tile = up_full.shape[1], 768
    block = pl.BlockSpec((tokens, tile), lambda i: (0, i))
    shape = jax.ShapeDtypeStruct((tokens, inner), jnp.bfloat16)
    return pl.pallas_call(
        up_kernel,
        grid=(inner // tile,),
        out_shape=[shape, shape],
        in_specs=[
            pl.BlockSpec((tokens, width), lambda i: (0, 0)),
            pl.BlockSpec((width, tile), lambda i: (0, i)),
            pl.BlockSpec((1, tile), lambda i: (0, i)),
        ],
        out_specs=[block, block],
        compiler_params=pltpu.CompilerParams(vmem_limit_bytes=18 * MIB),
        cost_estimate=SMALL,
    )(normed, in_hbm(up_full), bias_row)


def pre_kernel(cot_ref, weight_ref, slope_ref, pre_ref, sum_ref):
    f32 = jnp.float32
    grads = lax.dot_general(cot_ref[...], weight_ref[...], NT, preferred_element_type=f32)
    low = (grads * slope_ref[...].astype(f32)).astype(jnp.bfloat16)
    pre_ref[...] = low
    sum_ref[...] = column_sum(low)


def pre_back(cot_low, down_full, slope):
    tokens, width = cot_low.shape
    inner, tile = down_full.shape[0], 512
    block = pl.BlockSpec((tokens, tile), lambda i: (0, i))
    return pl.pallas_call(
        pre_kernel,
        grid=(inner // tile,),
        out_shape=[
            jax.ShapeDtypeStruct((tokens, inner), jnp.bfloat16),
            jax.ShapeDtypeStruct((1, inner), jnp.float32),
        ],
        in_specs=[
            pl.BlockSpec((tokens, width), lambda i: (0, 0)),
            pl.BlockSpec((tile, width), lambda i: (i, 0)),
            block,
        ],
        out_specs=[block, pl.BlockSpec((1, tile), lambda i: (0, i))],
        compiler_params=pltpu.CompilerParams(vmem_limit_bytes=12 * MIB),
        cost_estimate=SMALL,
    )(cot_low, down_full, slope)


def middle_kernel(pre_ref, up_ref, resid_ref, gain_ref, cot_ref, out_ref, mid_ref, low_ref, mixed_ref, sums_ref):
    f32, bf16 = jnp.float32, jnp.bfloat16

    @pl.when(pl.program_id(0) == 0)
    def _():
        sums_ref[...] = jnp.zeros_like(sums_ref)

    grads = lax.dot_general(pre_ref[...], up_ref[...], NT, preferred_element_type=f32)
    part, gain, shift = norm_back(grads, resid_ref[...], gain_ref[...])
    cot = cot_ref[...].astype(f32)
    mid = cot + part
    low = mid.astype(bf16)
    mid_ref[...] = mid
    low_ref[...] = low
    mixed_ref[...] = lax.dot_general(
        low, out_ref[...], NT, preferred_element_type=f32
    ).astype(bf16)
    for row, value in enumerate((column_sum(low), gain, shift, column_sum(cot))):
        sums_ref[row : row + 1] += value


def middle_back(grad_pre, up_full, resid_mid, gain_row, cot_low, out_full):
    tokens, inner = grad_pre.shape
    width, tile = resid_mid.shape[1], 256
    block = pl.BlockSpec((tile, width), lambda i: (i, 0))
    whole = lambda *shape: pl.BlockSpec(shape, lambda i: (0, 0))
    return pl.pallas_call(
        middle_kernel,
        grid=(tokens // tile,),
        out_shape=[
            jax.ShapeDtypeStruct((tokens, width), jnp.float32),
            jax.ShapeDtypeStruct((tokens, width), jnp.bfloat16),
            jax.ShapeDtypeStruct((tokens, width), jnp.bfloat16),
            jax.ShapeDtypeStruct((8, width), jnp.float32),
        ],
        in_specs=[
            pl.BlockSpec((tile, inner), lambda i: (i, 0)),
            whole(width, inner),
            block,
            whole(1, width),
            block,
            whole(width, width),
        ],
        out_specs=[block, block, block, whole(8, width)],
        compiler_params=pltpu.CompilerParams(vmem_limit_bytes=20 * MIB),
        cost_estimate=SMALL,
    )(grad_pre, up_full, resid_mid, gain_row, cot_low, out_full)


def first_kernel(
    query_ref, key_ref, value_ref, weight_ref, token_ref, gain_ref, mid_ref, in_ref, sums_ref
):
    f32 = jnp.float32

    @pl.when(pl.program_id(0) == 0)
    def _():
        sums_ref[...] = jnp.zeros_like(sums_ref)

    width = query_ref.shape[1]
    grads = sum(
        lax.dot_general(
            ref[...],
            weight_ref[:, width * i : width * (i + 1)],
            NT,
            preferred_element_type=f32,
        )
        for i, ref in enumerate((query_ref, key_ref, value_ref))
    )
    part, gain, shift = norm_back(grads, token_ref[...].astype(f32), gain_ref[...])
    in_ref[...] = (mid_ref[...] + part).astype(jnp.bfloat16)
    rows = (gain, shift, column_sum(query_ref[...]), column_sum(value_ref[...]))
    for row, value in enumerate(rows):
        sums_ref[row : row + 1] += value


def first_back(grad_query, grad_key, grad_value, qkv_full, tokens_in, gain_row, grad_mid):
    tokens, width = tokens_in.shape
    tile = 256
    block = pl.BlockSpec((tile, width), lambda i: (i, 0))
    whole = lambda *shape: pl.BlockSpec(shape, lambda i: (0, 0))
    return pl.pallas_call(
        first_kernel,
        grid=(tokens // tile,),
        out_shape=[
            jax.ShapeDtypeStruct((tokens, width), jnp.bfloat16),
            jax.ShapeDtypeStruct((8, width), jnp.float32),
        ],
        in_specs=[
            block,
            block,
            block,
            whole(width, 3 * width),
            block,
            whole(1, width),
            block,
        ],
        out_specs=[block, whole(8, width)],
        compiler_params=pltpu.CompilerParams(vmem_limit_bytes=16 * MIB),
        cost_estimate=SMALL,
    )(grad_query, grad_key, grad_value, qkv_full, tokens_in, gain_row, grad_mid)


def pick(values, index, axis=0):
    return lax.dynamic_index_in_dim(values, index, axis, keepdims=False)


def to_micro_x(values, side):
    count, rows, width = values.shape
    halves = values.reshape(2, 2, rows, width)
    return swap(pick(halves, 1 - side), 2), halves


def to_micro_c(got, halves, side, core):
    both = jnp.stack([pick(halves, side), got], 1)
    return pick(both, core), swap(pick(both, 1 - core), CORE)


def to_micro_end(kept, got):
    return jnp.concatenate([kept, got]).reshape(-1, kept.shape[-1])


def from_micro_c(values):
    rows, width = values.shape[0] // 4, values.shape[1]
    parts = values.reshape(2, 2, rows, width)
    return parts[0], swap(parts[1], CORE)


def from_micro_pick(kept, got, core):
    both = jnp.where(core == 0, jnp.stack([kept, got]), jnp.stack([got, kept]))
    return both[:, 0], both[:, 1]


def from_micro_end(kept, got, side):
    halves = jnp.where(side == 0, jnp.stack([kept, got]), jnp.stack([got, kept]))
    return halves.reshape(4, *kept.shape[1:])


def on_device_fast(
    inputs,
    segments,
    norm1_gain,
    norm1_bias,
    qkv_weight,
    query_bias,
    value_bias,
    out_weight,
    out_bias,
    norm2_gain,
    norm2_bias,
    up_weight,
    up_bias,
    down_weight,
    down_bias,
    cotangent,
):
    f32, bf16 = jnp.float32, jnp.bfloat16
    local_rows, width = inputs.shape[1], inputs.shape[2]
    rows = width // DEVICES
    wide, inner = qkv_weight.shape[1], up_weight.shape[1]
    group = lax.axis_index("fsdp")
    side, core = group // 2, group % 2
    me = (lax.axis_index("dp") * 4 + group).astype(jnp.int32).reshape(1)

    vectors = (
        norm1_gain,
        norm1_bias,
        query_bias,
        value_bias,
        out_bias,
        norm2_gain,
        norm2_bias,
        down_bias,
    )
    row = lax.broadcasted_iota(jnp.int32, (rows, rows), 0)
    block = jnp.zeros((rows, rows), bf16)
    for j, vector in enumerate(vectors):
        block = jnp.where(row == j, vector[None], block)
    block = jnp.pad(block, ((0, 0), (0, 128 - rows)))
    row = lax.broadcasted_iota(jnp.int32, (rows, 128), 0)
    block = jnp.where(row == 8, jnp.pad(up_bias, (0, 128 - up_bias.shape[0]))[None], block)
    first = Gather(jnp.concatenate([qkv_weight, block], 1))
    second = Gather(jnp.concatenate([out_weight, up_weight], 1))
    third = Gather(down_weight)

    first.line()
    token_got, token_halves = to_micro_x(inputs, side)
    own = pick(segments, group).reshape(4, local_rows)
    labels = jnp.concatenate(
        [pick(own, lax.bitwise_xor(group, source)) for source in (0, 2, 1, 3)]
    )
    first.held, first.got, token_got, token_halves, second.held = fence(
        first.held, first.got, token_got, token_halves, second.held
    )

    first.plane()
    second.far()
    second.near()
    token_kept, token_got = to_micro_c(token_got, token_halves, side, core)
    tokens = to_micro_end(token_kept, token_got)
    resid_in = tokens.astype(f32)
    unit_one, _ = norm_parts(resid_in)
    first.held, first.got, second.held, second.got, third.held, unit_one = fence(
        first.held, first.got, second.held, second.got, third.held, unit_one
    )

    first.cores()
    second.plane_one()
    third.far()
    qkv_full, vectors = restore(first, cuts_of((wide, 128)), me)
    qkv_full = qkv_full.reshape(width, wide)
    vectors = vectors[:, :9].astype(f32)
    bias_up = vectors[:, 8, : up_bias.shape[0]].reshape(1, -1)
    (vectors,) = fence(vectors[:, :8, :rows].transpose(1, 0, 2).reshape(8, width))
    (
        gain_one,
        shift_one,
        bias_query,
        bias_value,
        bias_out,
        gain_two,
        shift_two,
        bias_down,
    ) = (vectors[i : i + 1] for i in range(8))
    normed_one = (unit_one * gain_one + shift_one).astype(bf16)
    bias_project = jnp.concatenate([bias_query, jnp.zeros_like(bias_query), bias_value], 1)
    project = (
        jnp.dot(normed_one, qkv_full, preferred_element_type=f32) + bias_project
    ).astype(bf16)
    second.quads, second.got, third.held, third.got, project = fence(
        second.quads, second.got, third.held, third.got, project
    )

    second.plane_two()
    third.near()
    mixed, probs = attend(labels, project)
    second.held, second.got, third.held, third.got, mixed, cotangent = fence(
        second.held, second.got, third.held, third.got, mixed, cotangent
    )

    second.cores()
    cot_got, cot_halves = to_micro_x(cotangent, side)
    second.parts, third.held, third.got, mixed, cot_got, cot_halves = fence(
        second.parts, third.held, third.got, mixed, cot_got, cot_halves
    )

    third.plane()
    cot_kept, cot_got = to_micro_c(cot_got, cot_halves, side, core)
    cot_low = to_micro_end(cot_kept, cot_got)
    out_full, up_full = restore(second, cuts_of((width, inner)), me)
    out_full, up_full = out_full.reshape(width, width), up_full.reshape(width, inner)
    resid_mid = resid_in + jnp.dot(mixed, out_full, preferred_element_type=f32) + bias_out
    unit_two, _ = norm_parts(resid_mid)
    normed_two = (unit_two * gain_two + shift_two).astype(bf16)
    hidden, slope = up_forward(normed_two, up_full, bias_up)
    deep = inner // DEVICES
    down_sum = Scatter(
        parts_call(
            third_parts_kernel, [hidden, cot_low], deep, width, (4 * deep, width), 16, me
        )
    )
    third.held, third.got, down_sum.kept, down_sum.sent, hidden, cot_low = fence(
        third.held, third.got, down_sum.kept, down_sum.sent, hidden, cot_low
    )

    third.cores()
    down_sum.cores()
    third.parts, down_sum.kept, down_sum.got, hidden, cot_low = fence(
        third.parts, down_sum.kept, down_sum.got, hidden, cot_low
    )

    down_sum.plane_one()
    (down_full,) = restore(third, cuts_of((width,)), me, False)
    down_full = down_full.reshape(inner, width)
    grad_pre, grad_bias_up = pre_back(cot_low, down_full, slope)
    grad_mid, branch_low, grad_mixed, sums_two = middle_back(
        grad_pre, up_full, resid_mid, gain_two, cot_low, out_full
    )
    (
        down_sum.kept,
        down_sum.got,
        grad_mid,
        branch_low,
        grad_mixed,
        grad_pre,
        down_full,
        hidden,
    ) = fence(
        down_sum.kept,
        down_sum.got,
        grad_mid,
        branch_low,
        grad_mixed,
        grad_pre,
        down_full,
        hidden,
    )
    down_sum.plane_two()
    up_sum = Scatter(
        parts_call(
            second_parts_kernel,
            [mixed, branch_low, normed_two, grad_pre],
            rows,
            width + inner,
            (width, width),
            20,
            me,
        )
    )
    down_sum.kept, down_sum.got, up_sum.kept, up_sum.sent, grad_mixed, hidden, down_full = fence(
        down_sum.kept, down_sum.got, up_sum.kept, up_sum.sent, grad_mixed, hidden, down_full
    )

    up_sum.cores()
    down_sum.plane_end()
    result = resid_mid + jnp.dot(hidden, down_full, preferred_element_type=f32) + bias_down
    result = result.astype(bf16)
    down_sum.kept, down_sum.got, up_sum.kept, up_sum.got, grad_mixed, result = fence(
        down_sum.kept, down_sum.got, up_sum.kept, up_sum.got, grad_mixed, result
    )

    up_sum.plane_one()
    down_sum.near()
    out_kept, out_got = from_micro_c(result)
    grad_query, grad_key, grad_value = attend_back(project, probs, grad_mixed)
    (
        down_sum.kept,
        down_sum.got,
        up_sum.kept,
        up_sum.got,
        grad_query,
        grad_key,
        grad_value,
        out_kept,
        out_got,
    ) = fence(
        down_sum.kept,
        down_sum.got,
        up_sum.kept,
        up_sum.got,
        grad_query,
        grad_key,
        grad_value,
        out_kept,
        out_got,
    )
    up_sum.plane_two()
    down_sum.far()
    in_grad, sums_one = first_back(
        grad_query, grad_key, grad_value, qkv_full, tokens, gain_one, grad_mid
    )
    qkv_sum = Scatter(
        parts_call(
            first_parts_kernel,
            [
                normed_one,
                grad_query,
                grad_key,
                grad_value,
                sums_one,
                sums_two,
                grad_bias_up,
            ],
            rows,
            wide + 128,
            (width, width),
            16,
            me,
        )
    )
    (
        down_sum.kept,
        down_sum.got,
        up_sum.kept,
        up_sum.got,
        qkv_sum.kept,
        qkv_sum.sent,
        in_grad,
        out_kept,
        out_got,
    ) = fence(
        down_sum.kept,
        down_sum.got,
        up_sum.kept,
        up_sum.got,
        qkv_sum.kept,
        qkv_sum.sent,
        in_grad,
        out_kept,
        out_got,
    )

    up_sum.plane_end()
    qkv_sum.cores()
    in_kept, in_got = from_micro_c(in_grad)
    out_kept, out_sent = from_micro_pick(out_kept, out_got, core)
    (
        up_sum.kept,
        up_sum.got,
        qkv_sum.kept,
        qkv_sum.got,
        in_kept,
        in_got,
        out_kept,
        out_sent,
    ) = fence(
        up_sum.kept,
        up_sum.got,
        qkv_sum.kept,
        qkv_sum.got,
        in_kept,
        in_got,
        out_kept,
        out_sent,
    )

    qkv_sum.plane_one()
    up_sum.near()
    in_kept, in_sent = from_micro_pick(in_kept, in_got, core)
    grad_down = down_sum.total()
    (
        qkv_sum.kept,
        qkv_sum.got,
        up_sum.kept,
        up_sum.got,
        in_kept,
        in_sent,
        out_kept,
        out_sent,
        grad_down,
    ) = fence(
        qkv_sum.kept,
        qkv_sum.got,
        up_sum.kept,
        up_sum.got,
        in_kept,
        in_sent,
        out_kept,
        out_sent,
        grad_down,
    )
    qkv_sum.plane_two()
    up_sum.far()
    out_got = swap(out_sent, X)
    (
        qkv_sum.kept,
        qkv_sum.got,
        up_sum.kept,
        up_sum.got,
        in_kept,
        in_sent,
        out_kept,
        out_got,
    ) = fence(
        qkv_sum.kept,
        qkv_sum.got,
        up_sum.kept,
        up_sum.got,
        in_kept,
        in_sent,
        out_kept,
        out_got,
    )

    in_got = swap(in_sent, X)
    qkv_sum.plane_end()
    qkv_sum.line()
    last = up_sum.total()
    grad_out, grad_up = last[:, :width], last[:, width:]
    output = from_micro_end(out_kept, out_got, side)
    qkv_sum.kept, qkv_sum.got, in_kept, in_got, output, grad_out, grad_up = fence(
        qkv_sum.kept, qkv_sum.got, in_kept, in_got, output, grad_out, grad_up
    )

    in_grad = from_micro_end(in_kept, in_got, side).astype(f32)
    last = qkv_sum.total()
    grad_qkv = last[:, :wide]
    deep, sums = last[8, wide : wide + deep], last[:8, wide : wide + rows]
    return (
        output,
        in_grad,
        sums[0],
        sums[1],
        grad_qkv,
        sums[2],
        sums[3],
        grad_out,
        sums[4],
        sums[5],
        sums[6],
        grad_up,
        deep,
        grad_down,
        sums[7],
    )


def solution(mesh):
    placed = (
        P(None, ("dp", "fsdp"), None),
        P(None, "dp"),
        P(("dp", "fsdp")),
        P(("dp", "fsdp")),
        P(("dp", "fsdp"), None),
        P(("dp", "fsdp")),
        P(("dp", "fsdp")),
        P(("dp", "fsdp"), None),
        P(("dp", "fsdp")),
        P(("dp", "fsdp")),
        P(("dp", "fsdp")),
        P(("dp", "fsdp"), None),
        P(("dp", "fsdp")),
        P(("dp", "fsdp"), None),
        P(("dp", "fsdp")),
        P(None, ("dp", "fsdp"), None),
    )
    fits = mesh.shape["dp"] == 8 and mesh.shape["fsdp"] == 4
    return jax.shard_map(
        on_device_fast if fits else on_device_general,
        mesh=mesh,
        in_specs=placed,
        out_specs=(
            P(None, ("dp", "fsdp"), None),
            P(None, ("dp", "fsdp"), None),
            P(("dp", "fsdp")),
            P(("dp", "fsdp")),
            P(("dp", "fsdp"), None),
            P(("dp", "fsdp")),
            P(("dp", "fsdp")),
            P(("dp", "fsdp"), None),
            P(("dp", "fsdp")),
            P(("dp", "fsdp")),
            P(("dp", "fsdp")),
            P(("dp", "fsdp"), None),
            P(("dp", "fsdp")),
            P(("dp", "fsdp"), None),
            P(("dp", "fsdp")),
        ),
        check_vma=False,
    )
```

```python
import functools
import math

import jax
import jax.numpy as jnp
from jax import lax
from jax.experimental import pallas as pl
from jax.experimental.pallas import tpu as pltpu
from jax.sharding import PartitionSpec as P

HEADS = 12


EPSILON = 1e-06
NEG_LARGE = -1e30
SCALE_SCORE = 0.125


def layer_norm(values, gain_vec, shift_vec):
    centre = values - jnp.mean(values, -1, keepdims=True)
    spread = jnp.mean(centre * centre, -1, keepdims=True)
    return centre * lax.rsqrt(spread + EPSILON) * gain_vec + shift_vec


def gelu_tanh(values):
    return (
        0.5
        * values
        * (1.0 + jnp.tanh(0.7978845608028654 * (values + 0.044715 * values * values * values)))
    )


def add_terms(first_terms, second_terms):
    if first_terms is None:
        return second_terms
    return jax.tree.map(jnp.add, first_terms, second_terms)


def on_device_general(
    inputs,
    segments,
    norm1_gain,
    norm1_bias,
    qkv_weight,
    query_bias,
    value_bias,
    out_weight,
    out_bias,
    norm2_gain,
    norm2_bias,
    up_weight,
    up_bias,
    down_weight,
    down_bias,
    cotangent,
):
    micro_count = inputs.shape[0]
    local_rows = inputs.shape[1]
    model_width = inputs.shape[2]
    group_rows = segments.shape[1]
    key_rows = math.gcd(512, group_rows)
    key_count = group_rows // key_rows
    offset = lax.axis_index("fsdp") * local_rows
    f32 = jnp.float32
    bf16 = jnp.bfloat16
    outputs = []
    in_grads = []
    totals = None
    for micro_index in range(micro_count):
        params_fwd = (
            lax.all_gather(norm1_gain, ("dp", "fsdp"), axis=0, tiled=True),
            lax.all_gather(norm1_bias, ("dp", "fsdp"), axis=0, tiled=True),
            lax.all_gather(qkv_weight, ("dp", "fsdp"), axis=0, tiled=True),
            lax.all_gather(query_bias, ("dp", "fsdp"), axis=0, tiled=True),
            lax.all_gather(value_bias, ("dp", "fsdp"), axis=0, tiled=True),
            lax.all_gather(out_weight, ("dp", "fsdp"), axis=0, tiled=True),
            lax.all_gather(out_bias, ("dp", "fsdp"), axis=0, tiled=True),
            lax.all_gather(norm2_gain, ("dp", "fsdp"), axis=0, tiled=True),
            lax.all_gather(norm2_bias, ("dp", "fsdp"), axis=0, tiled=True),
            lax.all_gather(up_weight, ("dp", "fsdp"), axis=0, tiled=True),
            lax.all_gather(up_bias, ("dp", "fsdp"), axis=0, tiled=True),
            lax.all_gather(down_weight, ("dp", "fsdp"), axis=0, tiled=True),
            lax.all_gather(down_bias, ("dp", "fsdp"), axis=0, tiled=True),
        )
        (
            gain_one,
            shift_one,
            qkv_full,
            bias_query,
            bias_value,
            out_full,
            bias_out,
            gain_two,
            shift_two,
            up_full,
            bias_up,
            down_full,
            bias_down,
        ) = params_fwd
        resid_in = inputs[micro_index].astype(f32)
        normed_one = layer_norm(resid_in, gain_one.astype(f32), shift_one.astype(f32)).astype(bf16)
        project = jnp.dot(normed_one, qkv_full, preferred_element_type=f32)
        queries = (project[:, :model_width] + bias_query.astype(f32)).astype(bf16)
        keys_local = project[:, model_width : 2 * model_width].astype(bf16)
        values_local = (project[:, 2 * model_width :] + bias_value.astype(f32)).astype(bf16)
        keys_all, values_all = (
            lax.all_gather(keys_local, "fsdp", axis=0, tiled=True),
            lax.all_gather(values_local, "fsdp", axis=0, tiled=True),
        )
        labels_all = segments[micro_index]
        labels_query = lax.dynamic_slice_in_dim(labels_all, offset, local_rows)
        query_heads = queries.reshape(local_rows, HEADS, -1)
        key_blocks = keys_all.reshape(key_count, key_rows, HEADS, -1)
        value_blocks = values_all.reshape(key_count, key_rows, HEADS, -1)
        label_blocks = labels_all.reshape(key_count, key_rows)

        def block_scores(key_block, label_block):
            scores = (
                jnp.einsum("qhd,khd->hqk", query_heads, key_block, preferred_element_type=f32)
                * SCALE_SCORE
            )
            allowed = (labels_query[:, None] == label_block[None, :])[None]
            return (jnp.where(allowed, scores, NEG_LARGE), allowed)

        def stat_step(state_in, pieces):
            running_max, running_sum = state_in
            scores, allowed = block_scores(pieces[0], pieces[1])
            newmax = jnp.maximum(running_max, jnp.max(scores, -1))
            exponent = jnp.where(allowed, jnp.exp(scores - newmax[..., None]), 0.0)
            running_sum = running_sum * jnp.exp(running_max - newmax) + jnp.sum(exponent, -1)
            return ((newmax, running_sum), None)

        start_state = (
            jnp.full((HEADS, local_rows), NEG_LARGE, f32),
            jnp.zeros((HEADS, local_rows), f32),
        )
        (final_max, final_sum), _ = lax.scan(stat_step, start_state, (key_blocks, label_blocks))
        log_total = final_max + jnp.log(final_sum)

        def block_prob(key_block, label_block):
            scores, allowed = block_scores(key_block, label_block)
            attend_prob = jnp.where(allowed, jnp.exp(scores - log_total[..., None]), 0.0)
            return (attend_prob, attend_prob.astype(bf16))

        def mix_step(state_in, pieces):
            mixed_acc, extra_acc = state_in
            attend_prob, prob_low = block_prob(pieces[0], pieces[2])
            remainder = (attend_prob - prob_low.astype(f32)).astype(bf16)
            mixed_acc = mixed_acc + jnp.einsum(
                "hqk,khd->qhd", prob_low, pieces[1], preferred_element_type=f32
            )
            extra_acc = extra_acc + jnp.einsum(
                "hqk,khd->qhd", remainder, pieces[1], preferred_element_type=f32
            )
            return ((mixed_acc, extra_acc), None)

        zero_heads = jnp.zeros(query_heads.shape, f32)
        (mixed_heads, extra_heads), _ = lax.scan(
            mix_step, (zero_heads, zero_heads), (key_blocks, value_blocks, label_blocks)
        )
        mixed_low = mixed_heads.reshape(local_rows, model_width).astype(bf16)
        full_mix = mixed_heads + extra_heads
        resid_mid = (
            resid_in
            + jnp.dot(mixed_low, out_full, preferred_element_type=f32)
            + bias_out.astype(f32)
        )
        normed_two = layer_norm(resid_mid, gain_two.astype(f32), shift_two.astype(f32)).astype(bf16)
        pre_act = jnp.dot(normed_two, up_full, preferred_element_type=f32) + bias_up.astype(f32)
        hidden_low = gelu_tanh(pre_act).astype(bf16)
        result = (
            resid_mid
            + jnp.dot(hidden_low, down_full, preferred_element_type=f32)
            + bias_down.astype(f32)
        )
        outputs.append(result.astype(bf16))
        params_bwd = (
            lax.all_gather(norm1_gain, ("dp", "fsdp"), axis=0, tiled=True),
            lax.all_gather(norm1_bias, ("dp", "fsdp"), axis=0, tiled=True),
            lax.all_gather(qkv_weight, ("dp", "fsdp"), axis=0, tiled=True),
            lax.all_gather(query_bias, ("dp", "fsdp"), axis=0, tiled=True),
            lax.all_gather(value_bias, ("dp", "fsdp"), axis=0, tiled=True),
            lax.all_gather(out_weight, ("dp", "fsdp"), axis=0, tiled=True),
            lax.all_gather(out_bias, ("dp", "fsdp"), axis=0, tiled=True),
            lax.all_gather(norm2_gain, ("dp", "fsdp"), axis=0, tiled=True),
            lax.all_gather(norm2_bias, ("dp", "fsdp"), axis=0, tiled=True),
            lax.all_gather(up_weight, ("dp", "fsdp"), axis=0, tiled=True),
            lax.all_gather(up_bias, ("dp", "fsdp"), axis=0, tiled=True),
            lax.all_gather(down_weight, ("dp", "fsdp"), axis=0, tiled=True),
            lax.all_gather(down_bias, ("dp", "fsdp"), axis=0, tiled=True),
        )
        (
            gain_one_b,
            shift_one_b,
            qkv_back,
            bias_query_b,
            bias_value_b,
            out_back,
            bias_out_b,
            gain_two_b,
            shift_two_b,
            up_back,
            bias_up_b,
            down_back,
            bias_down_b,
        ) = params_bwd
        cot_low = cotangent[micro_index]
        cot_full = cot_low.astype(f32)
        grad_down = jnp.einsum("tf,td->fd", hidden_low, cot_low, preferred_element_type=f32)
        grad_bias_down = jnp.sum(cot_full, 0)
        grad_hidden = jnp.einsum("td,fd->tf", cot_low, down_back, preferred_element_type=f32)
        _, gelu_pull = jax.vjp(gelu_tanh, pre_act)
        grad_pre = gelu_pull(grad_hidden)[0].astype(bf16)
        grad_up = jnp.einsum("td,tf->df", normed_two, grad_pre, preferred_element_type=f32)
        grad_bias_up = jnp.sum(grad_pre.astype(f32), 0)
        grad_normed_two = jnp.einsum("tf,df->td", grad_pre, up_back, preferred_element_type=f32)
        _, norm_two_pull = jax.vjp(
            layer_norm, resid_mid, gain_two_b.astype(f32), shift_two_b.astype(f32)
        )
        grad_mid_part, grad_gain_two, grad_shift_two = norm_two_pull(grad_normed_two)
        grad_mid = cot_full + grad_mid_part
        branch_low = grad_mid.astype(bf16)
        grad_out = jnp.einsum("td,te->de", mixed_low, branch_low, preferred_element_type=f32)
        grad_bias_out = jnp.sum(branch_low.astype(f32), 0)
        grad_mixed = jnp.einsum(
            "te,de->td", branch_low, out_back, preferred_element_type=f32
        ).astype(bf16)
        grad_heads = grad_mixed.reshape(local_rows, HEADS, -1)
        delta = jnp.einsum("qhd,qhd->hq", grad_heads.astype(f32), full_mix)

        def grad_step(query_acc, pieces):
            key_block, value_block, label_block = pieces
            attend_prob, prob_low = block_prob(key_block, label_block)
            grad_prob = jnp.einsum(
                "qhd,khd->hqk", grad_heads, value_block, preferred_element_type=f32
            )
            grad_scores = (attend_prob * (grad_prob - delta[..., None]) * SCALE_SCORE).astype(bf16)
            query_acc = query_acc + jnp.einsum(
                "hqk,khd->qhd", grad_scores, key_block, preferred_element_type=f32
            )
            key_part = jnp.einsum(
                "hqk,qhd->khd", grad_scores, query_heads, preferred_element_type=f32
            )
            value_part = jnp.einsum(
                "hqk,qhd->khd", prob_low, grad_heads, preferred_element_type=f32
            )
            return (query_acc, (key_part, value_part))

        query_grad, (key_parts, value_parts) = lax.scan(
            grad_step, zero_heads, (key_blocks, value_blocks, label_blocks)
        )
        key_parts = key_parts.reshape(group_rows, model_width)
        value_parts = value_parts.reshape(group_rows, model_width)
        key_grad, value_grad = (
            lax.psum_scatter(
                key_parts.astype(jnp.bfloat16), "fsdp", scatter_dimension=0, tiled=True
            ).astype(jnp.float32),
            lax.psum_scatter(
                value_parts.astype(jnp.bfloat16), "fsdp", scatter_dimension=0, tiled=True
            ).astype(jnp.float32),
        )
        query_low = query_grad.reshape(local_rows, model_width).astype(bf16)
        key_low = key_grad.astype(bf16)
        value_low = value_grad.astype(bf16)
        grad_project = jnp.concatenate([query_low, key_low, value_low], 1)
        grad_qkv = jnp.einsum("td,te->de", normed_one, grad_project, preferred_element_type=f32)
        grad_bias_query = jnp.sum(query_low.astype(f32), 0)
        grad_bias_value = jnp.sum(value_low.astype(f32), 0)
        grad_normed_one = jnp.einsum(
            "te,de->td", grad_project, qkv_back, preferred_element_type=f32
        )
        _, norm_one_pull = jax.vjp(
            layer_norm, resid_in, gain_one_b.astype(f32), shift_one_b.astype(f32)
        )
        grad_in_part, grad_gain_one, grad_shift_one = norm_one_pull(grad_normed_one)
        in_grads.append(grad_mid + grad_in_part)
        local_terms = (
            grad_gain_one,
            grad_shift_one,
            grad_qkv,
            grad_bias_query,
            grad_bias_value,
            grad_out,
            grad_bias_out,
            grad_gain_two,
            grad_shift_two,
            grad_up,
            grad_bias_up,
            grad_down,
            grad_bias_down,
        )
        shard_terms = (
            lax.psum_scatter(local_terms[0], ("dp", "fsdp"), scatter_dimension=0, tiled=True),
            lax.psum_scatter(local_terms[1], ("dp", "fsdp"), scatter_dimension=0, tiled=True),
            lax.psum_scatter(local_terms[2], ("dp", "fsdp"), scatter_dimension=0, tiled=True),
            lax.psum_scatter(local_terms[3], ("dp", "fsdp"), scatter_dimension=0, tiled=True),
            lax.psum_scatter(local_terms[4], ("dp", "fsdp"), scatter_dimension=0, tiled=True),
            lax.psum_scatter(local_terms[5], ("dp", "fsdp"), scatter_dimension=0, tiled=True),
            lax.psum_scatter(local_terms[6], ("dp", "fsdp"), scatter_dimension=0, tiled=True),
            lax.psum_scatter(local_terms[7], ("dp", "fsdp"), scatter_dimension=0, tiled=True),
            lax.psum_scatter(local_terms[8], ("dp", "fsdp"), scatter_dimension=0, tiled=True),
            lax.psum_scatter(local_terms[9], ("dp", "fsdp"), scatter_dimension=0, tiled=True),
            lax.psum_scatter(local_terms[10], ("dp", "fsdp"), scatter_dimension=0, tiled=True),
            lax.psum_scatter(local_terms[11], ("dp", "fsdp"), scatter_dimension=0, tiled=True),
            lax.psum_scatter(local_terms[12], ("dp", "fsdp"), scatter_dimension=0, tiled=True),
        )
        totals = add_terms(totals, shard_terms)
    return (
        jnp.stack(outputs),
        jnp.stack(in_grads),
        totals[0],
        totals[1],
        totals[2],
        totals[3],
        totals[4],
        totals[5],
        totals[6],
        totals[7],
        totals[8],
        totals[9],
        totals[10],
        totals[11],
        totals[12],
    )


AXES = ("dp", "fsdp")
CORE, X, Y, Z0, Z1 = 1, 2, 4, 8, 16
LINE = (0, Z1, Z0, Z1 ^ Z0)
PLANE = (0, X, Y, X ^ Y)
DEVICES = 32
MIB = 1024 * 1024
SMALL = pl.CostEstimate(flops=1024, transcendentals=0, bytes_accessed=1024)


def swap(values, mask):
    pairs = [(i, i ^ mask) for i in range(DEVICES)]
    return lax.ppermute(values, AXES, pairs)


SLOTS = [core ^ plane ^ line for core in (0, CORE) for plane in PLANE for line in LINE]


def fence(*values):
    return lax.optimization_barrier(values)


def join(*parts):
    return lax.optimization_barrier(jnp.concatenate(parts, 0))


def halves_of(width):
    half = width // 256 * 128
    return ((0, half), (half, width))


class Gather:
    def __init__(self, shard):
        self.held = shard[None]
        self.across = []

    def line(self):
        self.got = [swap(self.held, mask) for mask in LINE[1:]]

    def far(self):
        self.got = [swap(self.held, Z1)]

    def near(self):
        self.held = join(self.held, *self.got)
        self.got = [swap(self.held, Z0)]

    def line_end(self):
        self.held, self.got = join(self.held, *self.got), []

    def plane(self):
        self.held = join(self.held, *self.got) if self.got else self.held
        self.got = [swap(self.held, mask) for mask in PLANE[1:]]

    def plane_one(self):
        self.held = join(self.held, *self.got)
        self.quads = [self.held[..., low:high] for low, high in halves_of(self.held.shape[2])]
        self.got = [swap(quad, bit) for quad, bit in zip(self.quads, (X, Y))]

    def plane_two(self):
        own = [one for pair in zip(self.quads, self.got) for one in pair]
        bits = (Y, Y, X, X)
        self.held, self.got = own[0], own[1:] + [swap(one, bit) for one, bit in zip(own, bits)]

    def cores(self):
        own = [self.held, *self.got]
        self.parts = own + [swap(piece, CORE) for piece in own]

    def places(self):
        width = self.held.shape[2]
        if len(self.got) == 3:
            masks = [core ^ plane ^ line for core in (0, CORE) for plane in PLANE for line in LINE]
            return [(i // 4, i % 4, mask, 0, width) for i, mask in enumerate(masks)]
        spans = ((0, width), (width, width + self.got[2].shape[2]))
        return [
            (8 * core + 4 * second + 2 * half + first, i, mask, low, high)
            for core in (0, CORE)
            for half, ((low, high), bits) in enumerate(zip(spans, ((X, Y), (Y, X))))
            for second in (0, 1)
            for first in (0, 1)
            for i, line in enumerate(LINE)
            for mask in (core ^ line ^ bits[0] * first ^ bits[1] * second,)
        ]


def sum_low(*terms):
    total = sum(term.astype(jnp.float32) for term in terms)
    return total.astype(jnp.bfloat16)


class Scatter:
    places = [
        [
            (slot // 16, slot % 16, core ^ plane ^ line)
            for slot, (core, plane, line) in enumerate(
                (core, plane, line) for core in (0, CORE) for plane in planes for line in LINE
            )
        ]
        for planes in ((0, X, Y, X ^ Y), (0, Y, X, X ^ Y))
    ]

    def __init__(self, halves):
        self.kept, self.sent = halves

    def cores(self):
        self.got = swap(self.sent, CORE)

    def line(self):
        terms = [self.kept, *self.got]
        ones = [sum_low(*(term[i : i + 1] for term in terms)) for i in range(1, 4)]
        self.kept = sum(term[0].astype(jnp.float32) for term in terms)
        self.got = [swap(one, mask) for one, mask in zip(ones, LINE[1:])]

    def plane_one(self):
        kept, sent = [], []
        for low, high in halves_of(self.kept.shape[2]):
            pairs = [(one[..., low:high]) for one in (self.kept, self.got)]
            kept.append(sum_low(*(one[:8] for one in pairs)))
            sent.append(sum_low(*(one[8:] for one in pairs)))
        self.kept, self.got = kept, [swap(one, bit) for one, bit in zip(sent, (Y, X))]

    def plane_two(self):
        sent = [
            swap(sum_low(kept[4:], got[4:]), bit)
            for kept, got, bit in zip(self.kept, self.got, (X, Y))
        ]
        kept = [sum_low(kept[:4], got[:4]) for kept, got in zip(self.kept, self.got)]
        self.kept, self.got = jnp.concatenate(kept, -1), sent

    def plane_end(self):
        self.got = [jnp.concatenate(self.got, -1)]

    def near(self):
        terms = [self.kept, *self.got]
        self.kept = sum_low(*(term[:2] for term in terms))
        self.got = [swap(sum_low(*(term[2:] for term in terms)), Z0)]

    def far(self):
        got = self.got[0]
        self.got = [swap(sum_low(self.kept[1:], got[1:]), Z1)]
        self.kept = self.kept[0].astype(jnp.float32) + got[0].astype(jnp.float32)

    def total(self):
        return self.kept + sum(got[0].astype(jnp.float32) for got in self.got)


def cuts_of(parts):
    ends = [sum(parts[: i + 1]) for i in range(len(parts))]
    return tuple((end - part, end) for end, part in zip(ends, parts))


def shuffle_kernel(moves, count, me_ref, *refs):
    me = me_ref[0]

    def part(slot):
        return pl.ds(lax.bitwise_xor(me, slot[0]) if isinstance(slot, tuple) else slot, 1)

    for source, source_slot, source_low, target, target_slot, target_low, width in moves:
        refs[count + target][part(target_slot), :, target_low : target_low + width] = refs[source][
            part(source_slot), :, source_low : source_low + width
        ]


def whole_block(shape):
    return pl.BlockSpec(shape, lambda i: (0,) * len(shape), pipeline_mode=pl.Buffered(1))


def shuffle(arrays, shapes, moves, me, pinned):
    dtype = arrays[0].dtype
    size = sum(math.prod(shape) for shape in shapes)
    make = pltpu.HBM if pinned else jax.ShapeDtypeStruct
    return pl.pallas_call(
        functools.partial(shuffle_kernel, moves, len(arrays)),
        grid=(1,),
        out_shape=[make(shape, dtype) for shape in shapes],
        in_specs=[pl.BlockSpec(memory_space=pltpu.SMEM)]
        + [whole_block(array.shape) for array in arrays],
        out_specs=[whole_block(shape) for shape in shapes],
        compiler_params=pltpu.CompilerParams(vmem_limit_bytes=16 * MIB),
        cost_estimate=SMALL,
    )(me, *arrays)


def restore(gather, cuts, me, pinned=True):
    moves = []
    for part, slot, mask, low, high in gather.places():
        for target, (begin, end) in enumerate(cuts):
            left, right = max(low, begin), min(high, end)
            if left < right:
                moves.append(
                    (part, slot, left - low, target, (mask,), left - begin, right - left)
                )
    rows = gather.parts[0].shape[1]
    shapes = [(DEVICES, rows, end - begin) for begin, end in cuts]
    return shuffle(gather.parts, shapes, moves, me, pinned)


TN = (((0,), (0,)), ((), ()))


def finish_kernel(cuts, *refs):
    kept_ref, got_refs, outs = refs[0], refs[1 : -len(cuts)], refs[-len(cuts) :]
    for out_ref, (begin, end) in zip(outs, cuts):
        total = kept_ref[:, begin:end]
        for ref in got_refs:
            total = total + ref[0, :, begin:end].astype(jnp.float32)
        out_ref[...] = total


def finish(scatter, parts):
    inputs = [scatter.kept, *scatter.got]
    shapes = [(scatter.kept.shape[0], part) for part in parts]
    return pl.pallas_call(
        functools.partial(finish_kernel, cuts_of(parts)),
        grid=(1,),
        out_shape=[jax.ShapeDtypeStruct(shape, jnp.float32) for shape in shapes],
        in_specs=[whole_block(value.shape) for value in inputs],
        out_specs=[whole_block(shape) for shape in shapes],
        compiler_params=pltpu.CompilerParams(vmem_limit_bytes=8 * MIB),
        cost_estimate=SMALL,
    )(*inputs)


def parts_call(kernel, inputs, rows, width, scratch, limit, me):
    half = (DEVICES // 2, rows, width)
    return pl.pallas_call(
        kernel,
        grid=(1,),
        out_shape=[jax.ShapeDtypeStruct(half, jnp.bfloat16)] * 2,
        in_specs=[pl.BlockSpec(memory_space=pltpu.SMEM)]
        + [whole_block(value.shape) for value in inputs],
        out_specs=[whole_block(half)] * 2,
        scratch_shapes=[pltpu.VMEM(scratch, jnp.float32)],
        compiler_params=pltpu.CompilerParams(vmem_limit_bytes=limit * MIB),
        cost_estimate=SMALL,
    )(me, *inputs)


def store_rows(me, sum_ref, outs, low, high):
    rows = sum_ref.shape[0] // DEVICES
    for places, (begin, end) in zip(Scatter.places, halves_of(outs[0].shape[2])):
        left, right = max(low, begin), min(high, end)
        if left < right:
            for half, slot, mask in places:
                first = pl.multiple_of(lax.bitwise_xor(me, mask) * rows, rows)
                outs[half][slot, :, left:right] = sum_ref[
                    pl.ds(first, rows), left - low : right - low
                ].astype(jnp.bfloat16)


def multiply_rows(me, left_ref, right_refs, sum_ref, outs, low):
    width = sum_ref.shape[1]
    for ref in right_refs:
        for begin in range(0, ref.shape[1], width):
            sum_ref[...] = lax.dot_general(
                left_ref[...],
                ref[:, begin : begin + width],
                TN,
                preferred_element_type=jnp.float32,
            )
            store_rows(me, sum_ref, outs, low + begin, low + begin + width)
        low += ref.shape[1]
    return low


def second_parts_kernel(
    me_ref, mixed_ref, branch_ref, normed_ref, pre_ref, kept_ref, sent_ref, sum_ref
):
    me, outs = me_ref[0], (kept_ref, sent_ref)
    low = multiply_rows(me, mixed_ref, [branch_ref], sum_ref, outs, 0)
    multiply_rows(me, normed_ref, [pre_ref], sum_ref, outs, low)


def first_parts_kernel(
    me_ref,
    normed_ref,
    query_ref,
    key_ref,
    value_ref,
    one_ref,
    two_ref,
    bias_ref,
    kept_ref,
    sent_ref,
    sum_ref,
):
    me, outs = me_ref[0], (kept_ref, sent_ref)
    low = multiply_rows(me, normed_ref, [query_ref, key_ref, value_ref], sum_ref, outs, 0)
    rows = kept_ref.shape[1]
    vectors = jnp.concatenate([one_ref[:4], two_ref[:4]], 0)
    width, bias = vectors.shape[1], jnp.broadcast_to(bias_ref[...], (8, bias_ref.shape[1]))
    deep = bias.shape[1] // DEVICES
    spare = jnp.zeros((rows - 16, 128), jnp.float32)
    for half, slot, mask in Scatter.places[1]:
        owner = lax.bitwise_xor(me, mask)
        here = pltpu.roll(vectors, lax.rem(width - rows * owner, width), 1)[:, :128]
        bias_here = pltpu.roll(bias, lax.rem(DEVICES * deep - deep * owner, DEVICES * deep), 1)
        outs[half][slot, :, low:] = jnp.concatenate(
            [here, bias_here[:, :128], spare], 0
        ).astype(jnp.bfloat16)


def third_parts_kernel(me_ref, hidden_ref, cot_ref, kept_ref, sent_ref, sum_ref):
    me, outs = me_ref[0], (kept_ref, sent_ref)
    rows = kept_ref.shape[1]
    for block in range(DEVICES // 4):
        first = pl.multiple_of(lax.bitwise_xor(me // 4, block) * (4 * rows), 4 * rows)
        sum_ref[...] = lax.dot_general(
            hidden_ref[:, pl.ds(first, 4 * rows)],
            cot_ref[...],
            TN,
            preferred_element_type=jnp.float32,
        )
        for places, (low, high) in zip(Scatter.places, halves_of(cot_ref.shape[1])):
            for half, slot, mask in places:
                if mask // 4 == block:
                    first = pl.multiple_of(lax.bitwise_xor(me % 4, mask % 4) * rows, rows)
                    outs[half][slot, :, low:high] = sum_ref[pl.ds(first, rows), low:high].astype(
                        jnp.bfloat16
                    )


NT = (((1,), (1,)), ((), ()))


def make_mask(labels_ref, mask_ref):
    @pl.when(pl.program_id(0) == 0)
    def _():
        across = labels_ref[...].astype(jnp.float32)
        down = jnp.broadcast_to(across, (8, across.shape[1])).T[:, :1]
        allowed = down == across
        mask_ref[...] = jnp.where(allowed, 0.0, NEG_LARGE)


def head_probs(keys, queries, head, mask_ref):
    f32 = jnp.float32
    lane = lax.broadcasted_iota(jnp.int32, queries.shape, 1)
    own = (lane // 64) == head
    chosen = jnp.where(own, queries.astype(f32) * SCALE_SCORE, 0.0).astype(jnp.bfloat16)
    scores = lax.dot_general(keys, chosen, NT, preferred_element_type=f32) + mask_ref[...]
    exponent = jnp.exp(scores - jnp.max(scores, 0, keepdims=True))
    return exponent * (1.0 / jnp.sum(exponent, 0, keepdims=True))


def attend_kernel(row_ref, query_ref, key_ref, value_ref, out_ref, prob_ref, mask_ref):
    make_mask(row_ref, mask_ref)
    keys, queries = key_ref[...], query_ref[...]
    values_across = value_ref[...].astype(jnp.float32).T.astype(jnp.bfloat16)
    mixed = []
    for head in range(2):
        prob_ref[head] = head_probs(keys, queries, head, mask_ref).astype(jnp.bfloat16)
        mixed.append(
            jnp.dot(
                values_across[64 * head : 64 * head + 64],
                prob_ref[head],
                preferred_element_type=jnp.float32,
            )
        )
    out_ref[...] = jnp.concatenate(mixed, 0).T.astype(jnp.bfloat16)


def attend_back_kernel(
    query_ref, key_ref, value_ref, prob_ref, grad_ref, dquery_ref, dkey_ref, dvalue_ref
):
    f32, bf16 = jnp.float32, jnp.bfloat16
    keys, queries, values, grads = key_ref[...], query_ref[...], value_ref[...], grad_ref[...]
    keys_across = keys.astype(f32).T.astype(bf16)
    lane = lax.broadcasted_iota(jnp.int32, keys.shape, 1)
    dquery, dkey, dvalue = [], [], []
    for head in range(2):
        chosen = jnp.where((lane // 64) == head, grads.astype(f32), 0.0).astype(bf16)
        grad_prob = lax.dot_general(values, chosen, NT, preferred_element_type=f32)
        prob = prob_ref[head].astype(f32)
        delta = jnp.sum(prob * grad_prob, 0, keepdims=True)
        grad_scores = (prob * (grad_prob - delta)).astype(bf16)
        dvalue.append(jnp.dot(prob_ref[head], grads, preferred_element_type=f32))
        dkey.append(jnp.dot(grad_scores, queries, preferred_element_type=f32))
        dquery.append(
            jnp.dot(
                keys_across[64 * head : 64 * head + 64], grad_scores, preferred_element_type=f32
            )
        )
    low_half = lane < 64
    dquery_ref[...] = (jnp.concatenate(dquery, 0).T * SCALE_SCORE).astype(bf16)
    dkey_ref[...] = (jnp.where(low_half, dkey[0], dkey[1]) * SCALE_SCORE).astype(bf16)
    dvalue_ref[...] = jnp.where(low_half, dvalue[0], dvalue[1]).astype(bf16)


def pair_specs(tokens, pairs):
    parts = [
        pl.BlockSpec((tokens, 128), lambda i, part=part: (0, i + part * pairs))
        for part in range(3)
    ]
    return parts, pl.BlockSpec((2, tokens, tokens), lambda i: (i, 0, 0))


def in_hbm(array):
    return pltpu.with_memory_space_constraint(array, pltpu.HBM)


def attend(labels, project):
    tokens, pairs = project.shape[0], HEADS // 2
    parts, probs = pair_specs(tokens, pairs)
    return pl.pallas_call(
        attend_kernel,
        grid=(pairs,),
        out_shape=[
            jax.ShapeDtypeStruct((tokens, 128 * pairs), jnp.bfloat16),
            pltpu.HBM((HEADS, tokens, tokens), jnp.bfloat16),
        ],
        in_specs=[
            pl.BlockSpec((1, tokens), lambda i: (0, 0)),
            *parts,
        ],
        out_specs=[pl.BlockSpec((tokens, 128), lambda i: (0, i)), probs],
        scratch_shapes=[pltpu.VMEM((tokens, tokens), jnp.float32)],
        compiler_params=pltpu.CompilerParams(vmem_limit_bytes=12 * MIB),
        cost_estimate=SMALL,
    )(labels.reshape(1, tokens), project, project, project)


def attend_back(project, probs, grads):
    tokens, pairs = project.shape[0], HEADS // 2
    block = pl.BlockSpec((tokens, 128), lambda i: (0, i))
    shape = jax.ShapeDtypeStruct((tokens, 128 * pairs), jnp.bfloat16)
    parts, prob_spec = pair_specs(tokens, pairs)
    return pl.pallas_call(
        attend_back_kernel,
        grid=(pairs,),
        out_shape=[shape] * 3,
        in_specs=[*parts, prob_spec, block],
        out_specs=[block] * 3,
        compiler_params=pltpu.CompilerParams(vmem_limit_bytes=14 * MIB),
        cost_estimate=SMALL,
    )(project, project, project, in_hbm(probs), grads)


def norm_parts(values):
    centre = values - jnp.mean(values, -1, keepdims=True)
    scale = lax.rsqrt(jnp.mean(centre * centre, -1, keepdims=True) + EPSILON)
    return centre * scale, scale


def norm_back(grads, values, gain_row):
    unit, scale = norm_parts(values)
    inner = grads * gain_row
    part = inner - jnp.mean(inner, -1, keepdims=True)
    part = part - unit * jnp.mean(inner * unit, -1, keepdims=True)
    gain, shift = jnp.sum(grads * unit, 0, keepdims=True), jnp.sum(grads, 0, keepdims=True)
    return part * scale, gain, shift


def column_sum(values):
    return jnp.sum(values.astype(jnp.float32), 0, keepdims=True)


def project_kernel(normed_ref, weight_ref, bias_ref, out_ref):
    for row in range(0, normed_ref.shape[0], 128):
        rows = slice(row, row + 128)
        out = jnp.dot(normed_ref[rows], weight_ref[...], preferred_element_type=jnp.float32)
        out_ref[rows] = (out + bias_ref[...]).astype(jnp.bfloat16)


def project_forward(normed, qkv_full, bias_row):
    tokens, width = normed.shape
    wide, tile = qkv_full.shape[1], 768
    return pl.pallas_call(
        project_kernel,
        grid=(wide // tile,),
        out_shape=jax.ShapeDtypeStruct((tokens, wide), jnp.bfloat16),
        in_specs=[
            pl.BlockSpec((tokens, width), lambda i: (0, 0)),
            pl.BlockSpec((width, tile), lambda i: (0, i)),
            pl.BlockSpec((1, tile), lambda i: (0, i)),
        ],
        out_specs=pl.BlockSpec((tokens, tile), lambda i: (0, i)),
        compiler_params=pltpu.CompilerParams(vmem_limit_bytes=12 * MIB),
        cost_estimate=SMALL,
    )(normed, in_hbm(qkv_full), bias_row)


def up_kernel(normed_ref, weight_ref, bias_ref, hidden_ref, slope_ref):
    bf16 = jnp.bfloat16
    first, third = 0.7978845608028654, 0.7978845608028654 * 0.044715
    for row in range(0, normed_ref.shape[0], 128):
        rows = slice(row, row + 128)
        pre = jnp.dot(normed_ref[rows], weight_ref[...], preferred_element_type=jnp.float32)
        pre = pre + bias_ref[...]
        square = pre * pre
        half = 0.5 + 0.5 * jnp.tanh(pre * (first + third * square))
        hidden_ref[rows] = (pre * half).astype(bf16)
        inner = pre * (2 * first + 6 * third * square)
        slope_ref[rows] = (half + half * inner * (1.0 - half)).astype(bf16)


def up_forward(normed, up_full, bias_row):
    tokens, width = normed.shape
    inner, tile = up_full.shape[1], 768
    block = pl.BlockSpec((tokens, tile), lambda i: (0, i))
    shape = jax.ShapeDtypeStruct((tokens, inner), jnp.bfloat16)
    return pl.pallas_call(
        up_kernel,
        grid=(inner // tile,),
        out_shape=[shape, shape],
        in_specs=[
            pl.BlockSpec((tokens, width), lambda i: (0, 0)),
            pl.BlockSpec((width, tile), lambda i: (0, i)),
            pl.BlockSpec((1, tile), lambda i: (0, i)),
        ],
        out_specs=[block, block],
        compiler_params=pltpu.CompilerParams(vmem_limit_bytes=18 * MIB),
        cost_estimate=SMALL,
    )(normed, in_hbm(up_full), bias_row)


def pre_kernel(cot_ref, weight_ref, slope_ref, pre_ref, sum_ref):
    f32 = jnp.float32
    grads = lax.dot_general(cot_ref[...], weight_ref[...], NT, preferred_element_type=f32)
    low = (grads * slope_ref[...].astype(f32)).astype(jnp.bfloat16)
    pre_ref[...] = low
    sum_ref[...] = column_sum(low)


def pre_back(cot_low, down_full, slope):
    tokens, width = cot_low.shape
    inner, tile = down_full.shape[0], 512
    block = pl.BlockSpec((tokens, tile), lambda i: (0, i))
    return pl.pallas_call(
        pre_kernel,
        grid=(inner // tile,),
        out_shape=[
            jax.ShapeDtypeStruct((tokens, inner), jnp.bfloat16),
            jax.ShapeDtypeStruct((1, inner), jnp.float32),
        ],
        in_specs=[
            pl.BlockSpec((tokens, width), lambda i: (0, 0)),
            pl.BlockSpec((tile, width), lambda i: (i, 0)),
            block,
        ],
        out_specs=[block, pl.BlockSpec((1, tile), lambda i: (0, i))],
        compiler_params=pltpu.CompilerParams(vmem_limit_bytes=12 * MIB),
        cost_estimate=SMALL,
    )(cot_low, down_full, slope)


def middle_kernel(pre_ref, up_ref, resid_ref, gain_ref, cot_ref, out_ref, mid_ref, low_ref, mixed_ref, sums_ref):
    f32, bf16 = jnp.float32, jnp.bfloat16

    @pl.when(pl.program_id(0) == 0)
    def _():
        sums_ref[...] = jnp.zeros_like(sums_ref)

    grads = lax.dot_general(pre_ref[...], up_ref[...], NT, preferred_element_type=f32)
    part, gain, shift = norm_back(grads, resid_ref[...], gain_ref[...])
    cot = cot_ref[...].astype(f32)
    mid = cot + part
    low = mid.astype(bf16)
    mid_ref[...] = mid
    low_ref[...] = low
    mixed_ref[...] = lax.dot_general(
        low, out_ref[...], NT, preferred_element_type=f32
    ).astype(bf16)
    for row, value in enumerate((column_sum(low), gain, shift, column_sum(cot))):
        sums_ref[row : row + 1] += value


def middle_back(grad_pre, up_full, resid_mid, gain_row, cot_low, out_full):
    tokens, inner = grad_pre.shape
    width, tile = resid_mid.shape[1], 256
    block = pl.BlockSpec((tile, width), lambda i: (i, 0))
    whole = lambda *shape: pl.BlockSpec(shape, lambda i: (0, 0))
    return pl.pallas_call(
        middle_kernel,
        grid=(tokens // tile,),
        out_shape=[
            jax.ShapeDtypeStruct((tokens, width), jnp.float32),
            jax.ShapeDtypeStruct((tokens, width), jnp.bfloat16),
            jax.ShapeDtypeStruct((tokens, width), jnp.bfloat16),
            jax.ShapeDtypeStruct((8, width), jnp.float32),
        ],
        in_specs=[
            pl.BlockSpec((tile, inner), lambda i: (i, 0)),
            whole(width, inner),
            block,
            whole(1, width),
            block,
            whole(width, width),
        ],
        out_specs=[block, block, block, whole(8, width)],
        compiler_params=pltpu.CompilerParams(vmem_limit_bytes=20 * MIB),
        cost_estimate=SMALL,
    )(grad_pre, up_full, resid_mid, gain_row, cot_low, out_full)


def first_kernel(
    query_ref, key_ref, value_ref, weight_ref, token_ref, gain_ref, mid_ref, in_ref, sums_ref
):
    f32 = jnp.float32

    @pl.when(pl.program_id(0) == 0)
    def _():
        sums_ref[...] = jnp.zeros_like(sums_ref)

    width = query_ref.shape[1]
    grads = sum(
        lax.dot_general(
            ref[...],
            weight_ref[:, width * i : width * (i + 1)],
            NT,
            preferred_element_type=f32,
        )
        for i, ref in enumerate((query_ref, key_ref, value_ref))
    )
    part, gain, shift = norm_back(grads, token_ref[...].astype(f32), gain_ref[...])
    in_ref[...] = (mid_ref[...] + part).astype(jnp.bfloat16)
    rows = (gain, shift, column_sum(query_ref[...]), column_sum(value_ref[...]))
    for row, value in enumerate(rows):
        sums_ref[row : row + 1] += value


def first_back(grad_query, grad_key, grad_value, qkv_full, tokens_in, gain_row, grad_mid):
    tokens, width = tokens_in.shape
    tile = 256
    block = pl.BlockSpec((tile, width), lambda i: (i, 0))
    whole = lambda *shape: pl.BlockSpec(shape, lambda i: (0, 0))
    return pl.pallas_call(
        first_kernel,
        grid=(tokens // tile,),
        out_shape=[
            jax.ShapeDtypeStruct((tokens, width), jnp.bfloat16),
            jax.ShapeDtypeStruct((8, width), jnp.float32),
        ],
        in_specs=[
            block,
            block,
            block,
            whole(width, 3 * width),
            block,
            whole(1, width),
            block,
        ],
        out_specs=[block, whole(8, width)],
        compiler_params=pltpu.CompilerParams(vmem_limit_bytes=16 * MIB),
        cost_estimate=SMALL,
    )(grad_query, grad_key, grad_value, qkv_full, tokens_in, gain_row, grad_mid)


def pick(values, index, axis=0):
    return lax.dynamic_index_in_dim(values, index, axis, keepdims=False)


def to_micro_x(values, side):
    count, rows, width = values.shape
    halves = values.reshape(2, 2, rows, width)
    return swap(pick(halves, 1 - side), 2), halves


def to_micro_c(got, halves, side, core):
    both = jnp.stack([pick(halves, side), got], 1)
    return pick(both, core), swap(pick(both, 1 - core), CORE)


def to_micro_end(kept, got):
    return jnp.concatenate([kept, got]).reshape(-1, kept.shape[-1])


def from_micro_c(values):
    rows, width = values.shape[0] // 4, values.shape[1]
    parts = values.reshape(2, 2, rows, width)
    return parts[0], swap(parts[1], CORE)


def from_micro_pick(kept, got, core):
    both = jnp.where(core == 0, jnp.stack([kept, got]), jnp.stack([got, kept]))
    return both[:, 0], both[:, 1]


def from_micro_end(kept, got, side):
    halves = jnp.where(side == 0, jnp.stack([kept, got]), jnp.stack([got, kept]))
    return halves.reshape(4, *kept.shape[1:])


def on_device_fast(
    inputs,
    segments,
    norm1_gain,
    norm1_bias,
    qkv_weight,
    query_bias,
    value_bias,
    out_weight,
    out_bias,
    norm2_gain,
    norm2_bias,
    up_weight,
    up_bias,
    down_weight,
    down_bias,
    cotangent,
):
    f32, bf16 = jnp.float32, jnp.bfloat16
    local_rows, width = inputs.shape[1], inputs.shape[2]
    rows = width // DEVICES
    wide, inner = qkv_weight.shape[1], up_weight.shape[1]
    group = lax.axis_index("fsdp")
    side, core = group // 2, group % 2
    me = (lax.axis_index("dp") * 4 + group).astype(jnp.int32).reshape(1)

    vectors = (
        norm1_gain,
        norm1_bias,
        query_bias,
        value_bias,
        out_bias,
        norm2_gain,
        norm2_bias,
        down_bias,
    )
    row = lax.broadcasted_iota(jnp.int32, (rows, rows), 0)
    block = jnp.zeros((rows, rows), bf16)
    for j, vector in enumerate(vectors):
        block = jnp.where(row == j, vector[None], block)
    block = jnp.pad(block, ((0, 0), (0, 128 - rows)))
    row = lax.broadcasted_iota(jnp.int32, (rows, 128), 0)
    block = jnp.where(row == 8, jnp.pad(up_bias, (0, 128 - up_bias.shape[0]))[None], block)
    first = Gather(jnp.concatenate([qkv_weight, block], 1))
    second = Gather(jnp.concatenate([out_weight, up_weight], 1))
    third = Gather(down_weight)

    first.line()
    token_got, token_halves = to_micro_x(inputs, side)
    own = pick(segments, group).reshape(4, local_rows)
    labels = jnp.concatenate(
        [pick(own, lax.bitwise_xor(group, source)) for source in (0, 2, 1, 3)]
    )
    first.held, first.got, token_got, token_halves, second.held = fence(
        first.held, first.got, token_got, token_halves, second.held
    )

    first.plane()
    second.far()
    second.near()
    token_kept, token_got = to_micro_c(token_got, token_halves, side, core)
    tokens = to_micro_end(token_kept, token_got)
    resid_in = tokens.astype(f32)
    unit_one, _ = norm_parts(resid_in)
    first.held, first.got, second.held, second.got, third.held, unit_one = fence(
        first.held, first.got, second.held, second.got, third.held, unit_one
    )

    first.cores()
    second.plane_one()
    third.far()
    qkv_full, vectors = restore(first, cuts_of((wide, 128)), me)
    qkv_full = qkv_full.reshape(width, wide)
    vectors = vectors[:, :9].astype(f32)
    bias_up = vectors[:, 8, : up_bias.shape[0]].reshape(1, -1)
    (vectors,) = fence(vectors[:, :8, :rows].transpose(1, 0, 2).reshape(8, width))
    (
        gain_one,
        shift_one,
        bias_query,
        bias_value,
        bias_out,
        gain_two,
        shift_two,
        bias_down,
    ) = (vectors[i : i + 1] for i in range(8))
    normed_one = (unit_one * gain_one + shift_one).astype(bf16)
    bias_project = jnp.concatenate([bias_query, jnp.zeros_like(bias_query), bias_value], 1)
    project = project_forward(normed_one, qkv_full, bias_project)
    second.quads, second.got, third.held, third.got, project = fence(
        second.quads, second.got, third.held, third.got, project
    )

    second.plane_two()
    third.near()
    cot_parts = cotangent.reshape(2, 2, local_rows, width)
    cot_sent, cot_own = pick(cot_parts, 1 - side), pick(cot_parts, side)
    mixed, probs = attend(labels, project)
    second.held, second.got, third.held, third.got, mixed, cot_sent, cot_own = fence(
        second.held, second.got, third.held, third.got, mixed, cot_sent, cot_own
    )

    second.cores()
    cot_got = swap(cot_sent, X)
    third.line_end()
    second.parts, third.held, third.got, mixed, cot_got, cot_own = fence(
        second.parts, third.held, third.got, mixed, cot_got, cot_own
    )

    third.plane()
    cot_parts = jnp.stack([cot_own, cot_got], 1)
    cot_kept, cot_got = pick(cot_parts, core), swap(pick(cot_parts, 1 - core), CORE)
    cot_low = to_micro_end(cot_kept, cot_got)
    second.parts = [in_hbm(part) for part in second.parts]
    out_full, up_full = restore(second, cuts_of((width, inner)), me)
    out_full, up_full = out_full.reshape(width, width), up_full.reshape(width, inner)
    resid_mid = resid_in + jnp.dot(mixed, out_full, preferred_element_type=f32) + bias_out
    unit_two, _ = norm_parts(resid_mid)
    normed_two = (unit_two * gain_two + shift_two).astype(bf16)
    hidden, slope = up_forward(normed_two, up_full, bias_up)
    deep = inner // DEVICES
    down_sum = Scatter(
        parts_call(
            third_parts_kernel, [hidden, cot_low], deep, width, (4 * deep, width), 16, me
        )
    )
    third.held, third.got, down_sum.kept, down_sum.sent, hidden, cot_low = fence(
        third.held, third.got, down_sum.kept, down_sum.sent, hidden, cot_low
    )

    third.cores()
    down_sum.cores()
    third.parts, down_sum.kept, down_sum.got, hidden, cot_low = fence(
        third.parts, down_sum.kept, down_sum.got, hidden, cot_low
    )

    down_sum.plane_one()
    (down_full,) = restore(third, cuts_of((width,)), me, False)
    down_full = down_full.reshape(inner, width)
    grad_pre, grad_bias_up = pre_back(cot_low, down_full, slope)
    grad_mid, branch_low, grad_mixed, sums_two = middle_back(
        grad_pre, up_full, resid_mid, gain_two, cot_low, out_full
    )
    (
        down_sum.kept,
        down_sum.got,
        grad_mid,
        branch_low,
        grad_mixed,
        grad_pre,
        down_full,
        hidden,
    ) = fence(
        down_sum.kept,
        down_sum.got,
        grad_mid,
        branch_low,
        grad_mixed,
        grad_pre,
        down_full,
        hidden,
    )
    down_sum.plane_two()
    up_sum = Scatter(
        parts_call(
            second_parts_kernel,
            [mixed, branch_low, normed_two, grad_pre],
            rows,
            width + inner,
            (width, width),
            20,
            me,
        )
    )
    down_sum.kept, down_sum.got, up_sum.kept, up_sum.sent, grad_mixed, hidden, down_full = fence(
        down_sum.kept, down_sum.got, up_sum.kept, up_sum.sent, grad_mixed, hidden, down_full
    )

    up_sum.cores()
    down_sum.plane_end()
    result = resid_mid + jnp.dot(hidden, down_full, preferred_element_type=f32) + bias_down
    result = result.astype(bf16)
    down_sum.kept, down_sum.got, up_sum.kept, up_sum.got, grad_mixed, result = fence(
        down_sum.kept, down_sum.got, up_sum.kept, up_sum.got, grad_mixed, result
    )

    up_sum.plane_one()
    down_sum.near()
    out_kept, out_got = from_micro_c(result)
    grad_query, grad_key, grad_value = attend_back(project, probs, grad_mixed)
    (
        down_sum.kept,
        down_sum.got,
        up_sum.kept,
        up_sum.got,
        grad_query,
        grad_key,
        grad_value,
        out_kept,
        out_got,
    ) = fence(
        down_sum.kept,
        down_sum.got,
        up_sum.kept,
        up_sum.got,
        grad_query,
        grad_key,
        grad_value,
        out_kept,
        out_got,
    )
    up_sum.plane_two()
    down_sum.far()
    in_grad, sums_one = first_back(
        grad_query, grad_key, grad_value, qkv_full, tokens, gain_one, grad_mid
    )
    qkv_sum = Scatter(
        parts_call(
            first_parts_kernel,
            [
                normed_one,
                grad_query,
                grad_key,
                grad_value,
                sums_one,
                sums_two,
                grad_bias_up,
            ],
            rows,
            wide + 128,
            (width, width),
            16,
            me,
        )
    )
    (
        down_sum.kept,
        down_sum.got,
        up_sum.kept,
        up_sum.got,
        qkv_sum.kept,
        qkv_sum.sent,
        in_grad,
        out_kept,
        out_got,
    ) = fence(
        down_sum.kept,
        down_sum.got,
        up_sum.kept,
        up_sum.got,
        qkv_sum.kept,
        qkv_sum.sent,
        in_grad,
        out_kept,
        out_got,
    )

    up_sum.plane_end()
    qkv_sum.cores()
    in_kept, in_got = from_micro_c(in_grad)
    out_kept, out_sent = from_micro_pick(out_kept, out_got, core)
    (
        up_sum.kept,
        up_sum.got,
        qkv_sum.kept,
        qkv_sum.got,
        in_kept,
        in_got,
        out_kept,
        out_sent,
    ) = fence(
        up_sum.kept,
        up_sum.got,
        qkv_sum.kept,
        qkv_sum.got,
        in_kept,
        in_got,
        out_kept,
        out_sent,
    )

    qkv_sum.plane_one()
    up_sum.near()
    in_kept, in_sent = from_micro_pick(in_kept, in_got, core)
    (
        qkv_sum.kept,
        qkv_sum.got,
        up_sum.kept,
        up_sum.got,
        in_kept,
        in_sent,
        out_kept,
        out_sent,
        down_sum.kept,
        down_sum.got,
    ) = fence(
        qkv_sum.kept,
        qkv_sum.got,
        up_sum.kept,
        up_sum.got,
        in_kept,
        in_sent,
        out_kept,
        out_sent,
        down_sum.kept,
        down_sum.got,
    )
    qkv_sum.plane_two()
    up_sum.far()
    out_got = swap(out_sent, X)
    (
        qkv_sum.kept,
        qkv_sum.got,
        up_sum.kept,
        up_sum.got,
        in_kept,
        in_sent,
        out_kept,
        out_got,
    ) = fence(
        qkv_sum.kept,
        qkv_sum.got,
        up_sum.kept,
        up_sum.got,
        in_kept,
        in_sent,
        out_kept,
        out_got,
    )

    in_got = swap(in_sent, X)
    qkv_sum.plane_end()
    qkv_sum.line()
    grad_out, grad_up = finish(up_sum, (width, inner))
    (grad_down,) = finish(down_sum, (width,))
    output = from_micro_end(out_kept, out_got, side)
    in_grad = from_micro_end(in_kept, in_got, side).astype(f32)
    qkv_sum.kept, qkv_sum.got, output, grad_out, grad_up, grad_down = fence(
        qkv_sum.kept, qkv_sum.got, output, grad_out, grad_up, grad_down
    )

    grad_qkv, sums = finish(qkv_sum, (wide, 128))
    deep, sums = sums[8, :deep], sums[:8, :rows]
    return (
        output,
        in_grad,
        sums[0],
        sums[1],
        grad_qkv,
        sums[2],
        sums[3],
        grad_out,
        sums[4],
        sums[5],
        sums[6],
        grad_up,
        deep,
        grad_down,
        sums[7],
    )


def solution(mesh):
    placed = (
        P(None, ("dp", "fsdp"), None),
        P(None, "dp"),
        P(("dp", "fsdp")),
        P(("dp", "fsdp")),
        P(("dp", "fsdp"), None),
        P(("dp", "fsdp")),
        P(("dp", "fsdp")),
        P(("dp", "fsdp"), None),
        P(("dp", "fsdp")),
        P(("dp", "fsdp")),
        P(("dp", "fsdp")),
        P(("dp", "fsdp"), None),
        P(("dp", "fsdp")),
        P(("dp", "fsdp"), None),
        P(("dp", "fsdp")),
        P(None, ("dp", "fsdp"), None),
    )
    fits = mesh.shape["dp"] == 8 and mesh.shape["fsdp"] == 4
    return jax.shard_map(
        on_device_fast if fits else on_device_general,
        mesh=mesh,
        in_specs=placed,
        out_specs=(
            P(None, ("dp", "fsdp"), None),
            P(None, ("dp", "fsdp"), None),
            P(("dp", "fsdp")),
            P(("dp", "fsdp")),
            P(("dp", "fsdp"), None),
            P(("dp", "fsdp")),
            P(("dp", "fsdp")),
            P(("dp", "fsdp"), None),
            P(("dp", "fsdp")),
            P(("dp", "fsdp")),
            P(("dp", "fsdp")),
            P(("dp", "fsdp"), None),
            P(("dp", "fsdp")),
            P(("dp", "fsdp"), None),
            P(("dp", "fsdp")),
        ),
        check_vma=False,
    )
```

```python
import functools
import math

import jax
import jax.numpy as jnp
from jax import lax
from jax.experimental import pallas as pl
from jax.experimental.pallas import tpu as pltpu
from jax.sharding import PartitionSpec as P

HEADS = 12


EPSILON = 1e-06
NEG_LARGE = -1e30
SCALE_SCORE = 0.125


def layer_norm(values, gain_vec, shift_vec):
    centre = values - jnp.mean(values, -1, keepdims=True)
    spread = jnp.mean(centre * centre, -1, keepdims=True)
    return centre * lax.rsqrt(spread + EPSILON) * gain_vec + shift_vec


def gelu_tanh(values):
    return (
        0.5
        * values
        * (1.0 + jnp.tanh(0.7978845608028654 * (values + 0.044715 * values * values * values)))
    )


def add_terms(first_terms, second_terms):
    if first_terms is None:
        return second_terms
    return jax.tree.map(jnp.add, first_terms, second_terms)


def on_device_general(
    inputs,
    segments,
    norm1_gain,
    norm1_bias,
    qkv_weight,
    query_bias,
    value_bias,
    out_weight,
    out_bias,
    norm2_gain,
    norm2_bias,
    up_weight,
    up_bias,
    down_weight,
    down_bias,
    cotangent,
):
    micro_count = inputs.shape[0]
    local_rows = inputs.shape[1]
    model_width = inputs.shape[2]
    group_rows = segments.shape[1]
    key_rows = math.gcd(512, group_rows)
    key_count = group_rows // key_rows
    offset = lax.axis_index("fsdp") * local_rows
    f32 = jnp.float32
    bf16 = jnp.bfloat16
    outputs = []
    in_grads = []
    totals = None
    for micro_index in range(micro_count):
        params_fwd = (
            lax.all_gather(norm1_gain, ("dp", "fsdp"), axis=0, tiled=True),
            lax.all_gather(norm1_bias, ("dp", "fsdp"), axis=0, tiled=True),
            lax.all_gather(qkv_weight, ("dp", "fsdp"), axis=0, tiled=True),
            lax.all_gather(query_bias, ("dp", "fsdp"), axis=0, tiled=True),
            lax.all_gather(value_bias, ("dp", "fsdp"), axis=0, tiled=True),
            lax.all_gather(out_weight, ("dp", "fsdp"), axis=0, tiled=True),
            lax.all_gather(out_bias, ("dp", "fsdp"), axis=0, tiled=True),
            lax.all_gather(norm2_gain, ("dp", "fsdp"), axis=0, tiled=True),
            lax.all_gather(norm2_bias, ("dp", "fsdp"), axis=0, tiled=True),
            lax.all_gather(up_weight, ("dp", "fsdp"), axis=0, tiled=True),
            lax.all_gather(up_bias, ("dp", "fsdp"), axis=0, tiled=True),
            lax.all_gather(down_weight, ("dp", "fsdp"), axis=0, tiled=True),
            lax.all_gather(down_bias, ("dp", "fsdp"), axis=0, tiled=True),
        )
        (
            gain_one,
            shift_one,
            qkv_full,
            bias_query,
            bias_value,
            out_full,
            bias_out,
            gain_two,
            shift_two,
            up_full,
            bias_up,
            down_full,
            bias_down,
        ) = params_fwd
        resid_in = inputs[micro_index].astype(f32)
        normed_one = layer_norm(resid_in, gain_one.astype(f32), shift_one.astype(f32)).astype(bf16)
        project = jnp.dot(normed_one, qkv_full, preferred_element_type=f32)
        queries = (project[:, :model_width] + bias_query.astype(f32)).astype(bf16)
        keys_local = project[:, model_width : 2 * model_width].astype(bf16)
        values_local = (project[:, 2 * model_width :] + bias_value.astype(f32)).astype(bf16)
        keys_all, values_all = (
            lax.all_gather(keys_local, "fsdp", axis=0, tiled=True),
            lax.all_gather(values_local, "fsdp", axis=0, tiled=True),
        )
        labels_all = segments[micro_index]
        labels_query = lax.dynamic_slice_in_dim(labels_all, offset, local_rows)
        query_heads = queries.reshape(local_rows, HEADS, -1)
        key_blocks = keys_all.reshape(key_count, key_rows, HEADS, -1)
        value_blocks = values_all.reshape(key_count, key_rows, HEADS, -1)
        label_blocks = labels_all.reshape(key_count, key_rows)

        def block_scores(key_block, label_block):
            scores = (
                jnp.einsum("qhd,khd->hqk", query_heads, key_block, preferred_element_type=f32)
                * SCALE_SCORE
            )
            allowed = (labels_query[:, None] == label_block[None, :])[None]
            return (jnp.where(allowed, scores, NEG_LARGE), allowed)

        def stat_step(state_in, pieces):
            running_max, running_sum = state_in
            scores, allowed = block_scores(pieces[0], pieces[1])
            newmax = jnp.maximum(running_max, jnp.max(scores, -1))
            exponent = jnp.where(allowed, jnp.exp(scores - newmax[..., None]), 0.0)
            running_sum = running_sum * jnp.exp(running_max - newmax) + jnp.sum(exponent, -1)
            return ((newmax, running_sum), None)

        start_state = (
            jnp.full((HEADS, local_rows), NEG_LARGE, f32),
            jnp.zeros((HEADS, local_rows), f32),
        )
        (final_max, final_sum), _ = lax.scan(stat_step, start_state, (key_blocks, label_blocks))
        log_total = final_max + jnp.log(final_sum)

        def block_prob(key_block, label_block):
            scores, allowed = block_scores(key_block, label_block)
            attend_prob = jnp.where(allowed, jnp.exp(scores - log_total[..., None]), 0.0)
            return (attend_prob, attend_prob.astype(bf16))

        def mix_step(state_in, pieces):
            mixed_acc, extra_acc = state_in
            attend_prob, prob_low = block_prob(pieces[0], pieces[2])
            remainder = (attend_prob - prob_low.astype(f32)).astype(bf16)
            mixed_acc = mixed_acc + jnp.einsum(
                "hqk,khd->qhd", prob_low, pieces[1], preferred_element_type=f32
            )
            extra_acc = extra_acc + jnp.einsum(
                "hqk,khd->qhd", remainder, pieces[1], preferred_element_type=f32
            )
            return ((mixed_acc, extra_acc), None)

        zero_heads = jnp.zeros(query_heads.shape, f32)
        (mixed_heads, extra_heads), _ = lax.scan(
            mix_step, (zero_heads, zero_heads), (key_blocks, value_blocks, label_blocks)
        )
        mixed_low = mixed_heads.reshape(local_rows, model_width).astype(bf16)
        full_mix = mixed_heads + extra_heads
        resid_mid = (
            resid_in
            + jnp.dot(mixed_low, out_full, preferred_element_type=f32)
            + bias_out.astype(f32)
        )
        normed_two = layer_norm(resid_mid, gain_two.astype(f32), shift_two.astype(f32)).astype(bf16)
        pre_act = jnp.dot(normed_two, up_full, preferred_element_type=f32) + bias_up.astype(f32)
        hidden_low = gelu_tanh(pre_act).astype(bf16)
        result = (
            resid_mid
            + jnp.dot(hidden_low, down_full, preferred_element_type=f32)
            + bias_down.astype(f32)
        )
        outputs.append(result.astype(bf16))
        params_bwd = (
            lax.all_gather(norm1_gain, ("dp", "fsdp"), axis=0, tiled=True),
            lax.all_gather(norm1_bias, ("dp", "fsdp"), axis=0, tiled=True),
            lax.all_gather(qkv_weight, ("dp", "fsdp"), axis=0, tiled=True),
            lax.all_gather(query_bias, ("dp", "fsdp"), axis=0, tiled=True),
            lax.all_gather(value_bias, ("dp", "fsdp"), axis=0, tiled=True),
            lax.all_gather(out_weight, ("dp", "fsdp"), axis=0, tiled=True),
            lax.all_gather(out_bias, ("dp", "fsdp"), axis=0, tiled=True),
            lax.all_gather(norm2_gain, ("dp", "fsdp"), axis=0, tiled=True),
            lax.all_gather(norm2_bias, ("dp", "fsdp"), axis=0, tiled=True),
            lax.all_gather(up_weight, ("dp", "fsdp"), axis=0, tiled=True),
            lax.all_gather(up_bias, ("dp", "fsdp"), axis=0, tiled=True),
            lax.all_gather(down_weight, ("dp", "fsdp"), axis=0, tiled=True),
            lax.all_gather(down_bias, ("dp", "fsdp"), axis=0, tiled=True),
        )
        (
            gain_one_b,
            shift_one_b,
            qkv_back,
            bias_query_b,
            bias_value_b,
            out_back,
            bias_out_b,
            gain_two_b,
            shift_two_b,
            up_back,
            bias_up_b,
            down_back,
            bias_down_b,
        ) = params_bwd
        cot_low = cotangent[micro_index]
        cot_full = cot_low.astype(f32)
        grad_down = jnp.einsum("tf,td->fd", hidden_low, cot_low, preferred_element_type=f32)
        grad_bias_down = jnp.sum(cot_full, 0)
        grad_hidden = jnp.einsum("td,fd->tf", cot_low, down_back, preferred_element_type=f32)
        _, gelu_pull = jax.vjp(gelu_tanh, pre_act)
        grad_pre = gelu_pull(grad_hidden)[0].astype(bf16)
        grad_up = jnp.einsum("td,tf->df", normed_two, grad_pre, preferred_element_type=f32)
        grad_bias_up = jnp.sum(grad_pre.astype(f32), 0)
        grad_normed_two = jnp.einsum("tf,df->td", grad_pre, up_back, preferred_element_type=f32)
        _, norm_two_pull = jax.vjp(
            layer_norm, resid_mid, gain_two_b.astype(f32), shift_two_b.astype(f32)
        )
        grad_mid_part, grad_gain_two, grad_shift_two = norm_two_pull(grad_normed_two)
        grad_mid = cot_full + grad_mid_part
        branch_low = grad_mid.astype(bf16)
        grad_out = jnp.einsum("td,te->de", mixed_low, branch_low, preferred_element_type=f32)
        grad_bias_out = jnp.sum(branch_low.astype(f32), 0)
        grad_mixed = jnp.einsum(
            "te,de->td", branch_low, out_back, preferred_element_type=f32
        ).astype(bf16)
        grad_heads = grad_mixed.reshape(local_rows, HEADS, -1)
        delta = jnp.einsum("qhd,qhd->hq", grad_heads.astype(f32), full_mix)

        def grad_step(query_acc, pieces):
            key_block, value_block, label_block = pieces
            attend_prob, prob_low = block_prob(key_block, label_block)
            grad_prob = jnp.einsum(
                "qhd,khd->hqk", grad_heads, value_block, preferred_element_type=f32
            )
            grad_scores = (attend_prob * (grad_prob - delta[..., None]) * SCALE_SCORE).astype(bf16)
            query_acc = query_acc + jnp.einsum(
                "hqk,khd->qhd", grad_scores, key_block, preferred_element_type=f32
            )
            key_part = jnp.einsum(
                "hqk,qhd->khd", grad_scores, query_heads, preferred_element_type=f32
            )
            value_part = jnp.einsum(
                "hqk,qhd->khd", prob_low, grad_heads, preferred_element_type=f32
            )
            return (query_acc, (key_part, value_part))

        query_grad, (key_parts, value_parts) = lax.scan(
            grad_step, zero_heads, (key_blocks, value_blocks, label_blocks)
        )
        key_parts = key_parts.reshape(group_rows, model_width)
        value_parts = value_parts.reshape(group_rows, model_width)
        key_grad, value_grad = (
            lax.psum_scatter(
                key_parts.astype(jnp.bfloat16), "fsdp", scatter_dimension=0, tiled=True
            ).astype(jnp.float32),
            lax.psum_scatter(
                value_parts.astype(jnp.bfloat16), "fsdp", scatter_dimension=0, tiled=True
            ).astype(jnp.float32),
        )
        query_low = query_grad.reshape(local_rows, model_width).astype(bf16)
        key_low = key_grad.astype(bf16)
        value_low = value_grad.astype(bf16)
        grad_project = jnp.concatenate([query_low, key_low, value_low], 1)
        grad_qkv = jnp.einsum("td,te->de", normed_one, grad_project, preferred_element_type=f32)
        grad_bias_query = jnp.sum(query_low.astype(f32), 0)
        grad_bias_value = jnp.sum(value_low.astype(f32), 0)
        grad_normed_one = jnp.einsum(
            "te,de->td", grad_project, qkv_back, preferred_element_type=f32
        )
        _, norm_one_pull = jax.vjp(
            layer_norm, resid_in, gain_one_b.astype(f32), shift_one_b.astype(f32)
        )
        grad_in_part, grad_gain_one, grad_shift_one = norm_one_pull(grad_normed_one)
        in_grads.append(grad_mid + grad_in_part)
        local_terms = (
            grad_gain_one,
            grad_shift_one,
            grad_qkv,
            grad_bias_query,
            grad_bias_value,
            grad_out,
            grad_bias_out,
            grad_gain_two,
            grad_shift_two,
            grad_up,
            grad_bias_up,
            grad_down,
            grad_bias_down,
        )
        shard_terms = (
            lax.psum_scatter(local_terms[0], ("dp", "fsdp"), scatter_dimension=0, tiled=True),
            lax.psum_scatter(local_terms[1], ("dp", "fsdp"), scatter_dimension=0, tiled=True),
            lax.psum_scatter(local_terms[2], ("dp", "fsdp"), scatter_dimension=0, tiled=True),
            lax.psum_scatter(local_terms[3], ("dp", "fsdp"), scatter_dimension=0, tiled=True),
            lax.psum_scatter(local_terms[4], ("dp", "fsdp"), scatter_dimension=0, tiled=True),
            lax.psum_scatter(local_terms[5], ("dp", "fsdp"), scatter_dimension=0, tiled=True),
            lax.psum_scatter(local_terms[6], ("dp", "fsdp"), scatter_dimension=0, tiled=True),
            lax.psum_scatter(local_terms[7], ("dp", "fsdp"), scatter_dimension=0, tiled=True),
            lax.psum_scatter(local_terms[8], ("dp", "fsdp"), scatter_dimension=0, tiled=True),
            lax.psum_scatter(local_terms[9], ("dp", "fsdp"), scatter_dimension=0, tiled=True),
            lax.psum_scatter(local_terms[10], ("dp", "fsdp"), scatter_dimension=0, tiled=True),
            lax.psum_scatter(local_terms[11], ("dp", "fsdp"), scatter_dimension=0, tiled=True),
            lax.psum_scatter(local_terms[12], ("dp", "fsdp"), scatter_dimension=0, tiled=True),
        )
        totals = add_terms(totals, shard_terms)
    return (
        jnp.stack(outputs),
        jnp.stack(in_grads),
        totals[0],
        totals[1],
        totals[2],
        totals[3],
        totals[4],
        totals[5],
        totals[6],
        totals[7],
        totals[8],
        totals[9],
        totals[10],
        totals[11],
        totals[12],
    )


AXES = ("dp", "fsdp")
CORE, X, Y, Z0, Z1 = 1, 2, 4, 8, 16
LINE = (0, Z1, Z0, Z1 ^ Z0)
PLANE = (0, X, Y, X ^ Y)
DEVICES = 32
MIB = 1024 * 1024
SMALL = pl.CostEstimate(flops=1024, transcendentals=0, bytes_accessed=1024)


def swap(values, mask):
    pairs = [(i, i ^ mask) for i in range(DEVICES)]
    return lax.ppermute(values, AXES, pairs)


SLOTS = [core ^ plane ^ line for core in (0, CORE) for plane in PLANE for line in LINE]


def fence(*values):
    return lax.optimization_barrier(values)


def join(*parts):
    return lax.optimization_barrier(jnp.concatenate(parts, 0))


def halves_of(width):
    half = width // 256 * 128
    return ((0, half), (half, width))


class Gather:
    def __init__(self, shard):
        self.held = shard[None]
        self.across = []

    def line(self):
        self.got = [swap(self.held, mask) for mask in LINE[1:]]

    def far(self):
        self.got = [swap(self.held, Z1)]

    def near(self):
        self.held = join(self.held, *self.got)
        self.got = [swap(self.held, Z0)]

    def line_end(self):
        self.held, self.got = join(self.held, *self.got), []

    def plane(self):
        self.held = join(self.held, *self.got) if self.got else self.held
        self.got = [swap(self.held, mask) for mask in PLANE[1:]]

    def plane_one(self):
        self.held = join(self.held, *self.got)
        self.quads = [self.held[..., low:high] for low, high in halves_of(self.held.shape[2])]
        self.got = [swap(quad, bit) for quad, bit in zip(self.quads, (X, Y))]

    def plane_two(self):
        own = [one for pair in zip(self.quads, self.got) for one in pair]
        bits = (Y, Y, X, X)
        self.held, self.got = own[0], own[1:] + [swap(one, bit) for one, bit in zip(own, bits)]

    def cores(self):
        own = [self.held, *self.got]
        self.parts = own + [swap(piece, CORE) for piece in own]

    def places(self):
        width = self.held.shape[2]
        if len(self.got) == 3:
            masks = [core ^ plane ^ line for core in (0, CORE) for plane in PLANE for line in LINE]
            return [(i // 4, i % 4, mask, 0, width) for i, mask in enumerate(masks)]
        spans = ((0, width), (width, width + self.got[2].shape[2]))
        return [
            (8 * core + 4 * second + 2 * half + first, i, mask, low, high)
            for core in (0, CORE)
            for half, ((low, high), bits) in enumerate(zip(spans, ((X, Y), (Y, X))))
            for second in (0, 1)
            for first in (0, 1)
            for i, line in enumerate(LINE)
            for mask in (core ^ line ^ bits[0] * first ^ bits[1] * second,)
        ]


def sum_low(*terms):
    total = sum(term.astype(jnp.float32) for term in terms)
    return total.astype(jnp.bfloat16)


class Scatter:
    places = [
        [
            (slot // 16, slot % 16, core ^ plane ^ line)
            for slot, (core, plane, line) in enumerate(
                (core, plane, line) for core in (0, CORE) for plane in planes for line in LINE
            )
        ]
        for planes in ((0, X, Y, X ^ Y), (0, Y, X, X ^ Y))
    ]

    def __init__(self, halves):
        self.kept, self.sent = halves

    def cores(self):
        self.got = swap(self.sent, CORE)

    def line(self):
        terms = [self.kept, *self.got]
        ones = [sum_low(*(term[i : i + 1] for term in terms)) for i in range(1, 4)]
        self.kept = sum(term[0].astype(jnp.float32) for term in terms)
        self.got = [swap(one, mask) for one, mask in zip(ones, LINE[1:])]

    def plane_one(self, more=None):
        kept, sent = [], []
        for low, high in halves_of(self.kept.shape[2]):
            pairs = [(one[..., low:high]) for one in (self.kept, self.got)]
            if more and low:
                pairs = [
                    jnp.concatenate(pair, -1) for pair in zip(pairs, (more.kept, more.got))
                ]
            kept.append(sum_low(*(one[:8] for one in pairs)))
            sent.append(sum_low(*(one[8:] for one in pairs)))
        self.kept, self.got = kept, [swap(one, bit) for one, bit in zip(sent, (Y, X))]

    def plane_two(self):
        sent = [
            swap(sum_low(kept[4:], got[4:]), bit)
            for kept, got, bit in zip(self.kept, self.got, (X, Y))
        ]
        kept = [sum_low(kept[:4], got[:4]) for kept, got in zip(self.kept, self.got)]
        self.kept, self.got = jnp.concatenate(kept, -1), sent

    def plane_end(self):
        self.got = [jnp.concatenate(self.got, -1)]

    def near(self):
        terms = [self.kept, *self.got]
        self.kept = sum_low(*(term[:2] for term in terms))
        self.got = [swap(sum_low(*(term[2:] for term in terms)), Z0)]

    def far(self):
        got = self.got[0]
        self.got = [swap(sum_low(self.kept[1:], got[1:]), Z1)]
        self.kept = self.kept[0].astype(jnp.float32) + got[0].astype(jnp.float32)

    def total(self):
        return self.kept + sum(got[0].astype(jnp.float32) for got in self.got)


def cuts_of(parts):
    ends = [sum(parts[: i + 1]) for i in range(len(parts))]
    return tuple((end - part, end) for end, part in zip(ends, parts))


def shuffle_kernel(moves, count, me_ref, *refs):
    me = me_ref[0]

    def part(slot):
        return pl.ds(lax.bitwise_xor(me, slot[0]) if isinstance(slot, tuple) else slot, 1)

    for source, source_slot, source_low, target, target_slot, target_low, width in moves:
        refs[count + target][part(target_slot), :, target_low : target_low + width] = refs[source][
            part(source_slot), :, source_low : source_low + width
        ]


def whole_block(shape):
    return pl.BlockSpec(shape, lambda i: (0,) * len(shape), pipeline_mode=pl.Buffered(1))


def shuffle(arrays, shapes, moves, me, pinned):
    dtype = arrays[0].dtype
    size = sum(math.prod(shape) for shape in shapes)
    make = pltpu.HBM if pinned else jax.ShapeDtypeStruct
    return pl.pallas_call(
        functools.partial(shuffle_kernel, moves, len(arrays)),
        grid=(1,),
        out_shape=[make(shape, dtype) for shape in shapes],
        in_specs=[pl.BlockSpec(memory_space=pltpu.SMEM)]
        + [whole_block(array.shape) for array in arrays],
        out_specs=[whole_block(shape) for shape in shapes],
        compiler_params=pltpu.CompilerParams(vmem_limit_bytes=16 * MIB),
        cost_estimate=SMALL,
    )(me, *arrays)


def restore(gather, cuts, me, pinned=True):
    moves = []
    for part, slot, mask, low, high in gather.places():
        for target, (begin, end) in enumerate(cuts):
            left, right = max(low, begin), min(high, end)
            if left < right:
                moves.append(
                    (part, slot, left - low, target, (mask,), left - begin, right - left)
                )
    rows = gather.parts[0].shape[1]
    shapes = [(DEVICES, rows, end - begin) for begin, end in cuts]
    return shuffle(gather.parts, shapes, moves, me, pinned)


TN = (((0,), (0,)), ((), ()))


def finish_kernel(cuts, *refs):
    kept_ref, got_refs, outs = refs[0], refs[1 : -len(cuts)], refs[-len(cuts) :]
    for out_ref, (begin, end) in zip(outs, cuts):
        total = kept_ref[:, begin:end]
        for ref in got_refs:
            total = total + ref[0, :, begin:end].astype(jnp.float32)
        out_ref[...] = total


def finish(scatter, parts):
    inputs = [scatter.kept, *scatter.got]
    shapes = [(scatter.kept.shape[0], part) for part in parts]
    return pl.pallas_call(
        functools.partial(finish_kernel, cuts_of(parts)),
        grid=(1,),
        out_shape=[jax.ShapeDtypeStruct(shape, jnp.float32) for shape in shapes],
        in_specs=[whole_block(value.shape) for value in inputs],
        out_specs=[whole_block(shape) for shape in shapes],
        compiler_params=pltpu.CompilerParams(vmem_limit_bytes=8 * MIB),
        cost_estimate=SMALL,
    )(*inputs)


def parts_call(kernel, inputs, rows, width, scratch, limit, me):
    half = (DEVICES // 2, rows, width)
    return pl.pallas_call(
        kernel,
        grid=(1,),
        out_shape=[jax.ShapeDtypeStruct(half, jnp.bfloat16)] * 2,
        in_specs=[pl.BlockSpec(memory_space=pltpu.SMEM)]
        + [whole_block(value.shape) for value in inputs],
        out_specs=[whole_block(half)] * 2,
        scratch_shapes=[pltpu.VMEM(scratch, jnp.float32)],
        compiler_params=pltpu.CompilerParams(vmem_limit_bytes=limit * MIB),
        cost_estimate=SMALL,
    )(me, *inputs)


def store_rows(me, sum_ref, outs, low, high):
    rows = sum_ref.shape[0] // DEVICES
    for places, (begin, end) in zip(Scatter.places, halves_of(outs[0].shape[2])):
        left, right = max(low, begin), min(high, end)
        if left < right:
            for half, slot, mask in places:
                first = pl.multiple_of(lax.bitwise_xor(me, mask) * rows, rows)
                outs[half][slot, :, left:right] = sum_ref[
                    pl.ds(first, rows), left - low : right - low
                ].astype(jnp.bfloat16)


def multiply_rows(me, left_ref, right_refs, sum_ref, outs, low):
    width = sum_ref.shape[1]
    for ref in right_refs:
        for begin in range(0, ref.shape[1], width):
            sum_ref[...] = lax.dot_general(
                left_ref[...],
                ref[:, begin : begin + width],
                TN,
                preferred_element_type=jnp.float32,
            )
            store_rows(me, sum_ref, outs, low + begin, low + begin + width)
        low += ref.shape[1]
    return low


def second_parts_kernel(
    me_ref, mixed_ref, branch_ref, normed_ref, pre_ref, kept_ref, sent_ref, sum_ref
):
    me, outs = me_ref[0], (kept_ref, sent_ref)
    low = multiply_rows(me, mixed_ref, [branch_ref], sum_ref, outs, 0)
    multiply_rows(me, normed_ref, [pre_ref], sum_ref, outs, low)


def first_parts_kernel(
    me_ref, normed_ref, query_ref, key_ref, value_ref, kept_ref, sent_ref, sum_ref
):
    rights = [query_ref, key_ref, value_ref]
    multiply_rows(me_ref[0], normed_ref, rights, sum_ref, (kept_ref, sent_ref), 0)


def vector_parts_kernel(me_ref, one_ref, two_ref, bias_ref, kept_ref, sent_ref, sum_ref):
    me, outs, low = me_ref[0], (kept_ref, sent_ref), 0
    rows = kept_ref.shape[1]
    vectors = jnp.concatenate([one_ref[:4], two_ref[:4]], 0)
    width, bias = vectors.shape[1], jnp.broadcast_to(bias_ref[...], (8, bias_ref.shape[1]))
    deep = bias.shape[1] // DEVICES
    spare = jnp.zeros((rows - 16, 128), jnp.float32)
    for half, slot, mask in Scatter.places[1]:
        owner = lax.bitwise_xor(me, mask)
        here = pltpu.roll(vectors, lax.rem(width - rows * owner, width), 1)[:, :128]
        bias_here = pltpu.roll(bias, lax.rem(DEVICES * deep - deep * owner, DEVICES * deep), 1)
        outs[half][slot, :, low:] = jnp.concatenate(
            [here, bias_here[:, :128], spare], 0
        ).astype(jnp.bfloat16)


def third_parts_kernel(me_ref, hidden_ref, cot_ref, kept_ref, sent_ref, sum_ref):
    me, outs = me_ref[0], (kept_ref, sent_ref)
    rows = kept_ref.shape[1]
    for block in range(DEVICES // 4):
        first = pl.multiple_of(lax.bitwise_xor(me // 4, block) * (4 * rows), 4 * rows)
        sum_ref[...] = lax.dot_general(
            hidden_ref[:, pl.ds(first, 4 * rows)],
            cot_ref[...],
            TN,
            preferred_element_type=jnp.float32,
        )
        for places, (low, high) in zip(Scatter.places, halves_of(cot_ref.shape[1])):
            for half, slot, mask in places:
                if mask // 4 == block:
                    first = pl.multiple_of(lax.bitwise_xor(me % 4, mask % 4) * rows, rows)
                    outs[half][slot, :, low:high] = sum_ref[pl.ds(first, rows), low:high].astype(
                        jnp.bfloat16
                    )


NT = (((1,), (1,)), ((), ()))


def make_mask(labels_ref, mask_ref):
    @pl.when(pl.program_id(0) == 0)
    def _():
        across = labels_ref[...].astype(jnp.float32)
        down = jnp.broadcast_to(across, (8, across.shape[1])).T[:, :1]
        allowed = down == across
        mask_ref[...] = jnp.where(allowed, 0.0, NEG_LARGE)


def head_probs(keys, queries, head, mask_ref):
    f32 = jnp.float32
    lane = lax.broadcasted_iota(jnp.int32, queries.shape, 1)
    own = (lane // 64) == head
    chosen = jnp.where(own, queries.astype(f32) * SCALE_SCORE, 0.0).astype(jnp.bfloat16)
    scores = lax.dot_general(keys, chosen, NT, preferred_element_type=f32) + mask_ref[...]
    exponent = jnp.exp(scores - jnp.max(scores, 0, keepdims=True))
    return exponent * (1.0 / jnp.sum(exponent, 0, keepdims=True))


def attend_kernel(row_ref, query_ref, key_ref, value_ref, out_ref, prob_ref, mask_ref):
    make_mask(row_ref, mask_ref)
    keys, queries = key_ref[...], query_ref[...]
    values_across = value_ref[...].astype(jnp.float32).T.astype(jnp.bfloat16)
    mixed = []
    for head in range(2):
        prob_ref[head] = head_probs(keys, queries, head, mask_ref).astype(jnp.bfloat16)
        mixed.append(
            jnp.dot(
                values_across[64 * head : 64 * head + 64],
                prob_ref[head],
                preferred_element_type=jnp.float32,
            )
        )
    out_ref[...] = jnp.concatenate(mixed, 0).T.astype(jnp.bfloat16)


def attend_back_kernel(
    query_ref, key_ref, value_ref, prob_ref, grad_ref, dquery_ref, dkey_ref, dvalue_ref
):
    f32, bf16 = jnp.float32, jnp.bfloat16
    keys, queries, values, grads = key_ref[...], query_ref[...], value_ref[...], grad_ref[...]
    keys_across = keys.astype(f32).T.astype(bf16)
    lane = lax.broadcasted_iota(jnp.int32, keys.shape, 1)
    dquery, dkey, dvalue = [], [], []
    for head in range(2):
        chosen = jnp.where((lane // 64) == head, grads.astype(f32), 0.0).astype(bf16)
        grad_prob = lax.dot_general(values, chosen, NT, preferred_element_type=f32)
        prob = prob_ref[head].astype(f32)
        delta = jnp.sum(prob * grad_prob, 0, keepdims=True)
        grad_scores = (prob * (grad_prob - delta)).astype(bf16)
        dvalue.append(jnp.dot(prob_ref[head], grads, preferred_element_type=f32))
        dkey.append(jnp.dot(grad_scores, queries, preferred_element_type=f32))
        dquery.append(
            jnp.dot(
                keys_across[64 * head : 64 * head + 64], grad_scores, preferred_element_type=f32
            )
        )
    low_half = lane < 64
    dquery_ref[...] = (jnp.concatenate(dquery, 0).T * SCALE_SCORE).astype(bf16)
    dkey_ref[...] = (jnp.where(low_half, dkey[0], dkey[1]) * SCALE_SCORE).astype(bf16)
    dvalue_ref[...] = jnp.where(low_half, dvalue[0], dvalue[1]).astype(bf16)


def pair_specs(tokens, pairs):
    parts = [
        pl.BlockSpec((tokens, 128), lambda i, part=part: (0, i + part * pairs))
        for part in range(3)
    ]
    return parts, pl.BlockSpec((2, tokens, tokens), lambda i: (i, 0, 0))


def in_hbm(array):
    return pltpu.with_memory_space_constraint(array, pltpu.HBM)


def attend(labels, project):
    tokens, pairs = project.shape[0], HEADS // 2
    parts, probs = pair_specs(tokens, pairs)
    return pl.pallas_call(
        attend_kernel,
        grid=(pairs,),
        out_shape=[
            jax.ShapeDtypeStruct((tokens, 128 * pairs), jnp.bfloat16),
            pltpu.HBM((HEADS, tokens, tokens), jnp.bfloat16),
        ],
        in_specs=[
            pl.BlockSpec((1, tokens), lambda i: (0, 0)),
            *parts,
        ],
        out_specs=[pl.BlockSpec((tokens, 128), lambda i: (0, i)), probs],
        scratch_shapes=[pltpu.VMEM((tokens, tokens), jnp.float32)],
        compiler_params=pltpu.CompilerParams(vmem_limit_bytes=12 * MIB),
        cost_estimate=SMALL,
    )(labels.reshape(1, tokens), project, project, project)


def attend_back(project, probs, grads):
    tokens, pairs = project.shape[0], HEADS // 2
    block = pl.BlockSpec((tokens, 128), lambda i: (0, i))
    shape = jax.ShapeDtypeStruct((tokens, 128 * pairs), jnp.bfloat16)
    parts, prob_spec = pair_specs(tokens, pairs)
    return pl.pallas_call(
        attend_back_kernel,
        grid=(pairs,),
        out_shape=[shape] * 3,
        in_specs=[*parts, prob_spec, block],
        out_specs=[block] * 3,
        compiler_params=pltpu.CompilerParams(vmem_limit_bytes=14 * MIB),
        cost_estimate=SMALL,
    )(project, project, project, in_hbm(probs), grads)


def norm_parts(values):
    centre = values - jnp.mean(values, -1, keepdims=True)
    scale = lax.rsqrt(jnp.mean(centre * centre, -1, keepdims=True) + EPSILON)
    return centre * scale, scale


def norm_back(grads, values, gain_row):
    unit, scale = norm_parts(values)
    inner = grads * gain_row
    part = inner - jnp.mean(inner, -1, keepdims=True)
    part = part - unit * jnp.mean(inner * unit, -1, keepdims=True)
    gain, shift = jnp.sum(grads * unit, 0, keepdims=True), jnp.sum(grads, 0, keepdims=True)
    return part * scale, gain, shift


def column_sum(values):
    return jnp.sum(values.astype(jnp.float32), 0, keepdims=True)


def project_kernel(normed_ref, weight_ref, bias_ref, out_ref):
    for row in range(0, normed_ref.shape[0], 128):
        rows = slice(row, row + 128)
        out = jnp.dot(normed_ref[rows], weight_ref[...], preferred_element_type=jnp.float32)
        out_ref[rows] = (out + bias_ref[...]).astype(jnp.bfloat16)


def project_forward(normed, qkv_full, bias_row):
    tokens, width = normed.shape
    wide, tile = qkv_full.shape[1], 768
    return pl.pallas_call(
        project_kernel,
        grid=(wide // tile,),
        out_shape=jax.ShapeDtypeStruct((tokens, wide), jnp.bfloat16),
        in_specs=[
            pl.BlockSpec((tokens, width), lambda i: (0, 0)),
            pl.BlockSpec((width, tile), lambda i: (0, i)),
            pl.BlockSpec((1, tile), lambda i: (0, i)),
        ],
        out_specs=pl.BlockSpec((tokens, tile), lambda i: (0, i)),
        compiler_params=pltpu.CompilerParams(vmem_limit_bytes=12 * MIB),
        cost_estimate=SMALL,
    )(normed, in_hbm(qkv_full), bias_row)


def up_kernel(normed_ref, weight_ref, bias_ref, hidden_ref, slope_ref):
    bf16 = jnp.bfloat16
    first, third = 0.7978845608028654, 0.7978845608028654 * 0.044715
    for row in range(0, normed_ref.shape[0], 128):
        rows = slice(row, row + 128)
        pre = jnp.dot(normed_ref[rows], weight_ref[...], preferred_element_type=jnp.float32)
        pre = pre + bias_ref[...]
        square = pre * pre
        half = 0.5 + 0.5 * jnp.tanh(pre * (first + third * square))
        hidden_ref[rows] = (pre * half).astype(bf16)
        inner = pre * (2 * first + 6 * third * square)
        slope_ref[rows] = (half + half * inner * (1.0 - half)).astype(bf16)


def up_forward(normed, up_full, bias_row):
    tokens, width = normed.shape
    inner, tile = up_full.shape[1], 768
    block = pl.BlockSpec((tokens, tile), lambda i: (0, i))
    shape = jax.ShapeDtypeStruct((tokens, inner), jnp.bfloat16)
    return pl.pallas_call(
        up_kernel,
        grid=(inner // tile,),
        out_shape=[shape, shape],
        in_specs=[
            pl.BlockSpec((tokens, width), lambda i: (0, 0)),
            pl.BlockSpec((width, tile), lambda i: (0, i)),
            pl.BlockSpec((1, tile), lambda i: (0, i)),
        ],
        out_specs=[block, block],
        compiler_params=pltpu.CompilerParams(vmem_limit_bytes=18 * MIB),
        cost_estimate=SMALL,
    )(normed, in_hbm(up_full), bias_row)


def pre_kernel(cot_ref, weight_ref, slope_ref, pre_ref, sum_ref):
    f32 = jnp.float32
    grads = lax.dot_general(cot_ref[...], weight_ref[...], NT, preferred_element_type=f32)
    low = (grads * slope_ref[...].astype(f32)).astype(jnp.bfloat16)
    pre_ref[...] = low
    sum_ref[...] = column_sum(low)


def pre_back(cot_low, down_full, slope):
    tokens, width = cot_low.shape
    inner, tile = down_full.shape[0], 512
    block = pl.BlockSpec((tokens, tile), lambda i: (0, i))
    return pl.pallas_call(
        pre_kernel,
        grid=(inner // tile,),
        out_shape=[
            jax.ShapeDtypeStruct((tokens, inner), jnp.bfloat16),
            jax.ShapeDtypeStruct((1, inner), jnp.float32),
        ],
        in_specs=[
            pl.BlockSpec((tokens, width), lambda i: (0, 0)),
            pl.BlockSpec((tile, width), lambda i: (i, 0)),
            block,
        ],
        out_specs=[block, pl.BlockSpec((1, tile), lambda i: (0, i))],
        compiler_params=pltpu.CompilerParams(vmem_limit_bytes=12 * MIB),
        cost_estimate=SMALL,
    )(cot_low, down_full, slope)


def middle_kernel(pre_ref, up_ref, resid_ref, gain_ref, cot_ref, out_ref, mid_ref, low_ref, mixed_ref, sums_ref):
    f32, bf16 = jnp.float32, jnp.bfloat16

    @pl.when(pl.program_id(0) == 0)
    def _():
        sums_ref[...] = jnp.zeros_like(sums_ref)

    grads = lax.dot_general(pre_ref[...], up_ref[...], NT, preferred_element_type=f32)
    part, gain, shift = norm_back(grads, resid_ref[...], gain_ref[...])
    cot = cot_ref[...].astype(f32)
    mid = cot + part
    low = mid.astype(bf16)
    mid_ref[...] = mid
    low_ref[...] = low
    mixed_ref[...] = lax.dot_general(
        low, out_ref[...], NT, preferred_element_type=f32
    ).astype(bf16)
    for row, value in enumerate((column_sum(low), gain, shift, column_sum(cot))):
        sums_ref[row : row + 1] += value


def middle_back(grad_pre, up_full, resid_mid, gain_row, cot_low, out_full):
    tokens, inner = grad_pre.shape
    width, tile = resid_mid.shape[1], 256
    block = pl.BlockSpec((tile, width), lambda i: (i, 0))
    whole = lambda *shape: pl.BlockSpec(shape, lambda i: (0, 0))
    return pl.pallas_call(
        middle_kernel,
        grid=(tokens // tile,),
        out_shape=[
            jax.ShapeDtypeStruct((tokens, width), jnp.float32),
            jax.ShapeDtypeStruct((tokens, width), jnp.bfloat16),
            jax.ShapeDtypeStruct((tokens, width), jnp.bfloat16),
            jax.ShapeDtypeStruct((8, width), jnp.float32),
        ],
        in_specs=[
            pl.BlockSpec((tile, inner), lambda i: (i, 0)),
            whole(width, inner),
            block,
            whole(1, width),
            block,
            whole(width, width),
        ],
        out_specs=[block, block, block, whole(8, width)],
        compiler_params=pltpu.CompilerParams(vmem_limit_bytes=20 * MIB),
        cost_estimate=SMALL,
    )(grad_pre, up_full, resid_mid, gain_row, cot_low, out_full)


def first_kernel(
    query_ref, key_ref, value_ref, weight_ref, token_ref, gain_ref, mid_ref, in_ref, sums_ref
):
    f32 = jnp.float32

    @pl.when(pl.program_id(0) == 0)
    def _():
        sums_ref[...] = jnp.zeros_like(sums_ref)

    width = query_ref.shape[1]
    grads = sum(
        lax.dot_general(
            ref[...],
            weight_ref[:, width * i : width * (i + 1)],
            NT,
            preferred_element_type=f32,
        )
        for i, ref in enumerate((query_ref, key_ref, value_ref))
    )
    part, gain, shift = norm_back(grads, token_ref[...].astype(f32), gain_ref[...])
    in_ref[...] = (mid_ref[...] + part).astype(jnp.bfloat16)
    rows = (gain, shift, column_sum(query_ref[...]), column_sum(value_ref[...]))
    for row, value in enumerate(rows):
        sums_ref[row : row + 1] += value


def first_back(grad_query, grad_key, grad_value, qkv_full, tokens_in, gain_row, grad_mid):
    tokens, width = tokens_in.shape
    tile = 256
    block = pl.BlockSpec((tile, width), lambda i: (i, 0))
    whole = lambda *shape: pl.BlockSpec(shape, lambda i: (0, 0))
    return pl.pallas_call(
        first_kernel,
        grid=(tokens // tile,),
        out_shape=[
            jax.ShapeDtypeStruct((tokens, width), jnp.bfloat16),
            jax.ShapeDtypeStruct((8, width), jnp.float32),
        ],
        in_specs=[
            block,
            block,
            block,
            whole(width, 3 * width),
            block,
            whole(1, width),
            block,
        ],
        out_specs=[block, whole(8, width)],
        compiler_params=pltpu.CompilerParams(vmem_limit_bytes=16 * MIB),
        cost_estimate=SMALL,
    )(grad_query, grad_key, grad_value, qkv_full, tokens_in, gain_row, grad_mid)


def pick(values, index, axis=0):
    return lax.dynamic_index_in_dim(values, index, axis, keepdims=False)


def to_micro_x(values, side):
    count, rows, width = values.shape
    halves = values.reshape(2, 2, rows, width)
    return swap(pick(halves, 1 - side), 2), halves


def to_micro_c(got, halves, side, core):
    both = jnp.stack([pick(halves, side), got], 1)
    return pick(both, core), swap(pick(both, 1 - core), CORE)


def to_micro_end(kept, got):
    return jnp.concatenate([kept, got]).reshape(-1, kept.shape[-1])


def from_micro_c(values):
    rows, width = values.shape[0] // 4, values.shape[1]
    parts = values.reshape(2, 2, rows, width)
    return parts[0], swap(parts[1], CORE)


def from_micro_pick(kept, got, core):
    both = jnp.where(core == 0, jnp.stack([kept, got]), jnp.stack([got, kept]))
    return both[:, 0], both[:, 1]


def from_micro_end(kept, got, side):
    halves = jnp.where(side == 0, jnp.stack([kept, got]), jnp.stack([got, kept]))
    return halves.reshape(4, *kept.shape[1:])


def on_device_fast(
    inputs,
    segments,
    norm1_gain,
    norm1_bias,
    qkv_weight,
    query_bias,
    value_bias,
    out_weight,
    out_bias,
    norm2_gain,
    norm2_bias,
    up_weight,
    up_bias,
    down_weight,
    down_bias,
    cotangent,
):
    f32, bf16 = jnp.float32, jnp.bfloat16
    local_rows, width = inputs.shape[1], inputs.shape[2]
    rows = width // DEVICES
    wide, inner = qkv_weight.shape[1], up_weight.shape[1]
    group = lax.axis_index("fsdp")
    side, core = group // 2, group % 2
    me = (lax.axis_index("dp") * 4 + group).astype(jnp.int32).reshape(1)

    vectors = (
        norm1_gain,
        norm1_bias,
        query_bias,
        value_bias,
        out_bias,
        norm2_gain,
        norm2_bias,
        down_bias,
    )
    row = lax.broadcasted_iota(jnp.int32, (rows, rows), 0)
    block = jnp.zeros((rows, rows), bf16)
    for j, vector in enumerate(vectors):
        block = jnp.where(row == j, vector[None], block)
    block = jnp.pad(block, ((0, 0), (0, 128 - rows)))
    row = lax.broadcasted_iota(jnp.int32, (rows, 128), 0)
    block = jnp.where(row == 8, jnp.pad(up_bias, (0, 128 - up_bias.shape[0]))[None], block)
    first = Gather(jnp.concatenate([qkv_weight, block], 1))
    second = Gather(jnp.concatenate([out_weight, up_weight], 1))
    third = Gather(down_weight)

    first.line()
    token_got, token_halves = to_micro_x(inputs, side)
    own = pick(segments, group).reshape(4, local_rows)
    labels = jnp.concatenate(
        [pick(own, lax.bitwise_xor(group, source)) for source in (0, 2, 1, 3)]
    )
    first.held, first.got, token_got, token_halves, second.held = fence(
        first.held, first.got, token_got, token_halves, second.held
    )

    first.plane()
    second.far()
    second.near()
    token_kept, token_got = to_micro_c(token_got, token_halves, side, core)
    tokens = to_micro_end(token_kept, token_got)
    resid_in = tokens.astype(f32)
    unit_one, _ = norm_parts(resid_in)
    first.held, first.got, second.held, second.got, third.held, unit_one = fence(
        first.held, first.got, second.held, second.got, third.held, unit_one
    )

    first.cores()
    second.plane_one()
    third.far()
    qkv_full, vectors = restore(first, cuts_of((wide, 128)), me)
    qkv_full = qkv_full.reshape(width, wide)
    vectors = vectors[:, :9].astype(f32)
    bias_up = vectors[:, 8, : up_bias.shape[0]].reshape(1, -1)
    (vectors,) = fence(vectors[:, :8, :rows].transpose(1, 0, 2).reshape(8, width))
    (
        gain_one,
        shift_one,
        bias_query,
        bias_value,
        bias_out,
        gain_two,
        shift_two,
        bias_down,
    ) = (vectors[i : i + 1] for i in range(8))
    normed_one = (unit_one * gain_one + shift_one).astype(bf16)
    bias_project = jnp.concatenate([bias_query, jnp.zeros_like(bias_query), bias_value], 1)
    project = project_forward(normed_one, qkv_full, bias_project)
    second.quads, second.got, third.held, third.got, project = fence(
        second.quads, second.got, third.held, third.got, project
    )

    second.plane_two()
    third.near()
    cot_parts = cotangent.reshape(2, 2, local_rows, width)
    cot_sent, cot_own = pick(cot_parts, 1 - side), pick(cot_parts, side)
    mixed, probs = attend(labels, project)
    second.held, second.got, third.held, third.got, mixed, cot_sent, cot_own = fence(
        second.held, second.got, third.held, third.got, mixed, cot_sent, cot_own
    )

    second.cores()
    cot_got = swap(cot_sent, X)
    third.line_end()
    second.parts, third.held, third.got, mixed, cot_got, cot_own = fence(
        second.parts, third.held, third.got, mixed, cot_got, cot_own
    )

    third.plane()
    cot_parts = jnp.stack([cot_own, cot_got], 1)
    cot_kept, cot_got = pick(cot_parts, core), swap(pick(cot_parts, 1 - core), CORE)
    cot_low = to_micro_end(cot_kept, cot_got)
    second.parts = [in_hbm(part) for part in second.parts]
    out_full, up_full = restore(second, cuts_of((width, inner)), me)
    out_full, up_full = out_full.reshape(width, width), up_full.reshape(width, inner)
    resid_mid = resid_in + jnp.dot(mixed, out_full, preferred_element_type=f32) + bias_out
    unit_two, _ = norm_parts(resid_mid)
    normed_two = (unit_two * gain_two + shift_two).astype(bf16)
    hidden, slope = up_forward(normed_two, up_full, bias_up)
    deep = inner // DEVICES
    down_sum = Scatter(
        parts_call(
            third_parts_kernel, [hidden, cot_low], deep, width, (4 * deep, width), 16, me
        )
    )
    third.held, third.got, down_sum.kept, down_sum.sent, hidden, cot_low = fence(
        third.held, third.got, down_sum.kept, down_sum.sent, hidden, cot_low
    )

    third.cores()
    down_sum.cores()
    third.parts, down_sum.kept, down_sum.got, hidden, cot_low = fence(
        third.parts, down_sum.kept, down_sum.got, hidden, cot_low
    )

    down_sum.plane_one()
    (down_full,) = restore(third, cuts_of((width,)), me, False)
    down_full = down_full.reshape(inner, width)
    grad_pre, grad_bias_up = pre_back(cot_low, down_full, slope)
    grad_mid, branch_low, grad_mixed, sums_two = middle_back(
        grad_pre, up_full, resid_mid, gain_two, cot_low, out_full
    )
    (
        down_sum.kept,
        down_sum.got,
        grad_mid,
        branch_low,
        grad_mixed,
        grad_pre,
        down_full,
        hidden,
    ) = fence(
        down_sum.kept,
        down_sum.got,
        grad_mid,
        branch_low,
        grad_mixed,
        grad_pre,
        down_full,
        hidden,
    )
    down_sum.plane_two()
    up_sum = Scatter(
        parts_call(
            second_parts_kernel,
            [mixed, branch_low, normed_two, grad_pre],
            rows,
            width + inner,
            (width, width),
            20,
            me,
        )
    )
    down_sum.kept, down_sum.got, up_sum.kept, up_sum.sent, grad_mixed, hidden, down_full = fence(
        down_sum.kept, down_sum.got, up_sum.kept, up_sum.sent, grad_mixed, hidden, down_full
    )

    up_sum.cores()
    down_sum.plane_end()
    result = resid_mid + jnp.dot(hidden, down_full, preferred_element_type=f32) + bias_down
    result = result.astype(bf16)
    down_sum.kept, down_sum.got, up_sum.kept, up_sum.got, grad_mixed, result = fence(
        down_sum.kept, down_sum.got, up_sum.kept, up_sum.got, grad_mixed, result
    )

    up_sum.plane_one()
    down_sum.near()
    out_kept, out_got = from_micro_c(result)
    grad_query, grad_key, grad_value = attend_back(project, probs, grad_mixed)
    qkv_sum = Scatter(
        parts_call(
            first_parts_kernel,
            [normed_one, grad_query, grad_key, grad_value],
            rows,
            wide,
            (width, width),
            13,
            me,
        )
    )
    (
        down_sum.kept,
        down_sum.got,
        up_sum.kept,
        up_sum.got,
        grad_query,
        grad_key,
        grad_value,
        qkv_sum.kept,
        qkv_sum.sent,
        out_kept,
        out_got,
    ) = fence(
        down_sum.kept,
        down_sum.got,
        up_sum.kept,
        up_sum.got,
        grad_query,
        grad_key,
        grad_value,
        qkv_sum.kept,
        qkv_sum.sent,
        out_kept,
        out_got,
    )
    up_sum.plane_two()
    qkv_sum.cores()
    down_sum.far()
    in_grad, sums_one = first_back(
        grad_query, grad_key, grad_value, qkv_full, tokens, gain_one, grad_mid
    )
    vector_sum = Scatter(
        parts_call(
            vector_parts_kernel, [sums_one, sums_two, grad_bias_up], rows, 128, (8, 128), 8, me
        )
    )
    (
        down_sum.kept,
        down_sum.got,
        up_sum.kept,
        up_sum.got,
        qkv_sum.kept,
        qkv_sum.got,
        vector_sum.kept,
        vector_sum.sent,
        in_grad,
        out_kept,
        out_got,
    ) = fence(
        down_sum.kept,
        down_sum.got,
        up_sum.kept,
        up_sum.got,
        qkv_sum.kept,
        qkv_sum.got,
        vector_sum.kept,
        vector_sum.sent,
        in_grad,
        out_kept,
        out_got,
    )

    up_sum.plane_end()
    vector_sum.cores()
    in_kept, in_got = from_micro_c(in_grad)
    out_kept, out_sent = from_micro_pick(out_kept, out_got, core)
    (
        up_sum.kept,
        up_sum.got,
        qkv_sum.kept,
        qkv_sum.got,
        vector_sum.kept,
        vector_sum.got,
        in_kept,
        in_got,
        out_kept,
        out_sent,
    ) = fence(
        up_sum.kept,
        up_sum.got,
        qkv_sum.kept,
        qkv_sum.got,
        vector_sum.kept,
        vector_sum.got,
        in_kept,
        in_got,
        out_kept,
        out_sent,
    )

    qkv_sum.plane_one(vector_sum)
    up_sum.near()
    in_kept, in_sent = from_micro_pick(in_kept, in_got, core)
    (
        qkv_sum.kept,
        qkv_sum.got,
        up_sum.kept,
        up_sum.got,
        in_kept,
        in_sent,
        out_kept,
        out_sent,
        down_sum.kept,
        down_sum.got,
    ) = fence(
        qkv_sum.kept,
        qkv_sum.got,
        up_sum.kept,
        up_sum.got,
        in_kept,
        in_sent,
        out_kept,
        out_sent,
        down_sum.kept,
        down_sum.got,
    )
    qkv_sum.plane_two()
    up_sum.far()
    out_got = swap(out_sent, X)
    (
        qkv_sum.kept,
        qkv_sum.got,
        up_sum.kept,
        up_sum.got,
        in_kept,
        in_sent,
        out_kept,
        out_got,
    ) = fence(
        qkv_sum.kept,
        qkv_sum.got,
        up_sum.kept,
        up_sum.got,
        in_kept,
        in_sent,
        out_kept,
        out_got,
    )

    in_got = swap(in_sent, X)
    qkv_sum.plane_end()
    qkv_sum.line()
    grad_out, grad_up = finish(up_sum, (width, inner))
    (grad_down,) = finish(down_sum, (width,))
    output = from_micro_end(out_kept, out_got, side)
    in_grad = from_micro_end(in_kept, in_got, side).astype(f32)
    qkv_sum.kept, qkv_sum.got, output, grad_out, grad_up, grad_down = fence(
        qkv_sum.kept, qkv_sum.got, output, grad_out, grad_up, grad_down
    )

    grad_qkv, sums = finish(qkv_sum, (wide, 128))
    deep, sums = sums[8, :deep], sums[:8, :rows]
    return (
        output,
        in_grad,
        sums[0],
        sums[1],
        grad_qkv,
        sums[2],
        sums[3],
        grad_out,
        sums[4],
        sums[5],
        sums[6],
        grad_up,
        deep,
        grad_down,
        sums[7],
    )


def solution(mesh):
    placed = (
        P(None, ("dp", "fsdp"), None),
        P(None, "dp"),
        P(("dp", "fsdp")),
        P(("dp", "fsdp")),
        P(("dp", "fsdp"), None),
        P(("dp", "fsdp")),
        P(("dp", "fsdp")),
        P(("dp", "fsdp"), None),
        P(("dp", "fsdp")),
        P(("dp", "fsdp")),
        P(("dp", "fsdp")),
        P(("dp", "fsdp"), None),
        P(("dp", "fsdp")),
        P(("dp", "fsdp"), None),
        P(("dp", "fsdp")),
        P(None, ("dp", "fsdp"), None),
    )
    fits = mesh.shape["dp"] == 8 and mesh.shape["fsdp"] == 4
    return jax.shard_map(
        on_device_fast if fits else on_device_general,
        mesh=mesh,
        in_specs=placed,
        out_specs=(
            P(None, ("dp", "fsdp"), None),
            P(None, ("dp", "fsdp"), None),
            P(("dp", "fsdp")),
            P(("dp", "fsdp")),
            P(("dp", "fsdp"), None),
            P(("dp", "fsdp")),
            P(("dp", "fsdp")),
            P(("dp", "fsdp"), None),
            P(("dp", "fsdp")),
            P(("dp", "fsdp")),
            P(("dp", "fsdp")),
            P(("dp", "fsdp"), None),
            P(("dp", "fsdp")),
            P(("dp", "fsdp"), None),
            P(("dp", "fsdp")),
        ),
        check_vma=False,
    )
```
